128 devices in a mesh: member: 4 (over z_hi, core), space: 32 (over y, x, z_lo).
Axes of the slice: x: 4, y: 4, z: 4 (z_hi: 2, z_lo: 2; z = z_hi * 2 + z_lo), core: 2. Of those that a mesh axis runs over, the one named last changes fastest.
Arguments:
- hidden: bfloat16 [16, 2048, 1024], P('member', 'space')
- grid_state: bfloat16 [16384, 1024], P('space'), may hold values from -6 to 6
- project_weight: bfloat16 [1024, 1024], replicated, may hold values from -0.1875 to 0.1875
- node_weight: bfloat16 [1024, 1024], replicated, may hold values from -0.1875 to 0.1875
- output_weight: bfloat16 [1024, 100], replicated, may hold values from -0.1875 to 0.1875
- prior_state: float32 [100, 16384], P(None, 'space'), may hold values from -6 to 6
- target: float32 [100, 16384], P(None, 'space'), may hold values from -6 to 6
- area_weight: float32 [16384], P('space'), as said below
- variable_weight: float32 [100], replicated, may hold values from 0.3 to 3
- edge_source: int32 [65536], P('space'), may hold values from 0 to 95, as said below
- edge_target: int32 [65536], P('space'), may hold values from 0 to 511, as said below
- edge_count: int32 [32], P('space'), may hold values from 1024 to 2048, as said below
- send_index: int32 [64, 16], P('space'), may hold values from 0 to 63, as said below
Outputs:
- grad_hidden: bfloat16 [16, 2048, 1024], P('member', 'space')
- grad_project: float32 [1024, 1024], P('space')
- grad_node: float32 [1024, 1024], P('space')
- grad_output: float32 [1024, 100], P('space')
- crps_loss: float32 [], replicated
The draws below stay inside these ranges and needn't reach their ends.
Inputs may be any that keep to these rules, and one draw needn't show every extreme that they name: `edge_count`: within each shard, live slots come first and their points never fall; every point has 2 to 4 live edges; in every draw one shard has 4 for every point and another has 2 for every point. `edge_source`: rows 64 and above only in live slots; rows from 64 to 79 never in shard 0, rows from 80 on never in the last shard; slots past the live count hold 0. `edge_target`: slots past the live count hold 511. `send_index`: each row holds distinct, increasing nodes; row 2s lies among the first 32 nodes of shard s, row 2s+1 among its last 32. `area_weight`: Positive.
All inputs are finite; a program needn't handle non-finite values.
Results may differ from the reference program's by a relative error of at most 0.012.
The reference program's roundings to bfloat16 on the way count: a program that leaves them out, or rounds other values in their place, can miss the bound.
Values may be sent and summed in bfloat16 or wider, within the bound.
No kernel may reach another device: no remote copies, remote signals or barrier semaphores. Data moves between devices by JAX's collectives and lax.ppermute only.
A program may use at most 256 MiB of HBM per device.

```python
import math
import jax
import jax.numpy as jnp
from jax import lax

WIDTH = 1024
VARS = 100
PTS_DEV = 512
HID_DEV = 64
SEND = 16
EDGE_DEV = 2048
MEMBERS = 16
POINTS = 16384
NODES = 2048
N_SPACE = 32


def edge_plan(key):
    key_degree, key_full, key_local, key_coin, key_pick, key_send = jax.random.split(key, 6)
    degree = jax.random.randint(key_degree, (N_SPACE, PTS_DEV), 2, 5)
    full_shard = jax.random.randint(key_full, (), 0, N_SPACE)
    sparse_shard = (full_shard + 1) % N_SPACE
    shard_index = jnp.arange(N_SPACE, dtype=jnp.int32)[:, None]
    degree = jnp.where(shard_index == full_shard, 4, degree)
    degree = jnp.where(shard_index == sparse_shard, 2, degree).astype(jnp.int32)
    ends = jnp.cumsum(degree, axis=1).astype(jnp.int32)
    counts = ends[:, -1]
    slot_index = jnp.arange(EDGE_DEV, dtype=jnp.int32)
    owner = jnp.sum((slot_index[None, :, None] >= ends[:, None, :]).astype(jnp.int32), axis=-1)
    owner = jnp.minimum(owner, PTS_DEV - 1).astype(jnp.int32)
    centre = owner * HID_DEV // PTS_DEV
    local_row = jnp.clip(centre + jax.random.randint(key_local, (N_SPACE, EDGE_DEV), -2, 3), 0, HID_DEV - 1)
    coin = jax.random.randint(key_coin, (N_SPACE, EDGE_DEV), 0, 2) == 1
    pick = jax.random.randint(key_pick, (N_SPACE, EDGE_DEV), 0, SEND)
    near_left = owner < PTS_DEV // 8
    near_right = owner >= PTS_DEV - PTS_DEV // 8
    source = jnp.where(near_left & coin & (shard_index > 0), HID_DEV + pick, local_row)
    source = jnp.where(near_right & coin & (shard_index < N_SPACE - 1), HID_DEV + SEND + pick, source)
    padding = slot_index[None, :] >= counts[:, None]
    source = jnp.where(padding, 0, source).astype(jnp.int32)
    scores = jax.random.randint(key_send, (N_SPACE, 2, 2 * SEND), 0, 2 ** 20) * (2 * SEND) + jnp.arange(2 * SEND, dtype=jnp.int32)
    order = jnp.argsort(scores, axis=-1, stable=True).astype(jnp.int32)
    chosen = jnp.sort(order[:, :, :SEND], axis=-1)
    offset = jnp.array([0, HID_DEV - 2 * SEND], dtype=jnp.int32)[None, :, None]
    sends = (chosen + offset).astype(jnp.int32)
    return (source, owner, counts.astype(jnp.int32), sends)


def draw_edge_source(key, part):
    return edge_plan(key)[0].reshape(-1)


def draw_edge_target(key, part):
    return edge_plan(key)[1].reshape(-1)


def draw_edge_count(key, part):
    return edge_plan(key)[2]


def draw_send_index(key, part):
    return edge_plan(key)[3].reshape(2 * N_SPACE, SEND)


def draw_hidden(key, part):
    key = jax.random.fold_in(key, 11)
    key_base = jax.random.fold_in(key, 0)
    member = jnp.arange(MEMBERS, dtype=jnp.float32)[:, None, None]
    member_scale = 0.6 * 3.0 ** (member / (MEMBERS - 1))
    base = jnp.clip(jax.random.normal(key_base, (MEMBERS, NODES, WIDTH)), -5.0, 5.0)
    return (base * member_scale).astype(jnp.bfloat16)


def draw_area_weight(key, part):
    key = jax.random.fold_in(key, 23)
    ramp = 1.0 + 2.0 * jnp.arange(POINTS, dtype=jnp.float32) / (POINTS - 1)
    rough = jnp.exp(jax.random.uniform(key, (POINTS,), minval=-0.6931472, maxval=0.6931472))
    return (ramp * rough).astype(jnp.float32)


def block_levels(stream_key, dims, cuts, least, largest):
    loudness, own = 1.0, jax.random.fold_in(stream_key, 6)
    for dim, blocks in cuts:
        steps = jnp.exp(jax.random.uniform(jax.random.fold_in(own, dim), (blocks,), jnp.float32, least / len(cuts), largest / len(cuts)))
        loudness = loudness * jnp.repeat(steps, dims[dim] // blocks).reshape([-1 if axis == dim else 1 for axis in range(len(dims))])
    return loudness


def scatter_about(rng, extent, scale, bound, cuts=(), kind=jnp.bfloat16):
    level = block_levels(rng, extent, cuts, -0.22, 0.18) if cuts else 1.0
    result = jax.random.normal(rng, extent, jnp.float32) * scale * level
    return jnp.minimum(jnp.maximum(result, -bound), bound).astype(kind)


def setup_inputs(seed: int = 0) -> dict:
    key_of = jax.random.split(jax.random.key(seed), 14)
    return {
        "hidden": draw_hidden(jax.random.fold_in(key_of[13], 71), 0),
        "grid_state": scatter_about(key_of[1], (POINTS, WIDTH), 1.0, 6.0, ((0, 32),)),
        "project_weight": scatter_about(key_of[2], (WIDTH, WIDTH), WIDTH ** -0.5, 0.1875),
        "node_weight": scatter_about(key_of[3], (WIDTH, WIDTH), WIDTH ** -0.5, 0.1875),
        "output_weight": scatter_about(key_of[4], (WIDTH, VARS), WIDTH ** -0.5, 0.1875),
        "prior_state": scatter_about(key_of[5], (VARS, POINTS), 1.0, 6.0, ((1, 32),), jnp.float32),
        "target": scatter_about(key_of[6], (VARS, POINTS), 1.0, 6.0, ((1, 32),), jnp.float32),
        "area_weight": draw_area_weight(jax.random.fold_in(key_of[13], 71), 0),
        "variable_weight": jnp.clip(jnp.exp(jax.random.uniform(key_of[8], (VARS,), jnp.float32, math.log(0.3), math.log(3.0))), 0.3, 3.0),
        "edge_source": draw_edge_source(jax.random.fold_in(key_of[13], 71), 0),
        "edge_target": draw_edge_target(jax.random.fold_in(key_of[13], 71), 0),
        "edge_count": draw_edge_count(jax.random.fold_in(key_of[13], 71), 0),
        "send_index": draw_send_index(jax.random.fold_in(key_of[13], 71), 0),
    }


SQRT_TWO_PI = 0.7978845608028654
CUBIC = 0.044715
ALPHA = 0.95
SOFT_EDGE = 0.05

def gelu_tanh(value):
    tanh_arg = SQRT_TWO_PI * (value + CUBIC * value * value * value)
    return 0.5 * value * (1.0 + jnp.tanh(tanh_arg))

def gelu_slope(value):
    tanh_arg = SQRT_TWO_PI * (value + CUBIC * value * value * value)
    tangent = jnp.tanh(tanh_arg)
    return 0.5 * (1.0 + tangent) + 0.5 * value * (1.0 - tangent * tangent) * SQRT_TWO_PI * (1.0 + 3.0 * CUBIC * value * value)

def soft_abs(value):
    return jnp.sqrt(value * value + SOFT_EDGE * SOFT_EDGE) - SOFT_EDGE

def soft_sign(value):
    return value / jnp.sqrt(value * value + SOFT_EDGE * SOFT_EDGE)

def matmul(left, right):
    return jnp.dot(left.astype(jnp.float32), right.astype(jnp.float32), precision=lax.Precision.HIGHEST, preferred_element_type=jnp.float32)

def crps_terms(own_preds, ensemble_preds, truth_rows, weight_map):
    member_count = ensemble_preds.shape[0]
    fairness = 1.0 - (1.0 - ALPHA) / member_count
    spread = own_preds[:, None] - ensemble_preds[None]
    pair_abs = lax.optimization_barrier(jnp.sum(soft_abs(spread), axis=1))
    pair_sign = lax.optimization_barrier(jnp.sum(soft_sign(spread), axis=1))
    misfit = own_preds - truth_rows[None]
    partial_sum = jnp.sum(weight_map[None] * (soft_abs(misfit) / member_count - fairness / (2.0 * member_count * (member_count - 1)) * pair_abs))
    gradient = weight_map[None] * (soft_sign(misfit) - fairness / (member_count - 1) * pair_sign)
    return (gradient, partial_sum)

def edge_tables(edge_source, edge_target, edge_count, send_index):
    shards = edge_count.shape[0]
    source = edge_source.reshape(shards, EDGE_DEV)
    point_local = edge_target.reshape(shards, EDGE_DEV)
    send_table = send_index.reshape(shards, 2, SEND)
    shard_index = jnp.arange(shards, dtype=jnp.int32)
    slot_index = jnp.arange(EDGE_DEV, dtype=jnp.int32)
    live_mask = slot_index[None, :] < edge_count[:, None]
    from_left = (source >= HID_DEV) & (source < HID_DEV + SEND)
    from_right = source >= HID_DEV + SEND
    left_shard = jnp.maximum(shard_index - 1, 0)
    right_shard = jnp.minimum(shard_index + 1, shards - 1)
    left_slot = jnp.clip(source - HID_DEV, 0, SEND - 1)
    right_slot = jnp.clip(source - HID_DEV - SEND, 0, SEND - 1)
    left_node = jnp.take_along_axis(send_table[left_shard, 1, :], left_slot, axis=1)
    right_node = jnp.take_along_axis(send_table[right_shard, 0, :], right_slot, axis=1)
    node_index = jnp.where(from_left, left_shard[:, None] * HID_DEV + left_node, jnp.where(from_right, right_shard[:, None] * HID_DEV + right_node, shard_index[:, None] * HID_DEV + source))
    present = jnp.where(from_left, shard_index[:, None] > 0, jnp.where(from_right, shard_index[:, None] < shards - 1, True))
    point_index = shard_index[:, None] * PTS_DEV + point_local
    return (node_index.reshape(-1).astype(jnp.int32), point_index.reshape(-1).astype(jnp.int32), present.reshape(-1).astype(jnp.float32)[:, None], live_mask.reshape(-1).astype(jnp.float32)[:, None])

def reference(hidden, grid_state, project_weight, node_weight, output_weight, prior_state, target, area_weight, variable_weight, edge_source, edge_target, edge_count, send_index):
    node_index, point_index, present, live_mask = edge_tables(edge_source, edge_target, edge_count, send_index)
    grid_edge = grid_state[point_index].astype(jnp.float32)

    def forward(member_rows):
        projected = matmul(member_rows, project_weight).astype(jnp.bfloat16)
        pre_act = projected[node_index].astype(jnp.float32) * present + grid_edge
        summed = jax.ops.segment_sum(gelu_tanh(pre_act) * live_mask, point_index, num_segments=POINTS, indices_are_sorted=True).astype(jnp.bfloat16)
        node_pre = matmul(summed, node_weight)
        node_out = gelu_tanh(node_pre).astype(jnp.bfloat16)
        return (pre_act, summed, node_pre, node_out)

    def predict(member_rows):
        node_out = forward(member_rows)[3]
        return prior_state + matmul(node_out, output_weight).T
    predictions = lax.map(predict, hidden)
    weight_map = variable_weight[:, None] * area_weight[None, :]

    def member_terms(own_preds):
        gradient, partial_sum = crps_terms(own_preds[None], predictions, target, weight_map)
        return (gradient[0].astype(jnp.bfloat16), partial_sum)
    grad_pred, partial_sums = lax.map(member_terms, predictions)
    crps_loss = jnp.sum(partial_sums) / (POINTS * VARS)

    def backward(totals, inputs):
        member_rows, member_grad = inputs
        pre_act, summed, node_pre, node_out = forward(member_rows)
        node_grad = matmul(member_grad.T, output_weight.T)
        node_pre_grad = (node_grad * gelu_slope(node_pre)).astype(jnp.bfloat16)
        summed_grad = matmul(node_pre_grad, node_weight.T)
        edge_grad = summed_grad[point_index] * gelu_slope(pre_act) * (live_mask * present)
        projected_grad = jax.ops.segment_sum(edge_grad, node_index, num_segments=NODES).astype(jnp.bfloat16)
        row_grad = matmul(projected_grad, project_weight.T).astype(jnp.bfloat16)
        totals = (totals[0] + matmul(member_rows.T, projected_grad), totals[1] + matmul(summed.T, node_pre_grad), totals[2] + matmul(node_out.T, member_grad.T))
        return (totals, row_grad)
    start_totals = (jnp.zeros((WIDTH, WIDTH), jnp.float32), jnp.zeros((WIDTH, WIDTH), jnp.float32), jnp.zeros((WIDTH, VARS), jnp.float32))
    totals, grad_hidden = lax.scan(backward, start_totals, (hidden, grad_pred))
    return (grad_hidden, totals[0] / POINTS, totals[1] / POINTS, totals[2] / POINTS, crps_loss)
```

```python
import functools

import jax
import jax.numpy as jnp
from jax import lax
from jax.experimental import pallas as pl
from jax.experimental.pallas import tpu as pltpu
from jax.sharding import PartitionSpec as P

SQRT_TWO_PI = 0.7978845608028654
CUBIC = 0.044715
ALPHA = 0.95
SOFT_EDGE = 0.05
DEGREE = 4
TABLE = 128
EMPTY = -64.0
CHUNK = 128
TILE = 256
VMEM_LIMIT = 56 * 1024 * 1024


def tanh_of(u):
    s = u * u
    return s, jnp.tanh(u * (SQRT_TWO_PI + (SQRT_TWO_PI * CUBIC) * s))


def gelu_twice(u):
    _, t = tanh_of(u)
    return u + u * t


def slope_twice(u):
    s, t = tanh_of(u)
    q = u * (SQRT_TWO_PI + (3.0 * SQRT_TWO_PI * CUBIC) * s)
    return (1.0 + t) * (1.0 + (1.0 - t) * q)


def dot(left, right):
    return lax.dot_general(
        left, right, (((1,), (0,)), ((), ())), preferred_element_type=jnp.float32
    )


def dot_nt(left, right):
    return lax.dot_general(
        left, right, (((1,), (1,)), ((), ())), preferred_element_type=jnp.float32
    )


def forward_kernel(
    rows_ref, project_ref, pick_ref, grid_ref, node_ref, output_ref, prior_ref,
    pred_ref, summed_ref, out_ref, comb_ref,
):
    members, table_rows, width = rows_ref.shape

    @pl.when(pl.program_id(0) == 0)
    def _():
        for m in range(members):
            comb_ref[m, :table_rows] = dot(rows_ref[m], project_ref[...]).astype(jnp.bfloat16)
            comb_ref[m, table_rows:TABLE] = jnp.full(
                (TABLE - table_rows, width), EMPTY, jnp.bfloat16
            )

    for m in range(members):
        comb_ref[m, TABLE:] = grid_ref[...]
    pick = pick_ref[0]
    for m in range(members):
        for h in range(0, width, TILE):
            u = dot(pick, comb_ref[m, :, h : h + TILE])
            twice = jnp.sum(gelu_twice(u).reshape(DEGREE, CHUNK, TILE), axis=0)
            summed_ref[m, :, h : h + TILE] = (0.5 * twice).astype(jnp.bfloat16)
    summed = summed_ref[...].reshape(members * CHUNK, width)
    for h in range(0, width, TILE):
        u = dot(summed, node_ref[:, h : h + TILE])
        value = (0.5 * gelu_twice(u)).astype(jnp.bfloat16)
        out_ref[:, :, h : h + TILE] = value.reshape(members, CHUNK, TILE)
    for m in range(members):
        pred_ref[m] = prior_ref[...] + dot_nt(output_ref[...], out_ref[m])[: prior_ref.shape[0]]


def slope_kernel(comb_ref, pick_ref, grid_ref, summed_ref, node_ref, edge_ref, point_ref, both_ref):
    members, _, width = comb_ref.shape
    pick = pick_ref[0]
    for m in range(members):
        both_ref[m, :TABLE] = comb_ref[m]
        both_ref[m, TABLE:] = grid_ref[...]
    for m in range(members):
        for h in range(0, width, TILE):
            u = dot(pick, both_ref[m, :, h : h + TILE])
            value = (0.5 * slope_twice(u)).astype(jnp.bfloat16)
            edge_ref[m, :, :, h : h + TILE] = value.reshape(DEGREE, CHUNK, TILE)
    summed = summed_ref[...].reshape(members * CHUNK, width)
    for h in range(0, width, TILE):
        u = dot(summed, node_ref[:, h : h + TILE])
        value = (0.5 * slope_twice(u)).astype(jnp.bfloat16)
        point_ref[:, :, h : h + TILE] = value.reshape(members, CHUNK, TILE)


def loss_kernel(
    own_ref, all_ref, truth_ref, area_ref, variable_ref, slope_ref, output_ref,
    grad_ref, pre_ref, loss_ref,
):
    members, variables, _ = own_ref.shape
    width = output_ref.shape[1]
    everyone = all_ref.shape[0]
    fairness = 1.0 - (1.0 - ALPHA) / everyone
    weight = variable_ref[...] * area_ref[...]
    truth = truth_ref[...]
    edge = SOFT_EDGE * SOFT_EDGE
    terms = jnp.zeros((variables, CHUNK), jnp.float32)
    grads = []
    for j in range(members):
        own = own_ref[j]
        pair_abs = jnp.full((variables, CHUNK), -everyone * SOFT_EDGE, jnp.float32)
        pair_sign = jnp.zeros((variables, CHUNK), jnp.float32)
        for k in range(everyone):
            d = own - all_ref[k]
            square = d * d + edge
            r = lax.rsqrt(square)
            pair_abs = pair_abs + square * r
            pair_sign = pair_sign + d * r
        d = own - truth
        square = d * d + edge
        r = lax.rsqrt(square)
        terms = terms + weight * (
            (square * r - SOFT_EDGE) / everyone
            - fairness / (2.0 * everyone * (everyone - 1)) * pair_abs
        )
        gradient = weight * (d * r - fairness / (everyone - 1) * pair_sign)
        grad_ref[j] = gradient.astype(jnp.bfloat16)
        padded = jnp.concatenate(
            [gradient, jnp.zeros((TABLE - variables, CHUNK), jnp.float32)], axis=0
        )
        grads.append(padded.T.astype(jnp.bfloat16))

    @pl.when(pl.program_id(0) == 0)
    def _():
        loss_ref[...] = jnp.zeros_like(loss_ref)

    loss_ref[...] += jnp.sum(terms.reshape(variables // 8, 8, CHUNK), axis=0)
    stacked = jnp.concatenate(grads, axis=0)
    for h in range(0, width, TILE):
        node_grad = dot(stacked, output_ref[:, h : h + TILE]).reshape(members, CHUNK, TILE)
        slope = slope_ref[:, :, h : h + TILE].astype(jnp.float32)
        pre_ref[:, :, h : h + TILE] = (node_grad * slope).astype(jnp.bfloat16)


def table_kernel(pre_ref, node_ref, slope_ref, place_ref, rows_ref, grad_ref, term_ref):
    members, points, _ = pre_ref.shape
    table_rows = grad_ref.shape[1]
    cast = []
    for m in range(members):
        summed_grad = dot_nt(pre_ref[m], node_ref[...])
        edge = [
            (summed_grad * slope_ref[m, k].astype(jnp.float32)).astype(jnp.bfloat16)
            for k in range(DEGREE)
        ]
        table = dot(place_ref[...], jnp.concatenate(edge, axis=0))[:table_rows]
        grad_ref[m] = table
        cast.append(table.astype(jnp.bfloat16))
    term_ref[...] = dot(rows_ref[...], jnp.concatenate(cast, axis=0)).astype(jnp.bfloat16)


def params():
    return pltpu.CompilerParams(
        dimension_semantics=("arbitrary",), vmem_limit_bytes=VMEM_LIMIT
    )


def whole(array):
    return pl.BlockSpec(array.shape, lambda c: (0,) * array.ndim)


def shards(
    hidden,
    grid_state,
    project_weight,
    node_weight,
    output_weight,
    prior_state,
    target,
    area_weight,
    variable_weight,
    edge_source,
    edge_target,
    edge_count,
    send_index,
):
    members, own_nodes, width = hidden.shape
    points = grid_state.shape[0]
    send_rows = send_index.shape[1]
    variables = output_weight.shape[1]
    slots = edge_source.shape[0]
    everyone = members * lax.axis_size("member")
    space = lax.axis_size("space")
    total_points = points * space
    table_rows = own_nodes + 2 * send_rows
    chunks = points // CHUNK
    padded = -(-variables // 8) * 8

    nodes = jnp.arange(own_nodes, dtype=jnp.int32)
    chosen = (send_index[:, :, None] == nodes).astype(jnp.bfloat16)
    packed = jnp.einsum(
        "dsn,mnh->dmsh", chosen, hidden, preferred_element_type=jnp.float32
    ).astype(jnp.bfloat16)
    forward = [(i, i + 1) for i in range(space - 1)]
    backward = [(i + 1, i) for i in range(space - 1)]
    from_left = lax.ppermute(packed[1], "space", forward)
    from_right = lax.ppermute(packed[0], "space", backward)

    edges = jnp.arange(slots, dtype=jnp.int32)
    live = edges < edge_count[0]
    owner = jnp.where(live, edge_target, points)
    point = jnp.arange(points, dtype=jnp.int32)
    start = jnp.sum((owner[:, None] < point[None, :]).astype(jnp.int32), axis=0)
    end = jnp.sum((owner[:, None] <= point[None, :]).astype(jnp.int32), axis=0)
    order = start[None, :] + jnp.arange(DEGREE, dtype=jnp.int32)[:, None]
    found = jnp.sum(
        jnp.where(order[:, None, :] == edges[None, :, None], edge_source[None, :, None], 0), axis=1
    )
    slot = jnp.where(order < end[None, :], found, table_rows)
    columns = jnp.arange(TABLE + CHUNK, dtype=jnp.int32)
    within = jnp.arange(CHUNK, dtype=jnp.int32)
    by_chunk = slot.reshape(DEGREE, chunks, CHUNK).transpose(1, 0, 2)
    pick = (
        (by_chunk[..., None] == columns) | ((within[:, None] + TABLE) == columns)
    ).astype(jnp.bfloat16).reshape(chunks, DEGREE * CHUNK, TABLE + CHUNK)
    place = (
        slot.reshape(1, DEGREE * points) == jnp.arange(TABLE, dtype=jnp.int32)[:, None]
    ).astype(jnp.bfloat16)
    output_rows = jnp.pad(output_weight.T, ((0, TABLE - variables), (0, 0)))
    prior = jnp.pad(prior_state, ((0, padded - variables), (0, 0)))
    truth = jnp.pad(target, ((0, padded - variables), (0, 0)))
    scale = jnp.pad(variable_weight, (0, padded - variables))[:, None]

    source_rows = jnp.concatenate([hidden, from_left, from_right], axis=1)

    chunk_rows = pl.BlockSpec((CHUNK, width), lambda c: (c, 0))
    member_rows = pl.BlockSpec((members, CHUNK, width), lambda c: (0, c, 0))
    pick_block = pl.BlockSpec((1, DEGREE * CHUNK, TABLE + CHUNK), lambda c: (c, 0, 0))
    by_variable = pl.BlockSpec((padded, CHUNK), lambda c: (0, c))
    own_block = pl.BlockSpec((members, padded, CHUNK), lambda c: (0, 0, c))
    per_point = jax.ShapeDtypeStruct((members, points, width), jnp.bfloat16)
    pred, summed, node_out, comb = pl.pallas_call(
        forward_kernel_with_table,
        grid=(chunks,),
        in_specs=[
            whole(source_rows), whole(project_weight), pick_block, chunk_rows,
            whole(node_weight), whole(output_rows), by_variable,
        ],
        out_specs=[
            own_block, member_rows, member_rows,
            pl.BlockSpec((members, TABLE, width), lambda c: (0, 0, 0)),
        ],
        out_shape=[
            jax.ShapeDtypeStruct((members, padded, points), jnp.float32), per_point, per_point,
            jax.ShapeDtypeStruct((members, TABLE, width), jnp.bfloat16),
        ],
        scratch_shapes=[pltpu.VMEM((members, TABLE + CHUNK, width), jnp.bfloat16)],
        compiler_params=params(),
        name="forward",
    )(source_rows, project_weight, pick, grid_state, node_weight, output_rows, prior)

    everyones = lax.all_gather(pred, "member", axis=0, tiled=True)

    edge_slope, node_slope = pl.pallas_call(
        slope_kernel,
        grid=(chunks,),
        in_specs=[whole(comb), pick_block, chunk_rows, member_rows, whole(node_weight)],
        out_specs=[
            pl.BlockSpec((members, DEGREE, CHUNK, width), lambda c: (0, 0, c, 0)), member_rows,
        ],
        out_shape=[
            jax.ShapeDtypeStruct((members, DEGREE, points, width), jnp.bfloat16), per_point,
        ],
        scratch_shapes=[pltpu.VMEM((members, TABLE + CHUNK, width), jnp.bfloat16)],
        compiler_params=params(),
        name="slopes",
    )(comb, pick, grid_state, summed, node_weight)

    grad_pred, node_pre_grad, loss_rows = pl.pallas_call(
        loss_kernel,
        grid=(chunks,),
        in_specs=[
            own_block,
            pl.BlockSpec((everyone, padded, CHUNK), lambda c: (0, 0, c)),
            by_variable,
            pl.BlockSpec((1, CHUNK), lambda c: (0, c)),
            whole(scale), member_rows, whole(output_rows),
        ],
        out_specs=[own_block, member_rows, pl.BlockSpec((8, CHUNK), lambda c: (0, 0))],
        out_shape=[
            jax.ShapeDtypeStruct((members, padded, points), jnp.bfloat16), per_point,
            jax.ShapeDtypeStruct((8, CHUNK), jnp.float32),
        ],
        compiler_params=params(),
        name="loss",
    )(pred, everyones, truth, area_weight[None, :], scale, node_slope, output_rows)

    node_term = jnp.einsum(
        "mgh,mgk->hk", summed, node_pre_grad, preferred_element_type=jnp.float32
    ).astype(jnp.bfloat16)
    output_term = jnp.einsum(
        "mgh,mvg->hv", node_out, grad_pred, preferred_element_type=jnp.float32
    )[:, :variables]
    loss_part = jnp.broadcast_to(jnp.sum(loss_rows), (width, 1))
    small_term = jnp.concatenate([output_term, loss_part], axis=1)

    source_columns = source_rows.reshape(members * table_rows, width).T
    table_grad, project_term = pl.pallas_call(
        table_kernel,
        grid=(width // TILE,),
        in_specs=[
            whole(node_pre_grad),
            pl.BlockSpec((TILE, width), lambda c: (c, 0)),
            pl.BlockSpec((members, DEGREE, points, TILE), lambda c: (0, 0, 0, c)),
            whole(place),
            whole(source_columns),
        ],
        out_specs=[
            pl.BlockSpec((members, table_rows, TILE), lambda c: (0, 0, c)),
            pl.BlockSpec((width, TILE), lambda c: (0, c)),
        ],
        out_shape=[
            jax.ShapeDtypeStruct((members, table_rows, width), jnp.float32),
            jax.ShapeDtypeStruct((width, width), jnp.bfloat16),
        ],
        compiler_params=params(),
        name="table",
    )(node_pre_grad, node_weight, edge_slope, place, source_columns)

    def reduce_rows(term):
        part = lax.psum_scatter(term, "space", scatter_dimension=0, tiled=True)
        return lax.psum(part.astype(jnp.float32), "member")

    node_sum = reduce_rows(node_term)
    small_sum = reduce_rows(small_term)
    project_sum = reduce_rows(project_term)

    left_back = lax.ppermute(
        table_grad[:, own_nodes : own_nodes + send_rows].astype(jnp.bfloat16), "space", backward
    )
    right_back = lax.ppermute(
        table_grad[:, own_nodes + send_rows :].astype(jnp.bfloat16), "space", forward
    )
    projected_grad = (
        table_grad[:, :own_nodes]
        + jnp.einsum(
            "sn,msh->mnh", chosen[1], left_back, preferred_element_type=jnp.float32
        )
        + jnp.einsum(
            "sn,msh->mnh", chosen[0], right_back, preferred_element_type=jnp.float32
        )
    ).astype(jnp.bfloat16)
    grad_hidden = jnp.einsum(
        "mnk,hk->mnh", projected_grad, project_weight, preferred_element_type=jnp.float32
    ).astype(jnp.bfloat16)
    return (
        grad_hidden,
        project_sum / total_points,
        node_sum / total_points,
        small_sum[:, :variables] / total_points,
        small_sum[0, variables] / (total_points * variables),
    )


def forward_kernel_with_table(*refs):
    inputs, (pred_ref, summed_ref, out_ref, table_ref, comb_ref) = refs[:7], refs[7:]
    forward_kernel(*inputs, pred_ref, summed_ref, out_ref, comb_ref)

    @pl.when(pl.program_id(0) == 0)
    def _():
        table_ref[...] = comb_ref[:, :TABLE]


def solution(mesh):
    placed = (
        P("member", "space", None),
        P("space", None),
        P(),
        P(),
        P(),
        P(None, "space"),
        P(None, "space"),
        P("space"),
        P(),
        P("space"),
        P("space"),
        P("space"),
        P("space", None),
    )
    return jax.shard_map(
        shards,
        mesh=mesh,
        in_specs=placed,
        out_specs=(
            P("member", "space", None),
            P("space", None),
            P("space", None),
            P("space", None),
            P(),
        ),
        check_vma=False,
    )
```

```python
import functools

import jax
import jax.numpy as jnp
from jax import lax
from jax.experimental import pallas as pl
from jax.experimental.pallas import tpu as pltpu
from jax.sharding import PartitionSpec as P

SQRT_TWO_PI = 0.7978845608028654
CUBIC = 0.044715
ALPHA = 0.95
SOFT_EDGE = 0.05
DEGREE = 4
TABLE = 128
EMPTY = -64.0
CHUNK = 128
TILE = 256
PART = 32
LANES = 128
VMEM_LIMIT = 56 * 1024 * 1024


def tanh_of(u):
    s = u * u
    return s, jnp.tanh(u * (SQRT_TWO_PI + (SQRT_TWO_PI * CUBIC) * s))


def gelu_twice(u):
    _, t = tanh_of(u)
    return u + u * t


def slope_twice(u):
    s, t = tanh_of(u)
    q = u * (SQRT_TWO_PI + (3.0 * SQRT_TWO_PI * CUBIC) * s)
    return (1.0 + t) * (1.0 + (1.0 - t) * q)


def dot(left, right):
    return lax.dot_general(
        left, right, (((1,), (0,)), ((), ())), preferred_element_type=jnp.float32
    )


def dot_nt(left, right):
    return lax.dot_general(
        left, right, (((1,), (1,)), ((), ())), preferred_element_type=jnp.float32
    )


def parts(rows):
    return [(r, c) for r in range(0, rows, PART) for c in range(0, TILE, LANES)]


def staged(tiles, work_ref, matmul, finish):
    for i, tile in enumerate(tiles):
        result = matmul(*tile)
        work_ref[i % 2, : result.shape[0]] = result
        if i:
            finish(work_ref.at[(i - 1) % 2], *tiles[i - 1])
    finish(work_ref.at[(len(tiles) - 1) % 2], *tiles[-1])


def edge_stage(pick_ref, comb_ref, work_ref, finish):
    members, _, width = comb_ref.shape
    tiles = [(m, h) for m in range(members) for h in range(0, width, TILE)]
    staged(
        tiles, work_ref, lambda m, h: dot(pick_ref[0], comb_ref[m, :, h : h + TILE]), finish
    )


def node_stage(summed_ref, node_ref, work_ref, finish):
    members, rows, width = summed_ref.shape

    def matmul(h):
        return dot(summed_ref[...].reshape(members * rows, width), node_ref[:, h : h + TILE])

    def finish_all(buffer, h):
        for m in range(members):
            finish(buffer.at[m * rows : (m + 1) * rows], m, h)

    staged([(h,) for h in range(0, width, TILE)], work_ref, matmul, finish_all)


def forward_kernel(
    rows_ref, project_ref, pick_ref, grid_ref, node_ref, output_ref, prior_ref,
    pred_ref, summed_ref, out_ref, comb_ref, work_ref,
):
    members, table_rows, width = rows_ref.shape

    @pl.when(pl.program_id(0) == 0)
    def _():
        for m in range(members):
            comb_ref[m, :table_rows] = dot(rows_ref[m], project_ref[...]).astype(jnp.bfloat16)
            comb_ref[m, table_rows:TABLE] = jnp.full(
                (TABLE - table_rows, width), EMPTY, jnp.bfloat16
            )

    for m in range(members):
        comb_ref[m, TABLE:] = grid_ref[...]

    def sum_edges(buffer, m, h):
        for r, c in parts(CHUNK):
            twice = sum(
                gelu_twice(buffer[k * CHUNK + r : k * CHUNK + r + PART, c : c + LANES])
                for k in range(DEGREE)
            )
            summed_ref[m, r : r + PART, h + c : h + c + LANES] = (0.5 * twice).astype(jnp.bfloat16)

    def node_values(buffer, m, h):
        for r, c in parts(CHUNK):
            value = 0.5 * gelu_twice(buffer[r : r + PART, c : c + LANES])
            out_ref[m, r : r + PART, h + c : h + c + LANES] = value.astype(jnp.bfloat16)

    edge_stage(pick_ref, comb_ref, work_ref, sum_edges)
    node_stage(summed_ref, node_ref, work_ref, node_values)
    for m in range(members):
        pred_ref[m] = jnp.zeros(pred_ref.shape[1:], jnp.float32)
        pred_ref[m, : prior_ref.shape[0]] = prior_ref[...] + dot_nt(output_ref[...], out_ref[m])


def slope_kernel(
    comb_ref, pick_ref, grid_ref, summed_ref, node_ref, edge_ref, point_ref, both_ref, work_ref,
):
    members = comb_ref.shape[0]
    for m in range(members):
        both_ref[m, :TABLE] = comb_ref[m]
        both_ref[m, TABLE:] = grid_ref[...]

    def edge_slopes(buffer, m, h):
        for k in range(DEGREE):
            for r, c in parts(CHUNK):
                value = 0.5 * slope_twice(
                    buffer[k * CHUNK + r : k * CHUNK + r + PART, c : c + LANES]
                )
                edge_ref[m, k, r : r + PART, h + c : h + c + LANES] = value.astype(jnp.bfloat16)

    def node_slopes(buffer, m, h):
        for r, c in parts(CHUNK):
            value = 0.5 * slope_twice(buffer[r : r + PART, c : c + LANES])
            point_ref[m, r : r + PART, h + c : h + c + LANES] = value.astype(jnp.bfloat16)

    edge_stage(pick_ref, both_ref, work_ref, edge_slopes)
    node_stage(summed_ref, node_ref, work_ref, node_slopes)


def loss_kernel(
    core_index_ref, own_ref, core_ref, chip_ref, far_ref, truth_ref, area_ref, variable_ref, slope_ref, output_ref,
    grad_ref, pre_ref, loss_ref, tall_ref, sum_ref,
):
    members = own_ref.shape[0]
    variables = truth_ref.shape[0]
    width = output_ref.shape[1]
    everyone = 4 * members
    fairness = 1.0 - (1.0 - ALPHA) / everyone
    weight = variable_ref[...] * area_ref[...]
    truth = truth_ref[...]
    edge = SOFT_EDGE * SOFT_EDGE
    terms = jnp.zeros((variables, CHUNK), jnp.float32)

    @pl.when(pl.program_id(0) == 0)
    def _():
        sum_ref[...] = jnp.zeros_like(sum_ref)
        tall_ref[...] = jnp.zeros_like(tall_ref)

    grads = []
    for j in range(members):
        own = own_ref[j, :variables]
        pair_abs = jnp.full((variables, CHUNK), -everyone * SOFT_EDGE, jnp.float32)
        pair_sign = jnp.zeros((variables, CHUNK), jnp.float32)
        for other in [ref[k, :variables] for ref in (own_ref, core_ref, chip_ref, far_ref) for k in range(members)]:
            d = own - other
            square = d * d + edge
            r = lax.rsqrt(square)
            pair_abs = pair_abs + square * r
            pair_sign = pair_sign + d * r
        d = own - truth
        square = d * d + edge
        r = lax.rsqrt(square)
        terms = terms + weight * (
            (square * r - SOFT_EDGE) / everyone
            - fairness / (2.0 * everyone * (everyone - 1)) * pair_abs
        )
        gradient = weight * (d * r - fairness / (everyone - 1) * pair_sign)
        grad_ref[j] = gradient.astype(jnp.bfloat16)
        tall_ref[:variables] = gradient
        grads.append(tall_ref[...].T.astype(jnp.bfloat16))

    sum_ref[...] += jnp.sum(terms, axis=0, keepdims=True)

    @pl.when(pl.program_id(0) == pl.num_programs(0) - 1)
    def _():
        rest = jnp.sum(sum_ref[...], axis=1, keepdims=True)
        lane = lax.broadcasted_iota(jnp.int32, (1, CHUNK), 1)
        row = jnp.zeros((1, CHUNK), jnp.float32)
        for part in range(3):
            piece = rest.astype(jnp.bfloat16).astype(jnp.float32)
            row = jnp.where(lane == variables + 3 * core_index_ref[0] + part, piece, row)
            rest = rest - piece
        loss_ref[...] = row

    stacked = jnp.concatenate(grads, axis=0)
    for h in range(0, width, TILE):
        node_grad = dot(stacked, output_ref[:, h : h + TILE]).reshape(members, CHUNK, TILE)
        slope = slope_ref[:, :, h : h + TILE].astype(jnp.float32)
        pre_ref[:, :, h : h + TILE] = (node_grad * slope).astype(jnp.bfloat16)


def table_kernel(pre_ref, node_ref, slope_ref, place_ref, rows_ref, grad_ref, term_ref):
    members, points, _ = pre_ref.shape
    table_rows = grad_ref.shape[1]
    cast = []
    for m in range(members):
        summed_grad = dot_nt(pre_ref[m], node_ref[...]).astype(jnp.bfloat16)
        table = sum(
            dot(place_ref[:, k * points : (k + 1) * points], summed_grad * slope_ref[m, k])
            for k in range(DEGREE)
        )[:table_rows]
        grad_ref[m] = table
        cast.append(table.astype(jnp.bfloat16))
    term_ref[...] = dot(rows_ref[...], jnp.concatenate(cast, axis=0)).astype(jnp.bfloat16)


def params():
    return pltpu.CompilerParams(
        dimension_semantics=("arbitrary",), vmem_limit_bytes=VMEM_LIMIT
    )


def whole(array):
    return pl.BlockSpec(array.shape, lambda c: (0,) * array.ndim)


def shards(
    hidden,
    grid_state,
    project_weight,
    node_weight,
    output_weight,
    prior_state,
    target,
    area_weight,
    variable_weight,
    edge_source,
    edge_target,
    edge_count,
    send_index,
):
    members, own_nodes, width = hidden.shape
    points = grid_state.shape[0]
    send_rows = send_index.shape[1]
    variables = output_weight.shape[1]
    slots = edge_source.shape[0]
    core = lax.axis_index("member") % 2
    space = lax.axis_size("space")
    total_points = points * space
    table_rows = own_nodes + 2 * send_rows
    chunks = points // CHUNK

    nodes = jnp.arange(own_nodes, dtype=jnp.int32)
    chosen = (send_index[:, :, None] == nodes).astype(jnp.bfloat16)
    packed = jnp.einsum(
        "dsn,mnh->dmsh", chosen, hidden, preferred_element_type=jnp.float32
    ).astype(jnp.bfloat16)
    forward = [(i, i + 1) for i in range(space - 1)]
    backward = [(i + 1, i) for i in range(space - 1)]
    from_left = lax.ppermute(packed[1], "space", forward)
    from_right = lax.ppermute(packed[0], "space", backward)

    edges = jnp.arange(slots, dtype=jnp.int32)
    live = edges < edge_count[0]
    owner = jnp.where(live, edge_target, points)
    ahead = jnp.pad(owner, (DEGREE - 1, 0), constant_values=-1)
    rank = sum(
        (lax.slice_in_dim(ahead, k, k + slots) == owner).astype(jnp.int32)
        for k in range(DEGREE - 1)
    )
    ranked = jnp.where(
        rank[None, :] == jnp.arange(DEGREE, dtype=jnp.int32)[:, None], edge_source[None, :] + 1, 0
    ).astype(jnp.bfloat16)
    owned = (owner[:, None] == jnp.arange(points, dtype=jnp.int32)).astype(jnp.bfloat16)
    found = jnp.einsum("ke,eg->kg", ranked, owned, preferred_element_type=jnp.float32)
    found = found.astype(jnp.int32)
    slot = jnp.where(found > 0, found - 1, table_rows)
    columns = jnp.arange(TABLE + CHUNK, dtype=jnp.int32)
    within = jnp.arange(CHUNK, dtype=jnp.int32)
    by_chunk = slot.reshape(DEGREE, chunks, CHUNK).transpose(1, 0, 2)
    pick = (
        (by_chunk[..., None] == columns) | ((within[:, None] + TABLE) == columns)
    ).astype(jnp.bfloat16).reshape(chunks, DEGREE * CHUNK, TABLE + CHUNK)
    place = (
        slot.reshape(1, DEGREE * points) == jnp.arange(TABLE, dtype=jnp.int32)[:, None]
    ).astype(jnp.bfloat16)
    output_rows = output_weight.T
    output_padded = jnp.pad(output_rows, ((0, TABLE - variables), (0, 0)))
    scale = variable_weight[:, None]

    source_rows = jnp.concatenate([hidden, from_left, from_right], axis=1)

    chunk_rows = pl.BlockSpec((CHUNK, width), lambda c: (c, 0))
    member_rows = pl.BlockSpec((members, CHUNK, width), lambda c: (0, c, 0))
    pick_block = pl.BlockSpec((1, DEGREE * CHUNK, TABLE + CHUNK), lambda c: (c, 0, 0))
    by_variable = pl.BlockSpec((variables, CHUNK), lambda c: (0, c))
    tiled_rows = -(-variables // 8) * 8
    own_block = pl.BlockSpec((members, tiled_rows, CHUNK), lambda c: (0, 0, c))
    per_point = jax.ShapeDtypeStruct((members, points, width), jnp.bfloat16)
    pred, summed, node_out, comb = pl.pallas_call(
        forward_kernel_with_table,
        grid=(chunks,),
        in_specs=[
            whole(source_rows), whole(project_weight), pick_block, chunk_rows,
            whole(node_weight), whole(output_rows), by_variable,
        ],
        out_specs=[
            own_block, member_rows, member_rows,
            pl.BlockSpec((members, TABLE, width), lambda c: (0, 0, 0)),
        ],
        out_shape=[
            jax.ShapeDtypeStruct((members, tiled_rows, points), jnp.float32), per_point, per_point,
            jax.ShapeDtypeStruct((members, TABLE, width), jnp.bfloat16),
        ],
        scratch_shapes=[
            pltpu.VMEM((members, TABLE + CHUNK, width), jnp.bfloat16),
            pltpu.VMEM((2, DEGREE * CHUNK, TILE), jnp.float32),
        ],
        compiler_params=params(),
        name="forward",
    )(source_rows, project_weight, pick, grid_state, node_weight, output_rows, prior_state)

    def swap(value, flip):
        return lax.ppermute(value, "member", [(i, i ^ flip) for i in range(lax.axis_size("member"))])

    chip_pred = swap(pred, 2)
    core_pred = swap(pred, 1)
    far_pred = swap(chip_pred, 1)

    edge_slope, node_slope = pl.pallas_call(
        slope_kernel,
        grid=(chunks,),
        in_specs=[whole(comb), pick_block, chunk_rows, member_rows, whole(node_weight)],
        out_specs=[
            pl.BlockSpec((members, DEGREE, CHUNK, width), lambda c: (0, 0, c, 0)), member_rows,
        ],
        out_shape=[
            jax.ShapeDtypeStruct((members, DEGREE, points, width), jnp.bfloat16), per_point,
        ],
        scratch_shapes=[
            pltpu.VMEM((members, TABLE + CHUNK, width), jnp.bfloat16),
            pltpu.VMEM((2, DEGREE * CHUNK, TILE), jnp.float32),
        ],
        compiler_params=params(),
        name="slopes",
    )(comb, pick, grid_state, summed, node_weight)

    grad_pred, node_pre_grad, loss_row = pl.pallas_call(
        loss_kernel,
        grid=(chunks,),
        in_specs=[
            pl.BlockSpec(memory_space=pltpu.SMEM),
            own_block, own_block, own_block, own_block, by_variable,
            pl.BlockSpec((1, CHUNK), lambda c: (0, c)),
            whole(scale), member_rows, whole(output_padded),
        ],
        out_specs=[
            pl.BlockSpec((members, variables, CHUNK), lambda c: (0, 0, c)), member_rows,
            pl.BlockSpec((1, CHUNK), lambda c: (0, 0)),
        ],
        out_shape=[
            jax.ShapeDtypeStruct((members, variables, points), jnp.bfloat16), per_point,
            jax.ShapeDtypeStruct((1, CHUNK), jnp.float32),
        ],
        scratch_shapes=[
            pltpu.VMEM((TABLE, CHUNK), jnp.float32), pltpu.VMEM((1, CHUNK), jnp.float32),
        ],
        compiler_params=params(),
        name="loss",
    )(core[None], pred, core_pred, chip_pred, far_pred, target, area_weight[None, :], scale, node_slope, output_padded)

    def own_half(term):
        blocks = term.reshape(space, 2, width // space // 2, term.shape[1])
        mine = lax.dynamic_index_in_dim(blocks, core, 1, keepdims=False)
        other = swap(lax.dynamic_index_in_dim(blocks, 1 - core, 1, keepdims=False), 1)
        return (mine.astype(jnp.float32) + other.astype(jnp.float32)).astype(jnp.bfloat16)

    def reduce_rows(half):
        parts = lax.all_to_all(half, "space", 0, 0, tiled=True)
        part = jnp.sum(parts.astype(jnp.float32), axis=0)
        mine = part + swap(part, 2)
        other = swap(part, 1) + swap(part, 3)
        return jnp.where(
            core == 0,
            jnp.concatenate([mine, other], axis=0),
            jnp.concatenate([other, mine], axis=0),
        )

    node_term = jnp.einsum(
        "mgh,mgk->hk", summed, node_pre_grad, preferred_element_type=jnp.float32
    ).astype(jnp.bfloat16)
    output_term = jnp.einsum(
        "mgh,mvg->hv", node_out, grad_pred, preferred_element_type=jnp.float32
    )
    output_term = (
        jnp.pad(output_term, ((0, 0), (0, TABLE - variables))) + loss_row
    ).astype(jnp.bfloat16)
    node_half = own_half(jnp.concatenate([node_term, output_term], axis=1))

    source_columns = source_rows.reshape(members * table_rows, width).T
    table_grad, project_term = pl.pallas_call(
        table_kernel,
        grid=(width // TILE,),
        in_specs=[
            whole(node_pre_grad),
            pl.BlockSpec((TILE, width), lambda c: (c, 0)),
            pl.BlockSpec((members, DEGREE, points, TILE), lambda c: (0, 0, 0, c)),
            whole(place),
            whole(source_columns),
        ],
        out_specs=[
            pl.BlockSpec((members, table_rows, TILE), lambda c: (0, 0, c)),
            pl.BlockSpec((width, TILE), lambda c: (0, c)),
        ],
        out_shape=[
            jax.ShapeDtypeStruct((members, table_rows, width), jnp.float32),
            jax.ShapeDtypeStruct((width, width), jnp.bfloat16),
        ],
        compiler_params=params(),
        name="table",
    )(node_pre_grad, node_weight, edge_slope, place, source_columns)

    sums = reduce_rows(jnp.concatenate([own_half(project_term), node_half], axis=2))

    left_back = lax.ppermute(
        table_grad[:, own_nodes : own_nodes + send_rows].astype(jnp.bfloat16), "space", backward
    )
    right_back = lax.ppermute(
        table_grad[:, own_nodes + send_rows :].astype(jnp.bfloat16), "space", forward
    )
    projected_grad = (
        table_grad[:, :own_nodes]
        + jnp.einsum(
            "sn,msh->mnh", chosen[1], left_back, preferred_element_type=jnp.float32
        )
        + jnp.einsum(
            "sn,msh->mnh", chosen[0], right_back, preferred_element_type=jnp.float32
        )
    ).astype(jnp.bfloat16)
    grad_hidden = jnp.einsum(
        "mnk,hk->mnh", projected_grad, project_weight, preferred_element_type=jnp.float32
    ).astype(jnp.bfloat16)
    output_at = 2 * width
    loss_at = output_at + variables
    return (
        grad_hidden,
        sums[:, :width] / total_points,
        sums[:, width:output_at] / total_points,
        sums[:, output_at:loss_at] / total_points,
        jnp.sum(sums[0, loss_at:]) / (total_points * variables),
    )


def forward_kernel_with_table(*refs):
    inputs, (pred_ref, summed_ref, out_ref, table_ref, comb_ref, work_ref) = refs[:7], refs[7:]
    forward_kernel(*inputs, pred_ref, summed_ref, out_ref, comb_ref, work_ref)

    @pl.when(pl.program_id(0) == 0)
    def _():
        table_ref[...] = comb_ref[:, :TABLE]


def solution(mesh):
    placed = (
        P("member", "space", None),
        P("space", None),
        P(),
        P(),
        P(),
        P(None, "space"),
        P(None, "space"),
        P("space"),
        P(),
        P("space"),
        P("space"),
        P("space"),
        P("space", None),
    )
    return jax.shard_map(
        shards,
        mesh=mesh,
        in_specs=placed,
        out_specs=(
            P("member", "space", None),
            P("space", None),
            P("space", None),
            P("space", None),
            P(),
        ),
        check_vma=False,
    )
```

```python
import functools

import jax
import jax.numpy as jnp
from jax import lax
from jax.experimental import pallas as pl
from jax.experimental.pallas import tpu as pltpu
from jax.sharding import PartitionSpec as P

SQRT_TWO_PI = 0.7978845608028654
CUBIC = 0.044715
ALPHA = 0.95
SOFT_EDGE = 0.05
DEGREE = 4
TABLE = 128
EMPTY = -64.0
CHUNK = 128
TILE = 256
PART = 32
LANES = 128
VMEM_LIMIT = 56 * 1024 * 1024


def tanh_of(u):
    s = u * u
    return s, jnp.tanh(u * (SQRT_TWO_PI + (SQRT_TWO_PI * CUBIC) * s))


def gelu_twice(u):
    _, t = tanh_of(u)
    return u + u * t


def slope_twice(u):
    s, t = tanh_of(u)
    q = u * (SQRT_TWO_PI + (3.0 * SQRT_TWO_PI * CUBIC) * s)
    return (1.0 + t) * (1.0 + (1.0 - t) * q)


def dot(left, right):
    return lax.dot_general(
        left, right, (((1,), (0,)), ((), ())), preferred_element_type=jnp.float32
    )


def dot_nt(left, right):
    return lax.dot_general(
        left, right, (((1,), (1,)), ((), ())), preferred_element_type=jnp.float32
    )


def parts(rows):
    return [(r, c) for r in range(0, rows, PART) for c in range(0, TILE, LANES)]


def staged(tiles, work_ref, matmul, finish):
    for i, tile in enumerate(tiles):
        result = matmul(*tile)
        work_ref[i % 2, : result.shape[0]] = result.astype(work_ref.dtype)
        if i:
            finish(work_ref.at[(i - 1) % 2], *tiles[i - 1])
    finish(work_ref.at[(len(tiles) - 1) % 2], *tiles[-1])


def edge_stage(pick_ref, comb_ref, work_ref, finish):
    members, _, width = comb_ref.shape
    tiles = [(m, h) for m in range(members) for h in range(0, width, TILE)]
    staged(
        tiles, work_ref, lambda m, h: dot(pick_ref[0], comb_ref[m, :, h : h + TILE]), finish
    )


def node_stage(summed_ref, node_ref, work_ref, finish):
    members, rows, width = summed_ref.shape

    def matmul(h):
        return dot(summed_ref[...].reshape(members * rows, width), node_ref[:, h : h + TILE])

    def finish_all(buffer, h):
        for m in range(members):
            finish(buffer.at[m * rows : (m + 1) * rows], m, h)

    staged([(h,) for h in range(0, width, TILE)], work_ref, matmul, finish_all)


def forward_kernel(
    rows_ref, project_ref, pick_ref, grid_ref, node_ref, output_ref, prior_ref,
    pred_ref, summed_ref, out_ref, comb_ref, work_ref,
):
    members, table_rows, width = rows_ref.shape

    @pl.when(pl.program_id(0) == 0)
    def _():
        for m in range(members):
            comb_ref[m, :table_rows] = dot(rows_ref[m], project_ref[...]).astype(jnp.bfloat16)
            comb_ref[m, table_rows:TABLE] = jnp.full(
                (TABLE - table_rows, width), EMPTY, jnp.bfloat16
            )

    for m in range(members):
        comb_ref[m, TABLE:] = grid_ref[...]

    def sum_edges(buffer, m, h):
        for r, c in parts(CHUNK):
            twice = sum(
                gelu_twice(buffer[k * CHUNK + r : k * CHUNK + r + PART, c : c + LANES])
                for k in range(DEGREE)
            )
            summed_ref[m, r : r + PART, h + c : h + c + LANES] = (0.5 * twice).astype(jnp.bfloat16)

    def node_values(buffer, m, h):
        for r, c in parts(CHUNK):
            value = 0.5 * gelu_twice(buffer[r : r + PART, c : c + LANES])
            out_ref[m, r : r + PART, h + c : h + c + LANES] = value.astype(jnp.bfloat16)

    edge_stage(pick_ref, comb_ref, work_ref, sum_edges)
    node_stage(summed_ref, node_ref, work_ref, node_values)
    for m in range(members):
        pred_ref[m] = jnp.zeros(pred_ref.shape[1:], jnp.float32)
        pred_ref[m, : prior_ref.shape[0]] = prior_ref[...] + dot_nt(output_ref[...], out_ref[m])


def edge_slope_kernel(comb_ref, pick_ref, grid_ref, edge_ref, both_ref, work_ref):
    for m in range(comb_ref.shape[0]):
        both_ref[m, :TABLE] = comb_ref[m]
        both_ref[m, TABLE:] = grid_ref[...]

    def edge_slopes(buffer, m, h):
        for k in range(DEGREE):
            for r, c in parts(CHUNK):
                value = slope_twice(buffer[k * CHUNK + r : k * CHUNK + r + PART, c : c + LANES])
                edge_ref[m, k, r : r + PART, h + c : h + c + LANES] = value * 0.5

    edge_stage(pick_ref, both_ref, work_ref, edge_slopes)


def node_slope_kernel(summed_ref, node_ref, point_ref, work_ref):
    def node_slopes(buffer, m, h):
        for r, c in parts(CHUNK):
            value = 0.5 * slope_twice(buffer[r : r + PART, c : c + LANES])
            point_ref[m, r : r + PART, h + c : h + c + LANES] = value.astype(jnp.bfloat16)

    node_stage(summed_ref, node_ref, work_ref, node_slopes)


def loss_kernel(
    core_index_ref, own_ref, core_ref, chip_ref, far_ref, truth_ref, area_ref, variable_ref, slope_ref, output_ref,
    grad_ref, pre_ref, loss_ref, tall_ref, sum_ref,
):
    members = own_ref.shape[0]
    variables = truth_ref.shape[0]
    width = output_ref.shape[1]
    everyone = 4 * members
    fairness = 1.0 - (1.0 - ALPHA) / everyone
    weight = variable_ref[...] * area_ref[...]
    truth = truth_ref[...]
    edge = SOFT_EDGE * SOFT_EDGE
    terms = jnp.zeros((variables, CHUNK), jnp.float32)

    @pl.when(pl.program_id(0) == 0)
    def _():
        sum_ref[...] = jnp.zeros_like(sum_ref)
        tall_ref[...] = jnp.zeros_like(tall_ref)

    grads = []
    for j in range(members):
        own = own_ref[j, :variables]
        pair_abs = jnp.full((variables, CHUNK), -everyone * SOFT_EDGE, jnp.float32)
        pair_sign = jnp.zeros((variables, CHUNK), jnp.float32)
        for other in [ref[k, :variables] for ref in (own_ref, core_ref, chip_ref, far_ref) for k in range(members)]:
            d = own - other
            square = d * d + edge
            r = lax.rsqrt(square)
            pair_abs = pair_abs + square * r
            pair_sign = pair_sign + d * r
        d = own - truth
        square = d * d + edge
        r = lax.rsqrt(square)
        terms = terms + weight * (
            (square * r - SOFT_EDGE) / everyone
            - fairness / (2.0 * everyone * (everyone - 1)) * pair_abs
        )
        gradient = weight * (d * r - fairness / (everyone - 1) * pair_sign)
        tall_ref[:variables] = gradient
        tall = tall_ref[...].T.astype(jnp.bfloat16)
        grad_ref[j] = tall
        grads.append(tall)

    sum_ref[...] += jnp.sum(terms, axis=0, keepdims=True)

    @pl.when(pl.program_id(0) == pl.num_programs(0) - 1)
    def _():
        rest = jnp.sum(sum_ref[...], axis=1, keepdims=True)
        lane = lax.broadcasted_iota(jnp.int32, (1, CHUNK), 1)
        row = jnp.zeros((1, CHUNK), jnp.float32)
        for part in range(3):
            piece = rest.astype(jnp.bfloat16).astype(jnp.float32)
            row = jnp.where(lane == variables + 3 * core_index_ref[0] + part, piece, row)
            rest = rest - piece
        loss_ref[...] = row

    stacked = jnp.concatenate(grads, axis=0)
    for h in range(0, width, TILE):
        node_grad = dot(stacked, output_ref[:, h : h + TILE]).reshape(members, CHUNK, TILE)
        slope = slope_ref[:, :, h : h + TILE].astype(jnp.float32)
        pre_ref[:, :, h : h + TILE] = (node_grad * slope).astype(jnp.bfloat16)


def dot_tn(left, right):
    return lax.dot_general(
        left, right, (((0,), (0,)), ((), ())), preferred_element_type=jnp.float32
    )


def split_rows(value, core, mine_ref, other_ref, columns):
    rows = mine_ref.shape[1]
    pairs = value.reshape(value.shape[0] // (2 * rows), 2, rows, value.shape[1])
    first, second = pairs[:, 0], pairs[:, 1]
    mine_ref[:, :, columns] = jnp.where(core == 0, first, second).astype(jnp.bfloat16)
    other_ref[:, :, columns] = jnp.where(core == 0, second, first).astype(jnp.bfloat16)


def node_term_kernel(
    core_ref, summed_ref, out_ref, pre_ref, grad_ref, loss_ref, mine_ref, other_ref,
):
    members, _, width = pre_ref.shape
    core = core_ref[0]
    node = sum(dot_tn(summed_ref[m], pre_ref[m]) for m in range(members))
    split_rows(node, core, mine_ref, other_ref, slice(0, width))
    output = sum(dot_tn(out_ref[m], grad_ref[m]) for m in range(members)) + loss_ref[...]
    split_rows(output, core, mine_ref, other_ref, slice(width, width + TABLE))


def table_kernel(
    core_ref, pre_ref, node_ref, slope_ref, place_ref, rows_ref, grad_ref, mine_ref, other_ref,
):
    members, points, _ = pre_ref.shape
    table_rows = grad_ref.shape[1]
    cast = []
    for m in range(members):
        summed_grad = dot_nt(pre_ref[m], node_ref[...]).astype(jnp.bfloat16)
        table = sum(
            dot(place_ref[:, k * points : (k + 1) * points], summed_grad * slope_ref[m, k])
            for k in range(DEGREE)
        )[:table_rows]
        grad_ref[m] = table
        cast.append(table.astype(jnp.bfloat16))
    term = dot(rows_ref[...], jnp.concatenate(cast, axis=0))
    split_rows(term, core_ref[0], mine_ref, other_ref, slice(0, term.shape[1]))


def params():
    return pltpu.CompilerParams(
        dimension_semantics=("arbitrary",), vmem_limit_bytes=VMEM_LIMIT
    )


def cost(elements, depth, work):
    return pl.CostEstimate(
        flops=elements * (2 * depth + work), bytes_accessed=2 * elements, transcendentals=elements
    )


def whole(array):
    return pl.BlockSpec(array.shape, lambda c: (0,) * array.ndim)


def shards(
    hidden,
    grid_state,
    project_weight,
    node_weight,
    output_weight,
    prior_state,
    target,
    area_weight,
    variable_weight,
    edge_source,
    edge_target,
    edge_count,
    send_index,
):
    members, own_nodes, width = hidden.shape
    points = grid_state.shape[0]
    send_rows = send_index.shape[1]
    variables = output_weight.shape[1]
    slots = edge_source.shape[0]
    core = lax.axis_index("member") % 2
    space = lax.axis_size("space")
    total_points = points * space
    table_rows = own_nodes + 2 * send_rows
    chunks = points // CHUNK

    nodes = jnp.arange(own_nodes, dtype=jnp.int32)
    chosen = (send_index[:, :, None] == nodes).astype(jnp.bfloat16)
    packed = jnp.einsum(
        "dsn,mnh->dmsh", chosen, hidden, preferred_element_type=jnp.float32
    ).astype(jnp.bfloat16)
    forward = [(i, i + 1) for i in range(space - 1)]
    backward = [(i + 1, i) for i in range(space - 1)]
    from_left = lax.ppermute(packed[1], "space", forward)
    from_right = lax.ppermute(packed[0], "space", backward)

    edges = jnp.arange(slots, dtype=jnp.int32)
    live = edges < edge_count[0]
    owner = jnp.where(live, edge_target, points)
    ahead = jnp.pad(owner, (DEGREE - 1, 0), constant_values=-1)
    rank = sum(
        (lax.slice_in_dim(ahead, k, k + slots) == owner).astype(jnp.int32)
        for k in range(DEGREE - 1)
    )
    ranked = jnp.where(
        rank[None, :] == jnp.arange(DEGREE, dtype=jnp.int32)[:, None], edge_source[None, :] + 1, 0
    ).astype(jnp.bfloat16)
    owned = (owner[:, None] == jnp.arange(points, dtype=jnp.int32)).astype(jnp.bfloat16)
    found = jnp.einsum("ke,eg->kg", ranked, owned, preferred_element_type=jnp.float32)
    found = found.astype(jnp.int32)
    slot = jnp.where(found > 0, found - 1, table_rows)
    columns = jnp.arange(TABLE + CHUNK, dtype=jnp.int32)
    within = jnp.arange(CHUNK, dtype=jnp.int32)
    by_chunk = slot.reshape(DEGREE, chunks, CHUNK).transpose(1, 0, 2)
    pick = (
        (by_chunk[..., None] == columns) | ((within[:, None] + TABLE) == columns)
    ).astype(jnp.bfloat16).reshape(chunks, DEGREE * CHUNK, TABLE + CHUNK)
    place = (
        slot.reshape(1, DEGREE * points) == jnp.arange(TABLE, dtype=jnp.int32)[:, None]
    ).astype(jnp.bfloat16)
    output_rows = output_weight.T
    output_padded = jnp.pad(output_rows, ((0, TABLE - variables), (0, 0)))
    scale = variable_weight[:, None]

    source_rows = jnp.concatenate([hidden, from_left, from_right], axis=1)

    chunk_rows = pl.BlockSpec((CHUNK, width), lambda c: (c, 0))
    member_rows = pl.BlockSpec((members, CHUNK, width), lambda c: (0, c, 0))
    pick_block = pl.BlockSpec((1, DEGREE * CHUNK, TABLE + CHUNK), lambda c: (c, 0, 0))
    by_variable = pl.BlockSpec((variables, CHUNK), lambda c: (0, c))
    tiled_rows = -(-variables // 8) * 8
    own_block = pl.BlockSpec((members, tiled_rows, CHUNK), lambda c: (0, 0, c))
    per_point = jax.ShapeDtypeStruct((members, points, width), jnp.bfloat16)
    pred, summed, node_out, comb = pl.pallas_call(
        forward_kernel_with_table,
        grid=(chunks,),
        in_specs=[
            whole(source_rows), whole(project_weight), pick_block, chunk_rows,
            whole(node_weight), whole(output_rows), by_variable,
        ],
        out_specs=[
            own_block, member_rows, member_rows,
            pl.BlockSpec((members, TABLE, width), lambda c: (0, 0, 0)),
        ],
        out_shape=[
            jax.ShapeDtypeStruct((members, tiled_rows, points), jnp.float32), per_point, per_point,
            jax.ShapeDtypeStruct((members, TABLE, width), jnp.bfloat16),
        ],
        scratch_shapes=[
            pltpu.VMEM((members, TABLE + CHUNK, width), jnp.bfloat16),
            pltpu.VMEM((2, DEGREE * CHUNK, TILE), jnp.float32),
        ],
        compiler_params=params(),
        name="forward",
    )(source_rows, project_weight, pick, grid_state, node_weight, output_rows, prior_state)

    def swap(value, flip):
        return lax.ppermute(value, "member", [(i, i ^ flip) for i in range(lax.axis_size("member"))])

    chip_pred = swap(pred, 2)
    core_pred = swap(pred, 1)

    edge_slope = pl.pallas_call(
        edge_slope_kernel,
        grid=(chunks,),
        in_specs=[whole(comb), pick_block, chunk_rows],
        out_specs=pl.BlockSpec((members, DEGREE, CHUNK, width), lambda c: (0, 0, c, 0)),
        out_shape=jax.ShapeDtypeStruct((members, DEGREE, points, width), jnp.bfloat16),
        scratch_shapes=[
            pltpu.VMEM((members, TABLE + CHUNK, width), jnp.bfloat16),
            pltpu.VMEM((2, DEGREE * CHUNK, TILE), jnp.bfloat16),
        ],
        compiler_params=params(),
        cost_estimate=cost(members * DEGREE * points * width, 2 * TABLE, 20),
        name="edge_slopes",
    )(comb, pick, grid_state)
    chip_pred, edge_slope = lax.optimization_barrier((chip_pred, edge_slope))
    far_pred = swap(chip_pred, 1)
    node_slope = pl.pallas_call(
        node_slope_kernel,
        grid=(chunks,),
        in_specs=[member_rows, whole(node_weight)],
        out_specs=member_rows,
        out_shape=per_point,
        scratch_shapes=[pltpu.VMEM((2, DEGREE * CHUNK, TILE), jnp.float32)],
        compiler_params=params(),
        cost_estimate=cost(members * points * width, width, 20),
        name="node_slopes",
    )(summed, node_weight)

    grad_rows, node_pre_grad, loss_row = pl.pallas_call(
        loss_kernel,
        grid=(chunks,),
        in_specs=[
            pl.BlockSpec(memory_space=pltpu.SMEM),
            own_block, own_block, own_block, own_block, by_variable,
            pl.BlockSpec((1, CHUNK), lambda c: (0, c)),
            whole(scale), member_rows, whole(output_padded),
        ],
        out_specs=[
            pl.BlockSpec((members, CHUNK, TABLE), lambda c: (0, c, 0)), member_rows,
            pl.BlockSpec((1, CHUNK), lambda c: (0, 0)),
        ],
        out_shape=[
            jax.ShapeDtypeStruct((members, points, TABLE), jnp.bfloat16), per_point,
            jax.ShapeDtypeStruct((1, CHUNK), jnp.float32),
        ],
        scratch_shapes=[
            pltpu.VMEM((TABLE, CHUNK), jnp.float32), pltpu.VMEM((1, CHUNK), jnp.float32),
        ],
        compiler_params=params(),
        name="loss",
    )(core[None], pred, core_pred, chip_pred, far_pred, target, area_weight[None, :], scale, node_slope, output_padded)

    own_rows = width // space // 2
    smem = pl.BlockSpec(memory_space=pltpu.SMEM)

    def add_partner(mine, other):
        return (mine.astype(jnp.float32) + swap(other, 1).astype(jnp.float32)).astype(jnp.bfloat16)

    def reduce_rows(half):
        moved = lax.all_to_all(half, "space", 0, 0, tiled=True)
        part = jnp.sum(moved.astype(jnp.float32), axis=0)
        mine = part + swap(part, 2)
        other = swap(part, 1) + swap(part, 3)
        return jnp.where(
            core == 0,
            jnp.concatenate([mine, other], axis=0),
            jnp.concatenate([other, mine], axis=0),
        )

    terms_block = pl.BlockSpec(
        (TILE // (2 * own_rows), own_rows, width + TABLE), lambda c: (c, 0, 0)
    )
    terms_shape = jax.ShapeDtypeStruct((space, own_rows, width + TABLE), jnp.bfloat16)
    some_columns = pl.BlockSpec((members, points, TILE), lambda c: (0, 0, c))
    node_mine, node_other = pl.pallas_call(
        node_term_kernel,
        grid=(width // TILE,),
        in_specs=[
            smem, some_columns, some_columns, whole(node_pre_grad), whole(grad_rows),
            whole(loss_row),
        ],
        out_specs=[terms_block, terms_block],
        out_shape=[terms_shape, terms_shape],
        compiler_params=params(),
        cost_estimate=cost(width * width, members * points, 1),
        name="node_terms",
    )(core[None], summed, node_out, node_pre_grad, grad_rows, loss_row)

    source_columns = source_rows.reshape(members * table_rows, width).T
    halves = 2
    tiles = width // TILE // halves

    def table_half(first, pre_grad):
        columns = pl.BlockSpec((space, own_rows, TILE), lambda c: (0, 0, c))
        shape = jax.ShapeDtypeStruct((space, own_rows, tiles * TILE), jnp.bfloat16)
        return pl.pallas_call(
            table_kernel,
            grid=(tiles,),
            in_specs=[
                smem,
                whole(pre_grad),
                pl.BlockSpec((TILE, width), lambda c: (first + c, 0)),
                pl.BlockSpec((members, DEGREE, points, TILE), lambda c: (0, 0, 0, first + c)),
                whole(place),
                whole(source_columns),
            ],
            out_specs=[
                pl.BlockSpec((members, table_rows, TILE), lambda c: (0, 0, c)), columns, columns,
            ],
            out_shape=[
                jax.ShapeDtypeStruct((members, table_rows, tiles * TILE), jnp.float32),
                shape, shape,
            ],
            compiler_params=params(),
            cost_estimate=cost(members * points * width // halves, 4 * width, 8),
            name="table",
        )(core[None], pre_grad, node_weight, edge_slope, place, source_columns)

    first_grad, first_mine, first_other = table_half(0, node_pre_grad)
    node_half = add_partner(node_mine, node_other)
    second_input, node_half, first_mine = lax.optimization_barrier(
        (node_pre_grad, node_half, first_mine)
    )
    node_sums = reduce_rows(node_half)
    first_half = add_partner(first_mine, first_other)
    second_grad, second_mine, second_other = table_half(tiles, second_input)
    second_half = add_partner(second_mine, second_other)

    table_grad = jnp.concatenate([first_grad, second_grad], axis=2)
    left_back = lax.ppermute(
        table_grad[:, own_nodes : own_nodes + send_rows].astype(jnp.bfloat16), "space", backward
    )
    right_back = lax.ppermute(
        table_grad[:, own_nodes + send_rows :].astype(jnp.bfloat16), "space", forward
    )
    project_half = jnp.concatenate([first_half, second_half], axis=2)
    project_half, left_back, right_back = lax.optimization_barrier(
        (project_half, left_back, right_back)
    )
    project_sum = reduce_rows(project_half)
    projected_grad = (
        table_grad[:, :own_nodes]
        + jnp.einsum(
            "sn,msh->mnh", chosen[1], left_back, preferred_element_type=jnp.float32
        )
        + jnp.einsum(
            "sn,msh->mnh", chosen[0], right_back, preferred_element_type=jnp.float32
        )
    ).astype(jnp.bfloat16)
    grad_hidden = jnp.einsum(
        "mnk,hk->mnh", projected_grad, project_weight, preferred_element_type=jnp.float32
    ).astype(jnp.bfloat16)
    loss_at = width + variables
    return (
        grad_hidden,
        project_sum / total_points,
        node_sums[:, :width] / total_points,
        node_sums[:, width:loss_at] / total_points,
        jnp.sum(node_sums[0, loss_at:]) / (total_points * variables),
    )


def forward_kernel_with_table(*refs):
    inputs, (pred_ref, summed_ref, out_ref, table_ref, comb_ref, work_ref) = refs[:7], refs[7:]
    forward_kernel(*inputs, pred_ref, summed_ref, out_ref, comb_ref, work_ref)

    @pl.when(pl.program_id(0) == 0)
    def _():
        table_ref[...] = comb_ref[:, :TABLE]


def solution(mesh):
    placed = (
        P("member", "space", None),
        P("space", None),
        P(),
        P(),
        P(),
        P(None, "space"),
        P(None, "space"),
        P("space"),
        P(),
        P("space"),
        P("space"),
        P("space"),
        P("space", None),
    )
    return jax.shard_map(
        shards,
        mesh=mesh,
        in_specs=placed,
        out_specs=(
            P("member", "space", None),
            P("space", None),
            P("space", None),
            P("space", None),
            P(),
        ),
        check_vma=False,
    )
```

```python
import functools

import jax
import jax.numpy as jnp
from jax import lax
from jax.experimental import pallas as pl
from jax.experimental.pallas import tpu as pltpu
from jax.sharding import PartitionSpec as P

SQRT_TWO_PI = 0.7978845608028654
CUBIC = 0.044715
ALPHA = 0.95
SOFT_EDGE = 0.05
DEGREE = 4
TABLE = 128
EMPTY = -64.0
CHUNK = 128
TILE = 256
PART = 32
LANES = 128


def tanh_of(u):
    s = u * u
    return s, jnp.tanh(u * (SQRT_TWO_PI + (SQRT_TWO_PI * CUBIC) * s))


def gelu_twice(u):
    _, t = tanh_of(u)
    return u + u * t


def slope_twice(u, s=None, t=None):
    if t is None:
        s, t = tanh_of(u)
    q = u * (SQRT_TWO_PI + (3.0 * SQRT_TWO_PI * CUBIC) * s)
    return (1.0 + t) * (1.0 + (1.0 - t) * q)


def dot(left, right):
    return lax.dot_general(
        left, right, (((1,), (0,)), ((), ())), preferred_element_type=jnp.float32
    )


def dot_nt(left, right):
    return lax.dot_general(
        left, right, (((1,), (1,)), ((), ())), preferred_element_type=jnp.float32
    )


def parts(rows):
    return [(r, c) for r in range(0, rows, PART) for c in range(0, TILE, LANES)]


def staged(tiles, work_ref, matmul, finish):
    for i, tile in enumerate(tiles):
        result = matmul(*tile)
        work_ref[i % 2][: result.shape[0]] = result.astype(work_ref[0].dtype)
        if i:
            finish(work_ref[(i - 1) % 2], *tiles[i - 1])
    finish(work_ref[(len(tiles) - 1) % 2], *tiles[-1])


def edge_stage(pick_ref, comb_ref, work_ref, finish):
    members, _, width = comb_ref.shape
    tiles = [(m, h) for m in range(members) for h in range(0, width, TILE)]
    staged(
        tiles, work_ref, lambda m, h: dot(pick_ref[0], comb_ref[m, :, h : h + TILE]), finish
    )


def node_stage(summed_ref, node_ref, work_ref, finish):
    members, rows, width = summed_ref.shape

    def matmul(h):
        return dot(summed_ref[...].reshape(members * rows, width), node_ref[:, h : h + TILE])

    def finish_all(buffer, h):
        for m in range(members):
            finish(buffer.at[m * rows : (m + 1) * rows], m, h)

    staged([(h,) for h in range(0, width, TILE)], work_ref, matmul, finish_all)


def forward_kernel(
    rows_ref, project_ref, pick_ref, grid_ref, node_ref, output_ref, prior_ref,
    pred_ref, summed_ref, out_ref, slope_ref, comb_ref, *work_ref,
):
    members, table_rows, width = rows_ref.shape

    @pl.when(pl.program_id(0) == 0)
    def _():
        for m in range(members):
            comb_ref[m, :table_rows] = dot(rows_ref[m], project_ref[...]).astype(jnp.bfloat16)
            comb_ref[m, table_rows:TABLE] = jnp.full(
                (TABLE - table_rows, width), EMPTY, jnp.bfloat16
            )

    for m in range(members):
        comb_ref[m, TABLE:] = grid_ref[...]

    def sum_edges(buffer, m, h):
        for r, c in parts(CHUNK):
            twice = sum(
                gelu_twice(buffer[k * CHUNK + r : k * CHUNK + r + PART, c : c + LANES])
                for k in range(DEGREE)
            )
            summed_ref[m, r : r + PART, h + c : h + c + LANES] = (0.5 * twice).astype(jnp.bfloat16)

    def node_values(buffer, m, h):
        for r, c in parts(CHUNK):
            u = buffer[r : r + PART, c : c + LANES]
            s, t = tanh_of(u)
            place = (m, slice(r, r + PART), slice(h + c, h + c + LANES))
            out_ref[place] = (0.5 * (u + u * t)).astype(jnp.bfloat16)
            slope_ref[place] = (0.5 * slope_twice(u, s, t)).astype(jnp.bfloat16)

    edge_stage(pick_ref, comb_ref, work_ref, sum_edges)
    node_stage(summed_ref, node_ref, work_ref, node_values)
    for m in range(members):
        pred_ref[m] = jnp.zeros(pred_ref.shape[1:], jnp.float32)
        pred_ref[m, : prior_ref.shape[0]] = prior_ref[...] + dot_nt(output_ref[...], out_ref[m])


def edge_slope_kernel(comb_ref, pick_ref, grid_ref, edge_ref, both_ref, *work_ref):
    for m in range(comb_ref.shape[0]):
        both_ref[m, :TABLE] = comb_ref[m]
        both_ref[m, TABLE:] = grid_ref[...]

    def edge_slopes(buffer, m, h):
        for k in range(DEGREE):
            for r, c in parts(CHUNK):
                value = slope_twice(buffer[k * CHUNK + r : k * CHUNK + r + PART, c : c + LANES])
                edge_ref[m, k, r : r + PART, h + c : h + c + LANES] = value * 0.5

    edge_stage(pick_ref, both_ref, work_ref, edge_slopes)


def loss_kernel(
    core_index_ref, own_ref, core_ref, chip_ref, far_ref, truth_ref, area_ref, variable_ref, slope_ref, output_ref,
    grad_ref, pre_ref, loss_ref, tall_ref, sum_ref,
):
    members = own_ref.shape[0]
    variables = truth_ref.shape[0]
    width = output_ref.shape[1]
    everyone = 4 * members
    fairness = 1.0 - (1.0 - ALPHA) / everyone
    edge = SOFT_EDGE * SOFT_EDGE

    @pl.when(pl.program_id(0) == 0)
    def _():
        sum_ref[...] = jnp.zeros_like(sum_ref)
        tall_ref[...] = jnp.zeros_like(tall_ref)

    everyones = [ref.at[k] for ref in (own_ref, core_ref, chip_ref, far_ref) for k in range(members)]
    total = jnp.zeros((1, CHUNK), jnp.float32)
    for first in range(0, variables, PART):
        rows = slice(first, min(first + PART, variables))
        weight = variable_ref[rows] * area_ref[...]
        truth = truth_ref[rows]
        terms = jnp.zeros_like(truth)
        for j in range(members):
            own = own_ref[j, rows]
            pair_abs = jnp.full_like(truth, -everyone * SOFT_EDGE)
            pair_sign = jnp.zeros_like(truth)
            for other in everyones:
                d = own - other[rows]
                square = d * d + edge
                r = lax.rsqrt(square)
                pair_abs = pair_abs + square * r
                pair_sign = pair_sign + d * r
            d = own - truth
            square = d * d + edge
            r = lax.rsqrt(square)
            terms = terms + (
                (square * r - SOFT_EDGE) / everyone
                - fairness / (2.0 * everyone * (everyone - 1)) * pair_abs
            )
            tall_ref[j, rows] = weight * (d * r - fairness / (everyone - 1) * pair_sign)
        total = total + jnp.sum(weight * terms, axis=0, keepdims=True)
    sum_ref[...] += total
    grads = []
    for j in range(members):
        tall = tall_ref[j].T.astype(jnp.bfloat16)
        grad_ref[j] = tall
        grads.append(tall)

    @pl.when(pl.program_id(0) == pl.num_programs(0) - 1)
    def _():
        rest = jnp.sum(sum_ref[...], axis=1, keepdims=True)
        lane = lax.broadcasted_iota(jnp.int32, (1, CHUNK), 1)
        row = jnp.zeros((1, CHUNK), jnp.float32)
        for part in range(3):
            piece = rest.astype(jnp.bfloat16).astype(jnp.float32)
            row = jnp.where(lane == variables + 3 * core_index_ref[0] + part, piece, row)
            rest = rest - piece
        loss_ref[...] = row

    stacked = jnp.concatenate(grads, axis=0)
    for h in range(0, width, TILE):
        node_grad = dot(stacked, output_ref[:, h : h + TILE]).reshape(members, CHUNK, TILE)
        slope = slope_ref[:, :, h : h + TILE].astype(jnp.float32)
        pre_ref[:, :, h : h + TILE] = (node_grad * slope).astype(jnp.bfloat16)


def dot_tn(left, right):
    return lax.dot_general(
        left, right, (((0,), (0,)), ((), ())), preferred_element_type=jnp.float32
    )


def split_rows(value, core, mine_ref, other_ref, columns):
    rows = mine_ref.shape[1]
    pairs = value.reshape(value.shape[0] // (2 * rows), 2, rows, value.shape[1])
    first, second = pairs[:, 0], pairs[:, 1]
    mine_ref[:, :, columns] = jnp.where(core == 0, first, second).astype(jnp.bfloat16)
    other_ref[:, :, columns] = jnp.where(core == 0, second, first).astype(jnp.bfloat16)


def node_term_kernel(
    core_ref, summed_ref, out_ref, pre_ref, grad_ref, loss_ref, mine_ref, other_ref,
):
    members, _, width = pre_ref.shape
    core = core_ref[0]
    node = sum(dot_tn(summed_ref[m], pre_ref[m]) for m in range(members))
    split_rows(node, core, mine_ref, other_ref, slice(0, width))
    output = sum(dot_tn(out_ref[m], grad_ref[m]) for m in range(members)) + loss_ref[...]
    split_rows(output, core, mine_ref, other_ref, slice(width, width + TABLE))


def table_kernel(
    core_ref, pre_ref, node_ref, slope_ref, place_ref, rows_ref, grad_ref, mine_ref, other_ref,
):
    members, points, _ = pre_ref.shape
    table_rows = grad_ref.shape[1]
    cast = []
    for m in range(members):
        summed_grad = dot_nt(pre_ref[m], node_ref[...]).astype(jnp.bfloat16)
        table = sum(
            dot(place_ref[:, k * points : (k + 1) * points], summed_grad * slope_ref[m, k])
            for k in range(DEGREE)
        )[:table_rows]
        grad_ref[m] = table
        cast.append(table.astype(jnp.bfloat16))
    term = dot(rows_ref[...], jnp.concatenate(cast, axis=0))
    split_rows(term, core_ref[0], mine_ref, other_ref, slice(0, term.shape[1]))


def params(mebibytes):
    return pltpu.CompilerParams(
        dimension_semantics=("arbitrary",), vmem_limit_bytes=mebibytes * 1024 * 1024
    )


def cost(elements, depth, work):
    return pl.CostEstimate(
        flops=elements * (2 * depth + work), bytes_accessed=2 * elements, transcendentals=elements
    )


def whole(array):
    return pl.BlockSpec(array.shape, lambda c: (0,) * array.ndim)


def shards(
    hidden,
    grid_state,
    project_weight,
    node_weight,
    output_weight,
    prior_state,
    target,
    area_weight,
    variable_weight,
    edge_source,
    edge_target,
    edge_count,
    send_index,
):
    members, own_nodes, width = hidden.shape
    points = grid_state.shape[0]
    send_rows = send_index.shape[1]
    variables = output_weight.shape[1]
    slots = edge_source.shape[0]
    core = lax.axis_index("member") % 2
    space = lax.axis_size("space")
    total_points = points * space
    table_rows = own_nodes + 2 * send_rows
    chunks = points // CHUNK

    nodes = jnp.arange(own_nodes, dtype=jnp.int32)
    chosen = (send_index[:, :, None] == nodes).astype(jnp.bfloat16)
    packed = jnp.einsum(
        "dsn,mnh->dmsh", chosen, hidden, preferred_element_type=jnp.float32
    ).astype(jnp.bfloat16)
    forward = [(i, i + 1) for i in range(space - 1)]
    backward = [(i + 1, i) for i in range(space - 1)]
    from_left = lax.ppermute(packed[1], "space", forward)
    from_right = lax.ppermute(packed[0], "space", backward)

    edges = jnp.arange(slots, dtype=jnp.int32)
    live = edges < edge_count[0]
    owner = jnp.where(live, edge_target, points)
    ahead = jnp.pad(owner, (DEGREE - 1, 0), constant_values=-1)
    rank = sum(
        (lax.slice_in_dim(ahead, k, k + slots) == owner).astype(jnp.int32)
        for k in range(DEGREE - 1)
    )
    ranked = jnp.where(
        rank[None, :] == jnp.arange(DEGREE, dtype=jnp.int32)[:, None], edge_source[None, :] + 1, 0
    ).astype(jnp.bfloat16)
    owned = (owner[:, None] == jnp.arange(points, dtype=jnp.int32)).astype(jnp.bfloat16)
    found = jnp.einsum("ke,eg->kg", ranked, owned, preferred_element_type=jnp.float32)
    found = found.astype(jnp.int32)
    slot = jnp.where(found > 0, found - 1, table_rows)
    columns = jnp.arange(TABLE + CHUNK, dtype=jnp.int32)
    within = jnp.arange(CHUNK, dtype=jnp.int32)
    by_chunk = slot.reshape(DEGREE, chunks, CHUNK).transpose(1, 0, 2)
    pick = (
        (by_chunk[..., None] == columns) | ((within[:, None] + TABLE) == columns)
    ).astype(jnp.bfloat16).reshape(chunks, DEGREE * CHUNK, TABLE + CHUNK)
    place = (
        slot.reshape(1, DEGREE * points) == jnp.arange(TABLE, dtype=jnp.int32)[:, None]
    ).astype(jnp.bfloat16)
    output_rows = output_weight.T
    output_padded = jnp.pad(output_rows, ((0, TABLE - variables), (0, 0)))
    scale = variable_weight[:, None]

    source_rows = jnp.concatenate([hidden, from_left, from_right], axis=1)

    chunk_rows = pl.BlockSpec((CHUNK, width), lambda c: (c, 0))
    member_rows = pl.BlockSpec((members, CHUNK, width), lambda c: (0, c, 0))
    pick_block = pl.BlockSpec((1, DEGREE * CHUNK, TABLE + CHUNK), lambda c: (c, 0, 0))
    by_variable = pl.BlockSpec((variables, CHUNK), lambda c: (0, c))
    tiled_rows = -(-variables // 8) * 8
    own_block = pl.BlockSpec((members, tiled_rows, CHUNK), lambda c: (0, 0, c))
    per_point = jax.ShapeDtypeStruct((members, points, width), jnp.bfloat16)
    pred, summed, node_out, node_slope, comb = pl.pallas_call(
        forward_kernel_with_table,
        grid=(chunks,),
        in_specs=[
            whole(source_rows), whole(project_weight), pick_block, chunk_rows,
            whole(node_weight), whole(output_rows), by_variable,
        ],
        out_specs=[
            own_block, member_rows, member_rows, member_rows,
            pl.BlockSpec((members, TABLE, width), lambda c: (0, 0, 0)),
        ],
        out_shape=[
            jax.ShapeDtypeStruct((members, tiled_rows, points), jnp.float32), per_point, per_point,
            per_point, jax.ShapeDtypeStruct((members, TABLE, width), jnp.bfloat16),
        ],
        scratch_shapes=[
            pltpu.VMEM((members, TABLE + CHUNK, width), jnp.bfloat16),
            pltpu.VMEM((DEGREE * CHUNK, TILE), jnp.float32),
            pltpu.VMEM((DEGREE * CHUNK, TILE), jnp.float32),
        ],
        compiler_params=params(30),
        name="forward",
    )(source_rows, project_weight, pick, grid_state, node_weight, output_rows, prior_state)

    def swap(value, flip):
        return lax.ppermute(value, "member", [(i, i ^ flip) for i in range(lax.axis_size("member"))])

    chip_pred = swap(pred, 2)
    core_pred = swap(pred, 1)

    edge_slope = pl.pallas_call(
        edge_slope_kernel,
        grid=(chunks,),
        in_specs=[whole(comb), pick_block, chunk_rows],
        out_specs=pl.BlockSpec((members, DEGREE, CHUNK, width), lambda c: (0, 0, c, 0)),
        out_shape=jax.ShapeDtypeStruct((members, DEGREE, points, width), jnp.bfloat16),
        scratch_shapes=[
            pltpu.VMEM((members, TABLE + CHUNK, width), jnp.bfloat16),
            pltpu.VMEM((DEGREE * CHUNK, TILE), jnp.bfloat16),
            pltpu.VMEM((DEGREE * CHUNK, TILE), jnp.bfloat16),
        ],
        compiler_params=params(24),
        cost_estimate=cost(members * DEGREE * points * width, 2 * TABLE, 20),
        name="edge_slopes",
    )(comb, pick, grid_state)
    chip_pred, edge_slope = lax.optimization_barrier((chip_pred, edge_slope))
    far_pred = swap(chip_pred, 1)
    grad_rows, node_pre_grad, loss_row = pl.pallas_call(
        loss_kernel,
        grid=(chunks,),
        in_specs=[
            pl.BlockSpec(memory_space=pltpu.SMEM),
            own_block, own_block, own_block, own_block, by_variable,
            pl.BlockSpec((1, CHUNK), lambda c: (0, c)),
            whole(scale), member_rows, whole(output_padded),
        ],
        out_specs=[
            pl.BlockSpec((members, CHUNK, TABLE), lambda c: (0, c, 0)), member_rows,
            pl.BlockSpec((1, CHUNK), lambda c: (0, 0)),
        ],
        out_shape=[
            jax.ShapeDtypeStruct((members, points, TABLE), jnp.bfloat16), per_point,
            jax.ShapeDtypeStruct((1, CHUNK), jnp.float32),
        ],
        scratch_shapes=[
            pltpu.VMEM((members, TABLE, CHUNK), jnp.float32), pltpu.VMEM((1, CHUNK), jnp.float32),
        ],
        compiler_params=params(16),
        name="loss",
    )(core[None], pred, core_pred, chip_pred, far_pred, target, area_weight[None, :], scale, node_slope, output_padded)

    own_rows = width // space // 2
    smem = pl.BlockSpec(memory_space=pltpu.SMEM)

    def add_partner(mine, other):
        return (mine.astype(jnp.float32) + swap(other, 1).astype(jnp.float32)).astype(jnp.bfloat16)

    def sum_space(half):
        moved = lax.all_to_all(half, "space", 0, 0, tiled=True)
        return jnp.sum(moved.astype(jnp.float32), axis=0)

    def sum_members(part):
        mine = part + swap(part, 2)
        other = swap(part, 1) + swap(part, 3)
        return jnp.where(
            core == 0,
            jnp.concatenate([mine, other], axis=0),
            jnp.concatenate([other, mine], axis=0),
        )

    terms_block = pl.BlockSpec(
        (TILE // (2 * own_rows), own_rows, width + TABLE), lambda c: (c, 0, 0)
    )
    terms_shape = jax.ShapeDtypeStruct((space, own_rows, width + TABLE), jnp.bfloat16)
    some_columns = pl.BlockSpec((members, points, TILE), lambda c: (0, 0, c))
    node_mine, node_other = pl.pallas_call(
        node_term_kernel,
        grid=(width // TILE,),
        in_specs=[
            smem, some_columns, some_columns, whole(node_pre_grad), whole(grad_rows),
            whole(loss_row),
        ],
        out_specs=[terms_block, terms_block],
        out_shape=[terms_shape, terms_shape],
        compiler_params=params(32),
        cost_estimate=cost(width * width, members * points, 1),
        name="node_terms",
    )(core[None], summed, node_out, node_pre_grad, grad_rows, loss_row)

    source_columns = source_rows.reshape(members * table_rows, width).T
    halves = 2
    tiles = width // TILE // halves

    def table_half(first, pre_grad):
        columns = pl.BlockSpec((space, own_rows, TILE), lambda c: (0, 0, c))
        shape = jax.ShapeDtypeStruct((space, own_rows, tiles * TILE), jnp.bfloat16)
        return pl.pallas_call(
            table_kernel,
            grid=(tiles,),
            in_specs=[
                smem,
                whole(pre_grad),
                pl.BlockSpec((TILE, width), lambda c: (first + c, 0)),
                pl.BlockSpec((members, DEGREE, points, TILE), lambda c: (0, 0, 0, first + c)),
                whole(place),
                whole(source_columns),
            ],
            out_specs=[
                pl.BlockSpec((members, table_rows, TILE), lambda c: (0, 0, c)), columns, columns,
            ],
            out_shape=[
                jax.ShapeDtypeStruct((members, table_rows, tiles * TILE), jnp.float32),
                shape, shape,
            ],
            compiler_params=params(40),
            cost_estimate=cost(members * points * width // halves, 4 * width, 8),
            name="table",
        )(core[None], pre_grad, node_weight, edge_slope, place, source_columns)

    first_grad, first_mine, first_other = table_half(0, node_pre_grad)
    node_half = add_partner(node_mine, node_other)
    second_input, node_half, first_mine = lax.optimization_barrier(
        (node_pre_grad, node_half, first_mine)
    )
    node_part = sum_space(node_half)
    first_half = add_partner(first_mine, first_other)
    second_grad, second_mine, second_other = table_half(tiles, second_input)
    second_half = add_partner(second_mine, second_other)

    table_grad = jnp.concatenate([first_grad, second_grad], axis=2)
    left_back = lax.ppermute(
        table_grad[:, own_nodes : own_nodes + send_rows].astype(jnp.bfloat16), "space", backward
    )
    right_back = lax.ppermute(
        table_grad[:, own_nodes + send_rows :].astype(jnp.bfloat16), "space", forward
    )
    project_half = jnp.concatenate([first_half, second_half], axis=2)
    project_half, node_part, left_back, right_back = lax.optimization_barrier(
        (project_half, node_part, left_back, right_back)
    )
    sums = sum_members(jnp.concatenate([sum_space(project_half), node_part], axis=1))
    projected_grad = (
        table_grad[:, :own_nodes]
        + jnp.einsum(
            "sn,msh->mnh", chosen[1], left_back, preferred_element_type=jnp.float32
        )
        + jnp.einsum(
            "sn,msh->mnh", chosen[0], right_back, preferred_element_type=jnp.float32
        )
    ).astype(jnp.bfloat16)
    grad_hidden = jnp.einsum(
        "mnk,hk->mnh", projected_grad, project_weight, preferred_element_type=jnp.float32
    ).astype(jnp.bfloat16)
    output_at = 2 * width
    loss_at = output_at + variables
    return (
        grad_hidden,
        sums[:, :width] / total_points,
        sums[:, width:output_at] / total_points,
        sums[:, output_at:loss_at] / total_points,
        jnp.sum(sums[0, loss_at:]) / (total_points * variables),
    )


def forward_kernel_with_table(*refs):
    table_ref, comb_ref = refs[11:13]
    forward_kernel(*refs[:11], *refs[12:])

    @pl.when(pl.program_id(0) == 0)
    def _():
        table_ref[...] = comb_ref[:, :TABLE]


def solution(mesh):
    placed = (
        P("member", "space", None),
        P("space", None),
        P(),
        P(),
        P(),
        P(None, "space"),
        P(None, "space"),
        P("space"),
        P(),
        P("space"),
        P("space"),
        P("space"),
        P("space", None),
    )
    return jax.shard_map(
        shards,
        mesh=mesh,
        in_specs=placed,
        out_specs=(
            P("member", "space", None),
            P("space", None),
            P("space", None),
            P("space", None),
            P(),
        ),
        check_vma=False,
    )
```

```python
import functools

import jax
import jax.numpy as jnp
from jax import lax
from jax.experimental import pallas as pl
from jax.experimental.pallas import tpu as pltpu
from jax.sharding import PartitionSpec as P

SQRT_TWO_PI = 0.7978845608028654
CUBIC = 0.044715
ALPHA = 0.95
SOFT_EDGE = 0.05
DEGREE = 4
TABLE = 128
EMPTY = -64.0
CHUNK = 128
TILE = 256
PART = 32
PIECES = 2
VMEM_LIMIT = 56 * 1024 * 1024
LANES = 128


def tanh_of(u):
    s = u * u
    return s, jnp.tanh(u * (SQRT_TWO_PI + (SQRT_TWO_PI * CUBIC) * s))


def gelu_twice(u):
    _, t = tanh_of(u)
    return u + u * t


def slope_twice(u, s=None, t=None):
    if t is None:
        s, t = tanh_of(u)
    q = u * (SQRT_TWO_PI + (3.0 * SQRT_TWO_PI * CUBIC) * s)
    return (1.0 + t) * (1.0 + (1.0 - t) * q)


def dot(left, right):
    return lax.dot_general(
        left, right, (((1,), (0,)), ((), ())), preferred_element_type=jnp.float32
    )


def dot_nt(left, right):
    return lax.dot_general(
        left, right, (((1,), (1,)), ((), ())), preferred_element_type=jnp.float32
    )


def blocks(rows, piece):
    share = rows // PIECES
    first = piece * share
    return [(r, c) for r in range(first, first + share, PART) for c in range(0, TILE, LANES)]


def staged(tiles, work_ref, matmul, finish):
    for i in range(len(tiles) + 1):
        for piece in range(PIECES):
            if i < len(tiles):
                result = matmul(*tiles[i], piece)
                rows = result.shape[0]
                work_ref[i % 2][piece * rows : (piece + 1) * rows] = result
            if i:
                finish(work_ref[(i - 1) % 2], *tiles[i - 1], piece)


def edge_stage(pick_ref, comb_ref, work_ref, finish):
    members, _, width = comb_ref.shape
    tiles = [(m, h) for m in range(members) for h in range(0, width, TILE)]
    rows = pick_ref.shape[1] // PIECES

    def matmul(m, h, piece):
        return dot(pick_ref[0, piece * rows : (piece + 1) * rows], comb_ref[m, :, h : h + TILE])

    staged(tiles, work_ref, matmul, finish)


def node_stage(summed_ref, node_ref, work_ref, finish):
    members, rows, width = summed_ref.shape
    share = members // PIECES

    def matmul(h, piece):
        some = summed_ref[piece * share : (piece + 1) * share].reshape(share * rows, width)
        return dot(some, node_ref[:, h : h + TILE])

    def finish_members(buffer, h, piece):
        for m in range(piece * share, (piece + 1) * share):
            finish(buffer, m * rows, m, h)

    staged([(h,) for h in range(0, width, TILE)], work_ref, matmul, finish_members)


def forward_kernel(
    rows_ref, project_ref, pick_ref, grid_ref, node_ref, output_ref, prior_ref,
    pred_ref, summed_ref, out_ref, slope_ref, comb_ref, *work_ref,
):
    members, table_rows, width = rows_ref.shape

    @pl.when(pl.program_id(0) == 0)
    def _():
        for m in range(members):
            comb_ref[m, :table_rows] = dot(rows_ref[m], project_ref[...]).astype(jnp.bfloat16)
            comb_ref[m, table_rows:TABLE] = jnp.full(
                (TABLE - table_rows, width), EMPTY, jnp.bfloat16
            )

    for m in range(members):
        comb_ref[m, TABLE:] = grid_ref[...]

    def sum_edges(buffer, m, h, piece):
        for r, c in blocks(CHUNK, piece):
            twice = sum(
                gelu_twice(buffer[k * CHUNK + r : k * CHUNK + r + PART, c : c + LANES])
                for k in range(DEGREE)
            )
            summed_ref[m, r : r + PART, h + c : h + c + LANES] = (0.5 * twice).astype(jnp.bfloat16)

    def node_values(buffer, first, m, h):
        for r in range(0, CHUNK, PART):
            for c in range(0, TILE, LANES):
                u = buffer[first + r : first + r + PART, c : c + LANES]
                s, t = tanh_of(u)
                place = (m, slice(r, r + PART), slice(h + c, h + c + LANES))
                out_ref[place] = (0.5 * (u + u * t)).astype(jnp.bfloat16)
                slope_ref[place] = (0.5 * slope_twice(u, s, t)).astype(jnp.bfloat16)

    edge_stage(pick_ref, comb_ref, work_ref, sum_edges)
    node_stage(summed_ref, node_ref, work_ref, node_values)
    for m in range(members):
        pred_ref[m] = jnp.zeros(pred_ref.shape[1:], jnp.float32)
        pred_ref[m, : prior_ref.shape[0]] = prior_ref[...] + dot_nt(output_ref[...], out_ref[m])


def edge_slope_kernel(comb_ref, pick_ref, grid_ref, edge_ref, both_ref, *work_ref):
    for m in range(comb_ref.shape[0]):
        both_ref[m, :TABLE] = comb_ref[m]
        both_ref[m, TABLE:] = grid_ref[...]

    def edge_slopes(buffer, m, h, piece):
        for k in range(DEGREE):
            for r, c in blocks(CHUNK, piece):
                value = 0.5 * slope_twice(
                    buffer[k * CHUNK + r : k * CHUNK + r + PART, c : c + LANES]
                )
                edge_ref[m, k, r : r + PART, h + c : h + c + LANES] = value.astype(jnp.bfloat16)

    edge_stage(pick_ref, both_ref, work_ref, edge_slopes)


def loss_kernel(
    core_index_ref, own_ref, core_ref, chip_ref, far_ref, truth_ref, area_ref, variable_ref, slope_ref, output_ref,
    grad_ref, pre_ref, loss_ref, tall_ref, sum_ref,
):
    members = own_ref.shape[0]
    variables = truth_ref.shape[0]
    width = output_ref.shape[1]
    everyone = 4 * members
    fairness = 1.0 - (1.0 - ALPHA) / everyone
    edge = SOFT_EDGE * SOFT_EDGE

    @pl.when(pl.program_id(0) == 0)
    def _():
        sum_ref[...] = jnp.zeros_like(sum_ref)
        tall_ref[...] = jnp.zeros_like(tall_ref)

    everyones = [ref.at[k] for ref in (own_ref, core_ref, chip_ref, far_ref) for k in range(members)]
    total = jnp.zeros((1, CHUNK), jnp.float32)
    for first in range(0, variables, PART):
        rows = slice(first, min(first + PART, variables))
        weight = variable_ref[rows] * area_ref[...]
        truth = truth_ref[rows]
        terms = jnp.zeros_like(truth)
        for j in range(members):
            own = own_ref[j, rows]
            pair_abs = jnp.full_like(truth, -everyone * SOFT_EDGE)
            pair_sign = jnp.zeros_like(truth)
            for other in everyones:
                d = own - other[rows]
                square = d * d + edge
                r = lax.rsqrt(square)
                pair_abs = pair_abs + square * r
                pair_sign = pair_sign + d * r
            d = own - truth
            square = d * d + edge
            r = lax.rsqrt(square)
            terms = terms + (
                (square * r - SOFT_EDGE) / everyone
                - fairness / (2.0 * everyone * (everyone - 1)) * pair_abs
            )
            tall_ref[j, rows] = weight * (d * r - fairness / (everyone - 1) * pair_sign)
        total = total + jnp.sum(weight * terms, axis=0, keepdims=True)
    sum_ref[...] += total
    grads = []
    for j in range(members):
        tall = tall_ref[j].T.astype(jnp.bfloat16)
        grad_ref[j] = tall
        grads.append(tall)

    @pl.when(pl.program_id(0) == pl.num_programs(0) - 1)
    def _():
        rest = jnp.sum(sum_ref[...], axis=1, keepdims=True)
        lane = lax.broadcasted_iota(jnp.int32, (1, CHUNK), 1)
        row = jnp.zeros((1, CHUNK), jnp.float32)
        for part in range(3):
            piece = rest.astype(jnp.bfloat16).astype(jnp.float32)
            row = jnp.where(lane == variables + 3 * core_index_ref[0] + part, piece, row)
            rest = rest - piece
        loss_ref[...] = row

    stacked = jnp.concatenate(grads, axis=0)
    for h in range(0, width, TILE):
        node_grad = dot(stacked, output_ref[:, h : h + TILE]).reshape(members, CHUNK, TILE)
        slope = slope_ref[:, :, h : h + TILE].astype(jnp.float32)
        pre_ref[:, :, h : h + TILE] = (node_grad * slope).astype(jnp.bfloat16)


def dot_tn(left, right):
    return lax.dot_general(
        left, right, (((0,), (0,)), ((), ())), preferred_element_type=jnp.float32
    )


def split_rows(value, core, mine_ref, other_ref, columns):
    rows = mine_ref.shape[1]
    pairs = value.reshape(value.shape[0] // (2 * rows), 2, rows, value.shape[1])
    first, second = pairs[:, 0], pairs[:, 1]
    mine_ref[:, :, columns] = jnp.where(core == 0, first, second).astype(jnp.bfloat16)
    other_ref[:, :, columns] = jnp.where(core == 0, second, first).astype(jnp.bfloat16)


def node_term_kernel(
    core_ref, summed_ref, out_ref, pre_ref, grad_ref, loss_ref, mine_ref, other_ref,
):
    members, _, width = pre_ref.shape
    core = core_ref[0]
    node = sum(dot_tn(summed_ref[m], pre_ref[m]) for m in range(members))
    split_rows(node, core, mine_ref, other_ref, slice(0, width))
    output = sum(dot_tn(out_ref[m], grad_ref[m]) for m in range(members)) + loss_ref[...]
    split_rows(output, core, mine_ref, other_ref, slice(width, width + TABLE))


def table_kernel(
    core_ref, pre_ref, node_ref, slope_ref, place_ref, rows_ref, grad_ref, mine_ref, other_ref,
):
    members, points, _ = pre_ref.shape
    table_rows = grad_ref.shape[1]
    cast = []
    for m in range(members):
        summed_grad = dot_nt(pre_ref[m], node_ref[...]).astype(jnp.bfloat16)
        table = sum(
            dot(place_ref[:, k * points : (k + 1) * points], summed_grad * slope_ref[m, k])
            for k in range(DEGREE)
        )[:table_rows]
        grad_ref[m] = table
        cast.append(table.astype(jnp.bfloat16))
    term = dot(rows_ref[...], jnp.concatenate(cast, axis=0))
    split_rows(term, core_ref[0], mine_ref, other_ref, slice(0, term.shape[1]))


def params():
    return pltpu.CompilerParams(
        dimension_semantics=("arbitrary",), vmem_limit_bytes=VMEM_LIMIT
    )


def cost(elements, depth, work):
    return pl.CostEstimate(
        flops=elements * (2 * depth + work), bytes_accessed=2 * elements, transcendentals=elements
    )


def whole(array):
    return pl.BlockSpec(array.shape, lambda c: (0,) * array.ndim)


def shards(
    hidden,
    grid_state,
    project_weight,
    node_weight,
    output_weight,
    prior_state,
    target,
    area_weight,
    variable_weight,
    edge_source,
    edge_target,
    edge_count,
    send_index,
):
    members, own_nodes, width = hidden.shape
    points = grid_state.shape[0]
    send_rows = send_index.shape[1]
    variables = output_weight.shape[1]
    slots = edge_source.shape[0]
    core = lax.axis_index("member") % 2
    space = lax.axis_size("space")
    total_points = points * space
    table_rows = own_nodes + 2 * send_rows
    chunks = points // CHUNK

    nodes = jnp.arange(own_nodes, dtype=jnp.int32)
    chosen = (send_index[:, :, None] == nodes).astype(jnp.bfloat16)
    packed = jnp.einsum(
        "dsn,mnh->dmsh", chosen, hidden, preferred_element_type=jnp.float32
    ).astype(jnp.bfloat16)
    forward = [(i, i + 1) for i in range(space - 1)]
    backward = [(i + 1, i) for i in range(space - 1)]
    from_left = lax.ppermute(packed[1], "space", forward)
    from_right = lax.ppermute(packed[0], "space", backward)

    edges = jnp.arange(slots, dtype=jnp.int32)
    live = edges < edge_count[0]
    owner = jnp.where(live, edge_target, points)
    ahead = jnp.pad(owner, (DEGREE - 1, 0), constant_values=-1)
    rank = sum(
        (lax.slice_in_dim(ahead, k, k + slots) == owner).astype(jnp.int32)
        for k in range(DEGREE - 1)
    )
    ranked = jnp.where(
        rank[None, :] == jnp.arange(DEGREE, dtype=jnp.int32)[:, None], edge_source[None, :] + 1, 0
    ).astype(jnp.bfloat16)
    owned = (owner[:, None] == jnp.arange(points, dtype=jnp.int32)).astype(jnp.bfloat16)
    found = jnp.einsum("ke,eg->kg", ranked, owned, preferred_element_type=jnp.float32)
    found = found.astype(jnp.int32)
    slot = jnp.where(found > 0, found - 1, table_rows)
    columns = jnp.arange(TABLE + CHUNK, dtype=jnp.int32)
    within = jnp.arange(CHUNK, dtype=jnp.int32)
    by_chunk = slot.reshape(DEGREE, chunks, CHUNK).transpose(1, 0, 2)
    pick = (
        (by_chunk[..., None] == columns) | ((within[:, None] + TABLE) == columns)
    ).astype(jnp.bfloat16).reshape(chunks, DEGREE * CHUNK, TABLE + CHUNK)
    place = (
        slot.reshape(1, DEGREE * points) == jnp.arange(TABLE, dtype=jnp.int32)[:, None]
    ).astype(jnp.bfloat16)
    output_rows = output_weight.T
    output_padded = jnp.pad(output_rows, ((0, TABLE - variables), (0, 0)))
    scale = variable_weight[:, None]

    source_rows = jnp.concatenate([hidden, from_left, from_right], axis=1)

    chunk_rows = pl.BlockSpec((CHUNK, width), lambda c: (c, 0))
    member_rows = pl.BlockSpec((members, CHUNK, width), lambda c: (0, c, 0))
    pick_block = pl.BlockSpec((1, DEGREE * CHUNK, TABLE + CHUNK), lambda c: (c, 0, 0))
    by_variable = pl.BlockSpec((variables, CHUNK), lambda c: (0, c))
    tiled_rows = -(-variables // 8) * 8
    own_block = pl.BlockSpec((members, tiled_rows, CHUNK), lambda c: (0, 0, c))
    per_point = jax.ShapeDtypeStruct((members, points, width), jnp.bfloat16)
    pred, summed, node_out, node_slope, comb = pl.pallas_call(
        forward_kernel_with_table,
        grid=(chunks,),
        in_specs=[
            whole(source_rows), whole(project_weight), pick_block, chunk_rows,
            whole(node_weight), whole(output_rows), by_variable,
        ],
        out_specs=[
            own_block, member_rows, member_rows, member_rows,
            pl.BlockSpec((members, TABLE, width), lambda c: (0, 0, 0)),
        ],
        out_shape=[
            jax.ShapeDtypeStruct((members, tiled_rows, points), jnp.float32), per_point, per_point,
            per_point, jax.ShapeDtypeStruct((members, TABLE, width), jnp.bfloat16),
        ],
        scratch_shapes=[
            pltpu.VMEM((members, TABLE + CHUNK, width), jnp.bfloat16),
            pltpu.VMEM((DEGREE * CHUNK, TILE), jnp.float32),
            pltpu.VMEM((DEGREE * CHUNK, TILE), jnp.float32),
        ],
        compiler_params=params(),
        name="forward",
    )(source_rows, project_weight, pick, grid_state, node_weight, output_rows, prior_state)

    def swap(value, flip):
        return lax.ppermute(value, "member", [(i, i ^ flip) for i in range(lax.axis_size("member"))])

    chip_pred = swap(pred, 2)
    core_pred = swap(pred, 1)

    edge_slope = pl.pallas_call(
        edge_slope_kernel,
        grid=(chunks,),
        in_specs=[whole(comb), pick_block, chunk_rows],
        out_specs=pl.BlockSpec((members, DEGREE, CHUNK, width), lambda c: (0, 0, c, 0)),
        out_shape=jax.ShapeDtypeStruct((members, DEGREE, points, width), jnp.bfloat16),
        scratch_shapes=[
            pltpu.VMEM((members, TABLE + CHUNK, width), jnp.bfloat16),
            pltpu.VMEM((DEGREE * CHUNK, TILE), jnp.float32),
            pltpu.VMEM((DEGREE * CHUNK, TILE), jnp.float32),
        ],
        compiler_params=params(),
        cost_estimate=cost(members * DEGREE * points * width, 2 * TABLE, 20),
        name="edge_slopes",
    )(comb, pick, grid_state)
    chip_pred, core_pred, edge_slope = lax.optimization_barrier((chip_pred, core_pred, edge_slope))
    far_pred = swap(chip_pred, 1)
    source_columns = source_rows.reshape(members * table_rows, width).T
    far_pred, source_columns, place, output_padded = lax.optimization_barrier(
        (far_pred, source_columns, place, output_padded)
    )
    grad_rows, node_pre_grad, loss_row = pl.pallas_call(
        loss_kernel,
        grid=(chunks,),
        in_specs=[
            pl.BlockSpec(memory_space=pltpu.SMEM),
            own_block, own_block, own_block, own_block, by_variable,
            pl.BlockSpec((1, CHUNK), lambda c: (0, c)),
            whole(scale), member_rows, whole(output_padded),
        ],
        out_specs=[
            pl.BlockSpec((members, CHUNK, TABLE), lambda c: (0, c, 0)), member_rows,
            pl.BlockSpec((1, CHUNK), lambda c: (0, 0)),
        ],
        out_shape=[
            jax.ShapeDtypeStruct((members, points, TABLE), jnp.bfloat16), per_point,
            jax.ShapeDtypeStruct((1, CHUNK), jnp.float32),
        ],
        scratch_shapes=[
            pltpu.VMEM((members, TABLE, CHUNK), jnp.float32), pltpu.VMEM((1, CHUNK), jnp.float32),
        ],
        compiler_params=params(),
        name="loss",
    )(core[None], pred, core_pred, chip_pred, far_pred, target, area_weight[None, :], scale, node_slope, output_padded)

    own_rows = width // space // 2
    smem = pl.BlockSpec(memory_space=pltpu.SMEM)

    def add_partner(mine, other):
        return (mine.astype(jnp.float32) + swap(other, 1).astype(jnp.float32)).astype(jnp.bfloat16)

    def across_space(half):
        return lax.all_to_all(half, "space", 0, 0, tiled=True)

    def sum_members(part):
        mine = part + swap(part, 2)
        other = swap(part, 1) + swap(part, 3)
        return jnp.where(
            core == 0,
            jnp.concatenate([mine, other], axis=0),
            jnp.concatenate([other, mine], axis=0),
        )

    terms_block = pl.BlockSpec(
        (TILE // (2 * own_rows), own_rows, width + TABLE), lambda c: (c, 0, 0)
    )
    terms_shape = jax.ShapeDtypeStruct((space, own_rows, width + TABLE), jnp.bfloat16)
    some_columns = pl.BlockSpec((members, points, TILE), lambda c: (0, 0, c))
    node_mine, node_other = pl.pallas_call(
        node_term_kernel,
        grid=(width // TILE,),
        in_specs=[
            smem, some_columns, some_columns, whole(node_pre_grad), whole(grad_rows),
            whole(loss_row),
        ],
        out_specs=[terms_block, terms_block],
        out_shape=[terms_shape, terms_shape],
        compiler_params=params(),
        cost_estimate=cost(width * width, members * points, 1),
        name="node_terms",
    )(core[None], summed, node_out, node_pre_grad, grad_rows, loss_row)

    halves = 2
    tiles = width // TILE // halves

    def table_half(first, pre_grad):
        columns = pl.BlockSpec((space, own_rows, TILE), lambda c: (0, 0, c))
        shape = jax.ShapeDtypeStruct((space, own_rows, tiles * TILE), jnp.bfloat16)
        return pl.pallas_call(
            table_kernel,
            grid=(tiles,),
            in_specs=[
                smem,
                whole(pre_grad),
                pl.BlockSpec((TILE, width), lambda c: (first + c, 0)),
                pl.BlockSpec((members, DEGREE, points, TILE), lambda c: (0, 0, 0, first + c)),
                whole(place),
                whole(source_columns),
            ],
            out_specs=[
                pl.BlockSpec((members, table_rows, TILE), lambda c: (0, 0, c)), columns, columns,
            ],
            out_shape=[
                jax.ShapeDtypeStruct((members, table_rows, tiles * TILE), jnp.float32),
                shape, shape,
            ],
            compiler_params=params(),
            cost_estimate=cost(members * points * width // halves, 4 * width, 8),
            name="table",
        )(core[None], pre_grad, node_weight, edge_slope, place, source_columns)

    first_grad, first_mine, first_other = table_half(0, node_pre_grad)
    node_half = add_partner(node_mine, node_other)
    second_input, node_half, first_mine = lax.optimization_barrier(
        (node_pre_grad, node_half, first_mine)
    )
    node_moved = across_space(node_half)
    first_half = add_partner(first_mine, first_other)
    second_grad, second_mine, second_other = table_half(tiles, second_input)
    second_half = add_partner(second_mine, second_other)

    table_grad = jnp.concatenate([first_grad, second_grad], axis=2)
    left_back = lax.ppermute(
        table_grad[:, own_nodes : own_nodes + send_rows].astype(jnp.bfloat16), "space", backward
    )
    right_back = lax.ppermute(
        table_grad[:, own_nodes + send_rows :].astype(jnp.bfloat16), "space", forward
    )
    project_half = jnp.concatenate([first_half, second_half], axis=2)
    project_half, node_moved, left_back, right_back = lax.optimization_barrier(
        (project_half, node_moved, left_back, right_back)
    )
    node_part, project_part = (
        jnp.sum(moved.astype(jnp.float32), axis=0)
        for moved in (node_moved, across_space(project_half))
    )
    sums = sum_members(jnp.concatenate([project_part, node_part], axis=1))
    projected_grad = (
        table_grad[:, :own_nodes]
        + jnp.einsum(
            "sn,msh->mnh", chosen[1], left_back, preferred_element_type=jnp.float32
        )
        + jnp.einsum(
            "sn,msh->mnh", chosen[0], right_back, preferred_element_type=jnp.float32
        )
    ).astype(jnp.bfloat16)
    grad_hidden = jnp.einsum(
        "mnk,hk->mnh", projected_grad, project_weight, preferred_element_type=jnp.float32
    ).astype(jnp.bfloat16)
    output_at = 2 * width
    loss_at = output_at + variables
    return (
        grad_hidden,
        sums[:, :width] / total_points,
        sums[:, width:output_at] / total_points,
        sums[:, output_at:loss_at] / total_points,
        jnp.sum(sums[0, loss_at:]) / (total_points * variables),
    )


def forward_kernel_with_table(*refs):
    table_ref, comb_ref = refs[11:13]
    forward_kernel(*refs[:11], *refs[12:])

    @pl.when(pl.program_id(0) == 0)
    def _():
        table_ref[...] = comb_ref[:, :TABLE]


def solution(mesh):
    placed = (
        P("member", "space", None),
        P("space", None),
        P(),
        P(),
        P(),
        P(None, "space"),
        P(None, "space"),
        P("space"),
        P(),
        P("space"),
        P("space"),
        P("space"),
        P("space", None),
    )
    return jax.shard_map(
        shards,
        mesh=mesh,
        in_specs=placed,
        out_specs=(
            P("member", "space", None),
            P("space", None),
            P("space", None),
            P("space", None),
            P(),
        ),
        check_vma=False,
    )
```

```python
import functools

import jax
import jax.numpy as jnp
from jax import lax
from jax.experimental import pallas as pl
from jax.experimental.pallas import tpu as pltpu
from jax.sharding import PartitionSpec as P

SQRT_TWO_PI = 0.7978845608028654
CUBIC = 0.044715
ALPHA = 0.95
SOFT_EDGE = 0.05
DEGREE = 4
TABLE = 128
EMPTY = -64.0
CHUNK = 128
TILE = 256
PART = 32
PIECES = 1
VMEM_LIMIT = 56 * 1024 * 1024
LANES = 128


def tanh_of(u):
    s = u * u
    return s, jnp.tanh(u * (SQRT_TWO_PI + (SQRT_TWO_PI * CUBIC) * s))


def gelu_twice(u):
    _, t = tanh_of(u)
    return u + u * t


def slope_twice(u, s=None, t=None):
    if t is None:
        s, t = tanh_of(u)
    q = u * (SQRT_TWO_PI + (3.0 * SQRT_TWO_PI * CUBIC) * s)
    return (1.0 + t) * (1.0 + (1.0 - t) * q)


def dot(left, right):
    return lax.dot_general(
        left, right, (((1,), (0,)), ((), ())), preferred_element_type=jnp.float32
    )


def dot_nt(left, right):
    return lax.dot_general(
        left, right, (((1,), (1,)), ((), ())), preferred_element_type=jnp.float32
    )


def blocks(rows, piece):
    share = rows // PIECES
    first = piece * share
    return [(r, c) for r in range(first, first + share, PART) for c in range(0, TILE, LANES)]


def staged(tiles, work_ref, matmul, finish):
    for i in range(len(tiles) + 1):
        for piece in range(PIECES):
            if i < len(tiles):
                result = matmul(*tiles[i], piece)
                rows = result.shape[0]
                work_ref[i % 2][piece * rows : (piece + 1) * rows] = result
            if i:
                finish(work_ref[(i - 1) % 2], *tiles[i - 1], piece)


def edge_stage(pick_ref, comb_ref, work_ref, finish):
    members, _, width = comb_ref.shape
    tiles = [(m, h) for m in range(members) for h in range(0, width, TILE)]
    rows = pick_ref.shape[1] // PIECES

    def matmul(m, h, piece):
        return dot(pick_ref[0, piece * rows : (piece + 1) * rows], comb_ref[m, :, h : h + TILE])

    staged(tiles, work_ref, matmul, finish)


def node_stage(summed_ref, node_ref, work_ref, finish):
    members, rows, width = summed_ref.shape
    share = members // PIECES

    def matmul(h, piece):
        some = summed_ref[piece * share : (piece + 1) * share].reshape(share * rows, width)
        return dot(some, node_ref[:, h : h + TILE])

    def finish_members(buffer, h, piece):
        for m in range(piece * share, (piece + 1) * share):
            finish(buffer, m * rows, m, h)

    staged([(h,) for h in range(0, width, TILE)], work_ref, matmul, finish_members)


def forward_kernel(
    own_ref, left_ref, right_ref, project_ref, pick_ref, grid_ref, node_ref, output_ref, prior_ref,
    pred_ref, summed_ref, out_ref, slope_ref, table_ref, columns_ref,
    comb_ref, rows_ref, *work_ref,
):
    members, own_nodes, width = own_ref.shape
    table_rows = own_nodes + left_ref.shape[1] + right_ref.shape[1]

    @pl.when(pl.program_id(0) == 0)
    def _():
        for m in range(members):
            first = m * table_rows
            for ref in (own_ref, left_ref, right_ref):
                rows_ref[first : first + ref.shape[1]] = ref[m]
                first += ref.shape[1]
        projected = dot(rows_ref[...], project_ref[...]).astype(jnp.bfloat16)
        for m in range(members):
            comb_ref[m, :table_rows] = projected[m * table_rows : (m + 1) * table_rows]
            comb_ref[m, table_rows:TABLE] = jnp.full(
                (TABLE - table_rows, width), EMPTY, jnp.bfloat16
            )
        table_ref[...] = comb_ref[:, :TABLE]
        columns_ref[...] = rows_ref[...].astype(jnp.float32).T.astype(jnp.bfloat16)

    for m in range(members):
        comb_ref[m, TABLE:] = grid_ref[...]

    def sum_edges(buffer, m, h, piece):
        for r, c in blocks(CHUNK, piece):
            twice = sum(
                gelu_twice(buffer[k * CHUNK + r : k * CHUNK + r + PART, c : c + LANES])
                for k in range(DEGREE)
            )
            summed_ref[m, r : r + PART, h + c : h + c + LANES] = (0.5 * twice).astype(jnp.bfloat16)

    def node_values(buffer, first, m, h):
        for r in range(0, CHUNK, PART):
            for c in range(0, TILE, LANES):
                u = buffer[first + r : first + r + PART, c : c + LANES]
                s, t = tanh_of(u)
                place = (m, slice(r, r + PART), slice(h + c, h + c + LANES))
                out_ref[place] = (0.5 * (u + u * t)).astype(jnp.bfloat16)
                slope_ref[place] = (0.5 * slope_twice(u, s, t)).astype(jnp.bfloat16)

    edge_stage(pick_ref, comb_ref, work_ref, sum_edges)
    node_stage(summed_ref, node_ref, work_ref, node_values)
    for m in range(members):
        pred_ref[m] = jnp.zeros(pred_ref.shape[1:], jnp.float32)
        pred_ref[m, : prior_ref.shape[0]] = prior_ref[...] + dot_nt(output_ref[...], out_ref[m])


def edge_slope_kernel(comb_ref, pick_ref, grid_ref, edge_ref, both_ref, *work_ref):
    for m in range(comb_ref.shape[0]):
        both_ref[m, :TABLE] = comb_ref[m]
        both_ref[m, TABLE:] = grid_ref[...]

    def edge_slopes(buffer, m, h, piece):
        for k in range(DEGREE):
            for r, c in blocks(CHUNK, piece):
                value = 0.5 * slope_twice(
                    buffer[k * CHUNK + r : k * CHUNK + r + PART, c : c + LANES]
                )
                edge_ref[m, k, r : r + PART, h + c : h + c + LANES] = value.astype(jnp.bfloat16)

    edge_stage(pick_ref, both_ref, work_ref, edge_slopes)


def loss_kernel(
    core_index_ref, own_ref, core_ref, chip_ref, far_ref, truth_ref, weight_ref, slope_ref, output_ref,
    grad_ref, pre_ref, loss_ref, tall_ref, sum_ref,
):
    members = own_ref.shape[0]
    variables = truth_ref.shape[0]
    width = output_ref.shape[1]
    everyone = 4 * members
    fairness = 1.0 - (1.0 - ALPHA) / everyone
    edge = SOFT_EDGE * SOFT_EDGE

    @pl.when(pl.program_id(0) == 0)
    def _():
        sum_ref[...] = jnp.zeros_like(sum_ref)
        tall_ref[...] = jnp.zeros_like(tall_ref)

    everyones = [ref.at[k] for ref in (own_ref, core_ref, chip_ref, far_ref) for k in range(members)]
    total = jnp.zeros((1, CHUNK), jnp.float32)
    for first in range(0, variables, PART):
        rows = slice(first, min(first + PART, variables))
        weight = weight_ref[rows]
        truth = truth_ref[rows]
        terms = jnp.zeros_like(truth)
        for j in range(members):
            own = own_ref[j, rows]
            pair_abs = jnp.full_like(truth, -everyone * SOFT_EDGE)
            pair_sign = jnp.zeros_like(truth)
            for other in everyones:
                d = own - other[rows]
                square = d * d + edge
                r = lax.rsqrt(square)
                pair_abs = pair_abs + square * r
                pair_sign = pair_sign + d * r
            d = own - truth
            square = d * d + edge
            r = lax.rsqrt(square)
            terms = terms + (
                (square * r - SOFT_EDGE) / everyone
                - fairness / (2.0 * everyone * (everyone - 1)) * pair_abs
            )
            tall_ref[j, rows] = weight * (d * r - fairness / (everyone - 1) * pair_sign)
        total = total + jnp.sum(weight * terms, axis=0, keepdims=True)
    sum_ref[...] += total
    grads = []
    for j in range(members):
        tall = tall_ref[j].T.astype(jnp.bfloat16)
        grad_ref[j] = tall
        grads.append(tall)

    @pl.when(pl.program_id(0) == pl.num_programs(0) - 1)
    def _():
        rest = jnp.sum(sum_ref[...], axis=1, keepdims=True)
        lane = lax.broadcasted_iota(jnp.int32, (1, CHUNK), 1)
        row = jnp.zeros((1, CHUNK), jnp.float32)
        for part in range(3):
            piece = rest.astype(jnp.bfloat16).astype(jnp.float32)
            row = jnp.where(lane == variables + 3 * core_index_ref[0] + part, piece, row)
            rest = rest - piece
        loss_ref[...] = row

    stacked = jnp.concatenate(grads, axis=0)
    for h in range(0, width, TILE):
        node_grad = dot(stacked, output_ref[:, h : h + TILE]).reshape(members, CHUNK, TILE)
        slope = slope_ref[:, :, h : h + TILE].astype(jnp.float32)
        pre_ref[:, :, h : h + TILE] = (node_grad * slope).astype(jnp.bfloat16)


def dot_tn(left, right):
    return lax.dot_general(
        left, right, (((0,), (0,)), ((), ())), preferred_element_type=jnp.float32
    )


def split_rows(value, core, mine_ref, other_ref, columns):
    rows = mine_ref.shape[1]
    pairs = value.reshape(value.shape[0] // (2 * rows), 2, rows, value.shape[1])
    first, second = pairs[:, 0], pairs[:, 1]
    mine_ref[:, :, columns] = jnp.where(core == 0, first, second).astype(jnp.bfloat16)
    other_ref[:, :, columns] = jnp.where(core == 0, second, first).astype(jnp.bfloat16)


def node_term_kernel(
    core_ref, summed_ref, out_ref, pre_ref, grad_ref, loss_ref, mine_ref, other_ref,
):
    members, _, width = pre_ref.shape
    core = core_ref[0]
    node = sum(dot_tn(summed_ref[m], pre_ref[m]) for m in range(members))
    split_rows(node, core, mine_ref, other_ref, slice(0, width))
    output = sum(dot_tn(out_ref[m], grad_ref[m]) for m in range(members)) + loss_ref[...]
    split_rows(output, core, mine_ref, other_ref, slice(width, width + TABLE))


def table_kernel(
    core_ref, pre_ref, node_ref, slope_ref, slot_ref, rows_ref, grad_ref, mine_ref, other_ref,
    place_ref,
):
    members, points, _ = pre_ref.shape
    table_rows = grad_ref.shape[1]

    @pl.when(pl.program_id(0) == 0)
    def _():
        for k in range(DEGREE):
            columns = slice(k * points, (k + 1) * points)
            row = lax.broadcasted_iota(jnp.int32, (TABLE, points), 0)
            picked = jnp.where(slot_ref[:, columns] == row, 1.0, 0.0)
            place_ref[:, columns] = picked.astype(jnp.bfloat16)

    cast = []
    for m in range(members):
        summed_grad = dot_nt(pre_ref[m], node_ref[...]).astype(jnp.bfloat16)
        table = sum(
            dot(place_ref[:, k * points : (k + 1) * points], summed_grad * slope_ref[m, k])
            for k in range(DEGREE)
        )[:table_rows]
        grad_ref[m] = table
        cast.append(table.astype(jnp.bfloat16))
    term = dot(rows_ref[...], jnp.concatenate(cast, axis=0))
    split_rows(term, core_ref[0], mine_ref, other_ref, slice(0, term.shape[1]))


def params():
    return pltpu.CompilerParams(
        dimension_semantics=("arbitrary",), vmem_limit_bytes=VMEM_LIMIT
    )


def cost(elements, depth, work):
    return pl.CostEstimate(
        flops=elements * (2 * depth + work), bytes_accessed=2 * elements, transcendentals=elements
    )


def whole(array):
    return pl.BlockSpec(array.shape, lambda c: (0,) * array.ndim)


def shards(
    hidden,
    grid_state,
    project_weight,
    node_weight,
    output_weight,
    prior_state,
    target,
    area_weight,
    variable_weight,
    edge_source,
    edge_target,
    edge_count,
    send_index,
):
    members, own_nodes, width = hidden.shape
    points = grid_state.shape[0]
    send_rows = send_index.shape[1]
    variables = output_weight.shape[1]
    slots = edge_source.shape[0]
    core = lax.axis_index("member") % 2
    space = lax.axis_size("space")
    total_points = points * space
    table_rows = own_nodes + 2 * send_rows
    chunks = points // CHUNK

    nodes = jnp.arange(own_nodes, dtype=jnp.int32)
    chosen = (send_index[:, :, None] == nodes).astype(jnp.bfloat16)
    packed = jnp.einsum(
        "dsn,mnh->dmsh", chosen, hidden, preferred_element_type=jnp.float32
    ).astype(jnp.bfloat16)
    forward = [(i, i + 1) for i in range(space - 1)]
    backward = [(i + 1, i) for i in range(space - 1)]
    from_left = lax.ppermute(packed[1], "space", forward)
    from_right = lax.ppermute(packed[0], "space", backward)

    edges = jnp.arange(slots, dtype=jnp.int32)
    live = edges < edge_count[0]
    owner = jnp.where(live, edge_target, points)
    ahead = jnp.pad(owner, (DEGREE - 1, 0), constant_values=-1)
    rank = sum(
        (lax.slice_in_dim(ahead, k, k + slots) == owner).astype(jnp.int32)
        for k in range(DEGREE - 1)
    )
    ranked = jnp.where(
        rank[None, :] == jnp.arange(DEGREE, dtype=jnp.int32)[:, None], edge_source[None, :] + 1, 0
    ).astype(jnp.bfloat16)
    owned = (owner[:, None] == jnp.arange(points, dtype=jnp.int32)).astype(jnp.bfloat16)
    found = jnp.einsum("ke,eg->kg", ranked, owned, preferred_element_type=jnp.float32)
    found = found.astype(jnp.int32)
    slot = jnp.where(found > 0, found - 1, table_rows)
    columns = jnp.arange(TABLE + CHUNK, dtype=jnp.int32)
    within = jnp.arange(CHUNK, dtype=jnp.int32)
    by_chunk = slot.reshape(DEGREE, chunks, CHUNK).transpose(1, 0, 2)
    pick = (
        (by_chunk[..., None] == columns) | ((within[:, None] + TABLE) == columns)
    ).astype(jnp.bfloat16).reshape(chunks, DEGREE * CHUNK, TABLE + CHUNK)
    slot_row = slot.reshape(1, DEGREE * points)
    output_rows = output_weight.T
    output_padded = jnp.pad(output_rows, ((0, TABLE - variables), (0, 0)))
    weight_map = variable_weight[:, None] * area_weight[None, :]

    chunk_rows = pl.BlockSpec((CHUNK, width), lambda c: (c, 0))
    member_rows = pl.BlockSpec((members, CHUNK, width), lambda c: (0, c, 0))
    pick_block = pl.BlockSpec((1, DEGREE * CHUNK, TABLE + CHUNK), lambda c: (c, 0, 0))
    by_variable = pl.BlockSpec((variables, CHUNK), lambda c: (0, c))
    tiled_rows = -(-variables // 8) * 8
    own_block = pl.BlockSpec((members, tiled_rows, CHUNK), lambda c: (0, 0, c))
    per_point = jax.ShapeDtypeStruct((members, points, width), jnp.bfloat16)
    pred, summed, node_out, node_slope, comb, source_columns = pl.pallas_call(
        forward_kernel,
        grid=(chunks,),
        in_specs=[
            whole(hidden), whole(from_left), whole(from_right), whole(project_weight), pick_block,
            chunk_rows,
            whole(node_weight), whole(output_rows), by_variable,
        ],
        out_specs=[
            own_block, member_rows, member_rows, member_rows,
            pl.BlockSpec((members, TABLE, width), lambda c: (0, 0, 0)),
            pl.BlockSpec((width, members * table_rows), lambda c: (0, 0)),
        ],
        out_shape=[
            jax.ShapeDtypeStruct((members, tiled_rows, points), jnp.float32), per_point, per_point,
            per_point, jax.ShapeDtypeStruct((members, TABLE, width), jnp.bfloat16),
            jax.ShapeDtypeStruct((width, members * table_rows), jnp.bfloat16),
        ],
        scratch_shapes=[
            pltpu.VMEM((members, TABLE + CHUNK, width), jnp.bfloat16),
            pltpu.VMEM((members * table_rows, width), jnp.bfloat16),
            pltpu.VMEM((DEGREE * CHUNK, TILE), jnp.float32),
            pltpu.VMEM((DEGREE * CHUNK, TILE), jnp.float32),
        ],
        compiler_params=params(),
        name="forward",
    )(hidden, from_left, from_right, project_weight, pick, grid_state, node_weight, output_rows, prior_state)

    def swap(value, flip):
        return lax.ppermute(value, "member", [(i, i ^ flip) for i in range(lax.axis_size("member"))])

    chip_pred = swap(pred, 2)
    core_pred = swap(pred, 1)

    edge_slope = pl.pallas_call(
        edge_slope_kernel,
        grid=(chunks,),
        in_specs=[whole(comb), pick_block, chunk_rows],
        out_specs=pl.BlockSpec((members, DEGREE, CHUNK, width), lambda c: (0, 0, c, 0)),
        out_shape=jax.ShapeDtypeStruct((members, DEGREE, points, width), jnp.bfloat16),
        scratch_shapes=[
            pltpu.VMEM((members, TABLE + CHUNK, width), jnp.bfloat16),
            pltpu.VMEM((DEGREE * CHUNK, TILE), jnp.float32),
            pltpu.VMEM((DEGREE * CHUNK, TILE), jnp.float32),
        ],
        compiler_params=params(),
        cost_estimate=cost(members * DEGREE * points * width, 2 * TABLE, 20),
        name="edge_slopes",
    )(comb, pick, grid_state)
    chip_pred, core_pred, edge_slope = lax.optimization_barrier((chip_pred, core_pred, edge_slope))
    far_pred = swap(chip_pred, 1)
    far_pred, weight_map, output_padded = lax.optimization_barrier(
        (far_pred, weight_map, output_padded)
    )
    grad_rows, node_pre_grad, loss_row = pl.pallas_call(
        loss_kernel,
        grid=(chunks,),
        in_specs=[
            pl.BlockSpec(memory_space=pltpu.SMEM),
            own_block, own_block, own_block, own_block, by_variable, by_variable, member_rows, whole(output_padded),
        ],
        out_specs=[
            pl.BlockSpec((members, CHUNK, TABLE), lambda c: (0, c, 0)), member_rows,
            pl.BlockSpec((1, CHUNK), lambda c: (0, 0)),
        ],
        out_shape=[
            jax.ShapeDtypeStruct((members, points, TABLE), jnp.bfloat16), per_point,
            jax.ShapeDtypeStruct((1, CHUNK), jnp.float32),
        ],
        scratch_shapes=[
            pltpu.VMEM((members, TABLE, CHUNK), jnp.float32), pltpu.VMEM((1, CHUNK), jnp.float32),
        ],
        compiler_params=params(),
        name="loss",
    )(core[None], pred, core_pred, chip_pred, far_pred, target, weight_map, node_slope, output_padded)

    own_rows = width // space // 2
    smem = pl.BlockSpec(memory_space=pltpu.SMEM)

    def add_partner(mine, other):
        return (mine.astype(jnp.float32) + swap(other, 1).astype(jnp.float32)).astype(jnp.bfloat16)

    def across_space(half):
        return lax.all_to_all(half, "space", 0, 0, tiled=True)

    def sum_members(part):
        mine = part + swap(part, 2)
        other = swap(part, 1) + swap(part, 3)
        return jnp.where(
            core == 0,
            jnp.concatenate([mine, other], axis=0),
            jnp.concatenate([other, mine], axis=0),
        )

    terms_block = pl.BlockSpec(
        (TILE // (2 * own_rows), own_rows, width + TABLE), lambda c: (c, 0, 0)
    )
    terms_shape = jax.ShapeDtypeStruct((space, own_rows, width + TABLE), jnp.bfloat16)
    some_columns = pl.BlockSpec((members, points, TILE), lambda c: (0, 0, c))
    node_mine, node_other = pl.pallas_call(
        node_term_kernel,
        grid=(width // TILE,),
        in_specs=[
            smem, some_columns, some_columns, whole(node_pre_grad), whole(grad_rows),
            whole(loss_row),
        ],
        out_specs=[terms_block, terms_block],
        out_shape=[terms_shape, terms_shape],
        compiler_params=params(),
        cost_estimate=cost(width * width, members * points, 1),
        name="node_terms",
    )(core[None], summed, node_out, node_pre_grad, grad_rows, loss_row)

    node_half = add_partner(node_mine, node_other)
    pre_grad, node_half = lax.optimization_barrier((node_pre_grad, node_half))
    node_moved = across_space(node_half)
    columns = pl.BlockSpec((space, own_rows, TILE), lambda c: (0, 0, c))
    columns_shape = jax.ShapeDtypeStruct((space, own_rows, width), jnp.bfloat16)
    table_grad, project_mine, project_other = pl.pallas_call(
        table_kernel,
        grid=(width // TILE,),
        in_specs=[
            smem,
            whole(pre_grad),
            pl.BlockSpec((TILE, width), lambda c: (c, 0)),
            pl.BlockSpec((members, DEGREE, points, TILE), lambda c: (0, 0, 0, c)),
            whole(slot_row),
            whole(source_columns),
        ],
        out_specs=[
            pl.BlockSpec((members, table_rows, TILE), lambda c: (0, 0, c)), columns, columns,
        ],
        out_shape=[
            jax.ShapeDtypeStruct((members, table_rows, width), jnp.float32),
            columns_shape, columns_shape,
        ],
        scratch_shapes=[pltpu.VMEM((TABLE, DEGREE * points), jnp.bfloat16)],
        compiler_params=params(),
        cost_estimate=cost(members * points * width, 4 * width, 8),
        name="table",
    )(core[None], pre_grad, node_weight, edge_slope, slot_row, source_columns)
    project_half = add_partner(project_mine, project_other)

    left_back = lax.ppermute(
        table_grad[:, own_nodes : own_nodes + send_rows].astype(jnp.bfloat16), "space", backward
    )
    right_back = lax.ppermute(
        table_grad[:, own_nodes + send_rows :].astype(jnp.bfloat16), "space", forward
    )
    project_half, node_moved, left_back, right_back = lax.optimization_barrier(
        (project_half, node_moved, left_back, right_back)
    )
    project_moved = across_space(project_half)
    projected_grad = (
        table_grad[:, :own_nodes]
        + jnp.einsum(
            "sn,msh->mnh", chosen[1], left_back, preferred_element_type=jnp.float32
        )
        + jnp.einsum(
            "sn,msh->mnh", chosen[0], right_back, preferred_element_type=jnp.float32
        )
    ).astype(jnp.bfloat16)
    grad_hidden = jnp.einsum(
        "mnk,hk->mnh", projected_grad, project_weight, preferred_element_type=jnp.float32
    ).astype(jnp.bfloat16)
    project_moved, grad_hidden = lax.optimization_barrier((project_moved, grad_hidden))
    project_part, node_part = (
        jnp.sum(moved.astype(jnp.float32), axis=0) for moved in (project_moved, node_moved)
    )
    sums = sum_members(jnp.concatenate([project_part, node_part], axis=1))
    output_at = 2 * width
    loss_at = output_at + variables
    return (
        grad_hidden,
        sums[:, :width] / total_points,
        sums[:, width:output_at] / total_points,
        sums[:, output_at:loss_at] / total_points,
        jnp.sum(sums[0, loss_at:]) / (total_points * variables),
    )


def solution(mesh):
    placed = (
        P("member", "space", None),
        P("space", None),
        P(),
        P(),
        P(),
        P(None, "space"),
        P(None, "space"),
        P("space"),
        P(),
        P("space"),
        P("space"),
        P("space"),
        P("space", None),
    )
    return jax.shard_map(
        shards,
        mesh=mesh,
        in_specs=placed,
        out_specs=(
            P("member", "space", None),
            P("space", None),
            P("space", None),
            P("space", None),
            P(),
        ),
        check_vma=False,
    )
```

```python
import functools

import jax
import jax.numpy as jnp
from jax import lax
from jax.experimental import pallas as pl
from jax.experimental.pallas import tpu as pltpu
from jax.sharding import PartitionSpec as P

SQRT_TWO_PI = 0.7978845608028654
CUBIC = 0.044715
ALPHA = 0.95
SOFT_EDGE = 0.05
DEGREE = 4
TABLE = 128
EMPTY = -64.0
CHUNK = 128
TILE = 256
PART = 32
PIECES = 1
VMEM_LIMIT = 56 * 1024 * 1024
LANES = 128


def tanh_of(u):
    s = u * u
    return s, jnp.tanh(u * (SQRT_TWO_PI + (SQRT_TWO_PI * CUBIC) * s))


def gelu_twice(u):
    _, t = tanh_of(u)
    return u + u * t


def slope_twice(u, s=None, t=None):
    if t is None:
        s, t = tanh_of(u)
    q = u * (SQRT_TWO_PI + (3.0 * SQRT_TWO_PI * CUBIC) * s)
    return (1.0 + t) * (1.0 + (1.0 - t) * q)


def dot(left, right):
    return lax.dot_general(
        left, right, (((1,), (0,)), ((), ())), preferred_element_type=jnp.float32
    )


def dot_nt(left, right):
    return lax.dot_general(
        left, right, (((1,), (1,)), ((), ())), preferred_element_type=jnp.float32
    )


def blocks(rows, piece):
    share = rows // PIECES
    first = piece * share
    return [(r, c) for r in range(first, first + share, PART) for c in range(0, TILE, LANES)]


def staged(tiles, work_ref, matmul, finish):
    for i in range(len(tiles) + 1):
        for piece in range(PIECES):
            if i < len(tiles):
                result = matmul(*tiles[i], piece)
                rows = result.shape[0]
                work_ref[i % 2][piece * rows : (piece + 1) * rows] = result
            if i:
                finish(work_ref[(i - 1) % 2], *tiles[i - 1], piece)


def edge_stage(pick_ref, comb_ref, work_ref, finish):
    members, _, width = comb_ref.shape
    tiles = [(m, h) for m in range(members) for h in range(0, width, TILE)]
    rows = pick_ref.shape[1] // PIECES

    def matmul(m, h, piece):
        return dot(pick_ref[0, piece * rows : (piece + 1) * rows], comb_ref[m, :, h : h + TILE])

    staged(tiles, work_ref, matmul, finish)


def node_stage(summed_ref, node_ref, work_ref, finish):
    members, rows, width = summed_ref.shape
    share = members // PIECES

    def matmul(h, piece):
        some = summed_ref[piece * share : (piece + 1) * share].reshape(share * rows, width)
        return dot(some, node_ref[:, h : h + TILE])

    def finish_members(buffer, h, piece):
        for m in range(piece * share, (piece + 1) * share):
            finish(buffer, m * rows, m, h)

    staged([(h,) for h in range(0, width, TILE)], work_ref, matmul, finish_members)


def forward_kernel(
    own_ref, left_ref, right_ref, project_ref, pick_ref, grid_ref, node_ref, output_ref, prior_ref,
    pred_ref, summed_ref, out_ref, slope_ref, table_ref, columns_ref,
    comb_ref, rows_ref, *work_ref,
):
    members, own_nodes, width = own_ref.shape
    table_rows = own_nodes + left_ref.shape[1] + right_ref.shape[1]

    @pl.when(pl.program_id(0) == 0)
    def _():
        for m in range(members):
            first = m * table_rows
            for ref in (own_ref, left_ref, right_ref):
                rows_ref[first : first + ref.shape[1]] = ref[m]
                first += ref.shape[1]
        projected = dot(rows_ref[...], project_ref[...]).astype(jnp.bfloat16)
        for m in range(members):
            comb_ref[m, :table_rows] = projected[m * table_rows : (m + 1) * table_rows]
            comb_ref[m, table_rows:TABLE] = jnp.full(
                (TABLE - table_rows, width), EMPTY, jnp.bfloat16
            )
        table_ref[...] = comb_ref[:, :TABLE]
        columns_ref[...] = rows_ref[...].astype(jnp.float32).T.astype(jnp.bfloat16)

    for m in range(members):
        comb_ref[m, TABLE:] = grid_ref[...]

    def sum_edges(buffer, m, h, piece):
        for r, c in blocks(CHUNK, piece):
            twice = sum(
                gelu_twice(buffer[k * CHUNK + r : k * CHUNK + r + PART, c : c + LANES])
                for k in range(DEGREE)
            )
            summed_ref[m, r : r + PART, h + c : h + c + LANES] = (0.5 * twice).astype(jnp.bfloat16)

    def node_values(buffer, first, m, h):
        for r in range(0, CHUNK, PART):
            for c in range(0, TILE, LANES):
                u = buffer[first + r : first + r + PART, c : c + LANES]
                s, t = tanh_of(u)
                place = (m, slice(r, r + PART), slice(h + c, h + c + LANES))
                out_ref[place] = (0.5 * (u + u * t)).astype(jnp.bfloat16)
                slope_ref[place] = (0.5 * slope_twice(u, s, t)).astype(jnp.bfloat16)

    edge_stage(pick_ref, comb_ref, work_ref, sum_edges)
    node_stage(summed_ref, node_ref, work_ref, node_values)
    for m in range(members):
        pred_ref[m] = jnp.zeros(pred_ref.shape[1:], jnp.float32)
        pred_ref[m, : prior_ref.shape[0]] = prior_ref[...] + dot_nt(output_ref[...], out_ref[m])


def edge_slope_kernel(comb_ref, pick_ref, grid_ref, edge_ref, both_ref, *work_ref):
    for m in range(comb_ref.shape[0]):
        both_ref[m, :TABLE] = comb_ref[m]
        both_ref[m, TABLE:] = grid_ref[...]

    def edge_slopes(buffer, m, h, piece):
        for k in range(DEGREE):
            for r, c in blocks(CHUNK, piece):
                value = 0.5 * slope_twice(
                    buffer[k * CHUNK + r : k * CHUNK + r + PART, c : c + LANES]
                )
                edge_ref[m, k, r : r + PART, h + c : h + c + LANES] = value.astype(jnp.bfloat16)

    edge_stage(pick_ref, both_ref, work_ref, edge_slopes)


def loss_kernel(
    core_index_ref, own_ref, core_ref, chip_ref, far_ref, truth_ref, weight_ref, slope_ref, output_ref,
    grad_ref, pre_ref, loss_ref, tall_ref, sum_ref,
):
    members = own_ref.shape[0]
    variables = truth_ref.shape[0]
    width = output_ref.shape[1]
    everyone = 4 * members
    fairness = 1.0 - (1.0 - ALPHA) / everyone
    edge = SOFT_EDGE * SOFT_EDGE

    @pl.when(pl.program_id(0) == 0)
    def _():
        sum_ref[...] = jnp.zeros_like(sum_ref)
        tall_ref[...] = jnp.zeros_like(tall_ref)

    everyones = [ref.at[k] for ref in (own_ref, core_ref, chip_ref, far_ref) for k in range(members)]
    total = jnp.zeros((1, CHUNK), jnp.float32)
    for first in range(0, variables, PART):
        rows = slice(first, min(first + PART, variables))
        weight = weight_ref[rows]
        truth = truth_ref[rows]
        terms = jnp.zeros_like(truth)
        for j in range(members):
            own = own_ref[j, rows]
            pair_abs = jnp.full_like(truth, -everyone * SOFT_EDGE)
            pair_sign = jnp.zeros_like(truth)
            for other in everyones:
                d = own - other[rows]
                square = d * d + edge
                r = lax.rsqrt(square)
                pair_abs = pair_abs + square * r
                pair_sign = pair_sign + d * r
            d = own - truth
            square = d * d + edge
            r = lax.rsqrt(square)
            terms = terms + (
                (square * r - SOFT_EDGE) / everyone
                - fairness / (2.0 * everyone * (everyone - 1)) * pair_abs
            )
            tall_ref[j, rows] = weight * (d * r - fairness / (everyone - 1) * pair_sign)
        total = total + jnp.sum(weight * terms, axis=0, keepdims=True)
    sum_ref[...] += total
    grads = []
    for j in range(members):
        tall = tall_ref[j].T.astype(jnp.bfloat16)
        grad_ref[j] = tall
        grads.append(tall)

    @pl.when(pl.program_id(0) == pl.num_programs(0) - 1)
    def _():
        rest = jnp.sum(sum_ref[...], axis=1, keepdims=True)
        lane = lax.broadcasted_iota(jnp.int32, (1, CHUNK), 1)
        row = jnp.zeros((1, CHUNK), jnp.float32)
        for part in range(3):
            piece = rest.astype(jnp.bfloat16).astype(jnp.float32)
            row = jnp.where(lane == variables + 3 * core_index_ref[0] + part, piece, row)
            rest = rest - piece
        loss_ref[...] = row

    stacked = jnp.concatenate(grads, axis=0)
    for h in range(0, width, TILE):
        node_grad = dot(stacked, output_ref[:, h : h + TILE]).reshape(members, CHUNK, TILE)
        slope = slope_ref[:, :, h : h + TILE].astype(jnp.float32)
        pre_ref[:, :, h : h + TILE] = (node_grad * slope).astype(jnp.bfloat16)


def dot_tn(left, right):
    return lax.dot_general(
        left, right, (((0,), (0,)), ((), ())), preferred_element_type=jnp.float32
    )


def split_rows(value, core, mine_ref, other_ref, columns):
    rows = mine_ref.shape[1]
    pairs = value.reshape(value.shape[0] // (2 * rows), 2, rows, value.shape[1])
    first, second = pairs[:, 0], pairs[:, 1]
    mine_ref[:, :, columns] = jnp.where(core == 0, first, second).astype(jnp.bfloat16)
    other_ref[:, :, columns] = jnp.where(core == 0, second, first).astype(jnp.bfloat16)


def node_term_kernel(
    core_ref, summed_ref, out_ref, pre_ref, grad_ref, loss_ref, mine_ref, other_ref,
):
    members, _, width = pre_ref.shape
    core = core_ref[0]
    node = sum(dot_tn(summed_ref[m], pre_ref[m]) for m in range(members))
    split_rows(node, core, mine_ref, other_ref, slice(0, width))
    output = sum(dot_tn(out_ref[m], grad_ref[m]) for m in range(members)) + loss_ref[...]
    split_rows(output, core, mine_ref, other_ref, slice(width, width + TABLE))


def table_kernel(
    core_ref, pre_ref, node_ref, slope_ref, slot_ref, rows_ref, grad_ref, mine_ref, other_ref,
    place_ref,
):
    members, points, _ = pre_ref.shape
    table_rows = grad_ref.shape[1]

    @pl.when(pl.program_id(0) == 0)
    def _():
        for k in range(DEGREE):
            columns = slice(k * points, (k + 1) * points)
            row = lax.broadcasted_iota(jnp.int32, (TABLE, points), 0)
            picked = jnp.where(slot_ref[:, columns] == row, 1.0, 0.0)
            place_ref[:, columns] = picked.astype(jnp.bfloat16)

    cast = []
    for m in range(members):
        summed_grad = dot_nt(pre_ref[m], node_ref[...]).astype(jnp.bfloat16)
        table = sum(
            dot(place_ref[:, k * points : (k + 1) * points], summed_grad * slope_ref[m, k])
            for k in range(DEGREE)
        )[:table_rows]
        grad_ref[m] = table
        cast.append(table.astype(jnp.bfloat16))
    term = dot(rows_ref[...], jnp.concatenate(cast, axis=0))
    split_rows(term, core_ref[0], mine_ref, other_ref, slice(0, term.shape[1]))


def params():
    return pltpu.CompilerParams(
        dimension_semantics=("arbitrary",), vmem_limit_bytes=VMEM_LIMIT
    )


def cost(elements, depth, work):
    return pl.CostEstimate(
        flops=elements * (2 * depth + work), bytes_accessed=2 * elements, transcendentals=elements
    )


def whole(array):
    return pl.BlockSpec(array.shape, lambda c: (0,) * array.ndim)


def shards(
    hidden,
    grid_state,
    project_weight,
    node_weight,
    output_weight,
    prior_state,
    target,
    area_weight,
    variable_weight,
    edge_source,
    edge_target,
    edge_count,
    send_index,
):
    members, own_nodes, width = hidden.shape
    points = grid_state.shape[0]
    send_rows = send_index.shape[1]
    variables = output_weight.shape[1]
    slots = edge_source.shape[0]
    core = lax.axis_index("member") % 2
    space = lax.axis_size("space")
    total_points = points * space
    table_rows = own_nodes + 2 * send_rows
    chunks = points // CHUNK

    nodes = jnp.arange(own_nodes, dtype=jnp.int32)
    chosen = (send_index[:, :, None] == nodes).astype(jnp.bfloat16)
    packed = jnp.einsum(
        "dsn,mnh->dmsh", chosen, hidden, preferred_element_type=jnp.float32
    ).astype(jnp.bfloat16)
    forward = [(i, i + 1) for i in range(space - 1)]
    backward = [(i + 1, i) for i in range(space - 1)]
    from_left = lax.ppermute(packed[1], "space", forward)
    from_right = lax.ppermute(packed[0], "space", backward)

    edges = jnp.arange(slots, dtype=jnp.int32)
    live = edges < edge_count[0]
    owner = jnp.where(live, edge_target, points)
    ahead = jnp.pad(owner, (DEGREE - 1, 0), constant_values=-1)
    rank = sum(
        (lax.slice_in_dim(ahead, k, k + slots) == owner).astype(jnp.int32)
        for k in range(DEGREE - 1)
    )
    ranked = jnp.where(
        rank[None, :] == jnp.arange(DEGREE, dtype=jnp.int32)[:, None], edge_source[None, :] + 1, 0
    ).astype(jnp.bfloat16)
    owned = (owner[:, None] == jnp.arange(points, dtype=jnp.int32)).astype(jnp.bfloat16)
    found = jnp.einsum("ke,eg->kg", ranked, owned, preferred_element_type=jnp.float32)
    found = found.astype(jnp.int32)
    slot = jnp.where(found > 0, found - 1, table_rows)
    columns = jnp.arange(TABLE + CHUNK, dtype=jnp.int32)
    within = jnp.arange(CHUNK, dtype=jnp.int32)
    by_chunk = slot.reshape(DEGREE, chunks, CHUNK).transpose(1, 0, 2)
    pick = (
        (by_chunk[..., None] == columns) | ((within[:, None] + TABLE) == columns)
    ).astype(jnp.bfloat16).reshape(chunks, DEGREE * CHUNK, TABLE + CHUNK)
    slot_row = slot.reshape(1, DEGREE * points)
    output_rows = output_weight.T
    output_padded = jnp.pad(output_rows, ((0, TABLE - variables), (0, 0)))
    weight_map = variable_weight[:, None] * area_weight[None, :]

    chunk_rows = pl.BlockSpec((CHUNK, width), lambda c: (c, 0))
    member_rows = pl.BlockSpec((members, CHUNK, width), lambda c: (0, c, 0))
    pick_block = pl.BlockSpec((1, DEGREE * CHUNK, TABLE + CHUNK), lambda c: (c, 0, 0))
    by_variable = pl.BlockSpec((variables, CHUNK), lambda c: (0, c))
    tiled_rows = -(-variables // 8) * 8
    own_block = pl.BlockSpec((members, tiled_rows, CHUNK), lambda c: (0, 0, c))
    per_point = jax.ShapeDtypeStruct((members, points, width), jnp.bfloat16)
    pred, summed, node_out, node_slope, comb, source_columns = pl.pallas_call(
        forward_kernel,
        grid=(chunks,),
        in_specs=[
            whole(hidden), whole(from_left), whole(from_right), whole(project_weight), pick_block,
            chunk_rows,
            whole(node_weight), whole(output_rows), by_variable,
        ],
        out_specs=[
            own_block, member_rows, member_rows, member_rows,
            pl.BlockSpec((members, TABLE, width), lambda c: (0, 0, 0)),
            pl.BlockSpec((width, members * table_rows), lambda c: (0, 0)),
        ],
        out_shape=[
            jax.ShapeDtypeStruct((members, tiled_rows, points), jnp.float32), per_point, per_point,
            per_point, jax.ShapeDtypeStruct((members, TABLE, width), jnp.bfloat16),
            jax.ShapeDtypeStruct((width, members * table_rows), jnp.bfloat16),
        ],
        scratch_shapes=[
            pltpu.VMEM((members, TABLE + CHUNK, width), jnp.bfloat16),
            pltpu.VMEM((members * table_rows, width), jnp.bfloat16),
            pltpu.VMEM((DEGREE * CHUNK, TILE), jnp.float32),
            pltpu.VMEM((DEGREE * CHUNK, TILE), jnp.float32),
        ],
        compiler_params=params(),
        name="forward",
    )(hidden, from_left, from_right, project_weight, pick, grid_state, node_weight, output_rows, prior_state)

    def swap(value, flip):
        return lax.ppermute(value, "member", [(i, i ^ flip) for i in range(lax.axis_size("member"))])

    chip_pred = swap(pred, 2)
    core_pred = swap(pred, 1)

    edge_slope = pl.pallas_call(
        edge_slope_kernel,
        grid=(chunks,),
        in_specs=[whole(comb), pick_block, chunk_rows],
        out_specs=pl.BlockSpec((members, DEGREE, CHUNK, width), lambda c: (0, 0, c, 0)),
        out_shape=jax.ShapeDtypeStruct((members, DEGREE, points, width), jnp.bfloat16),
        scratch_shapes=[
            pltpu.VMEM((members, TABLE + CHUNK, width), jnp.bfloat16),
            pltpu.VMEM((DEGREE * CHUNK, TILE), jnp.float32),
            pltpu.VMEM((DEGREE * CHUNK, TILE), jnp.float32),
        ],
        compiler_params=params(),
        cost_estimate=cost(members * DEGREE * points * width, 2 * TABLE, 20),
        name="edge_slopes",
    )(comb, pick, grid_state)
    chip_pred, core_pred, edge_slope = lax.optimization_barrier((chip_pred, core_pred, edge_slope))
    far_pred = swap(chip_pred, 1)
    far_pred, weight_map, output_padded = lax.optimization_barrier(
        (far_pred, weight_map, output_padded)
    )
    grad_rows, node_pre_grad, loss_row = pl.pallas_call(
        loss_kernel,
        grid=(chunks,),
        in_specs=[
            pl.BlockSpec(memory_space=pltpu.SMEM),
            own_block, own_block, own_block, own_block, by_variable, by_variable, member_rows, whole(output_padded),
        ],
        out_specs=[
            pl.BlockSpec((members, CHUNK, TABLE), lambda c: (0, c, 0)), member_rows,
            pl.BlockSpec((1, CHUNK), lambda c: (0, 0)),
        ],
        out_shape=[
            jax.ShapeDtypeStruct((members, points, TABLE), jnp.bfloat16), per_point,
            jax.ShapeDtypeStruct((1, CHUNK), jnp.float32),
        ],
        scratch_shapes=[
            pltpu.VMEM((members, TABLE, CHUNK), jnp.float32), pltpu.VMEM((1, CHUNK), jnp.float32),
        ],
        compiler_params=params(),
        name="loss",
    )(core[None], pred, core_pred, chip_pred, far_pred, target, weight_map, node_slope, output_padded)

    own_rows = width // space // 2
    smem = pl.BlockSpec(memory_space=pltpu.SMEM)

    def add_partner(mine, other):
        return (mine.astype(jnp.float32) + swap(other, 1).astype(jnp.float32)).astype(jnp.bfloat16)

    def across_space(half):
        return lax.all_to_all(half, "space", 0, 0, tiled=True)

    def sum_members(part):
        mine = part + swap(part, 2)
        other = swap(part, 1) + swap(part, 3)
        return jnp.where(
            core == 0,
            jnp.concatenate([mine, other], axis=0),
            jnp.concatenate([other, mine], axis=0),
        )

    terms_block = pl.BlockSpec(
        (TILE // (2 * own_rows), own_rows, width + TABLE), lambda c: (c, 0, 0)
    )
    terms_shape = jax.ShapeDtypeStruct((space, own_rows, width + TABLE), jnp.bfloat16)
    some_columns = pl.BlockSpec((members, points, TILE), lambda c: (0, 0, c))
    node_mine, node_other = pl.pallas_call(
        node_term_kernel,
        grid=(width // TILE,),
        in_specs=[
            smem, some_columns, some_columns, whole(node_pre_grad), whole(grad_rows),
            whole(loss_row),
        ],
        out_specs=[terms_block, terms_block],
        out_shape=[terms_shape, terms_shape],
        compiler_params=params(),
        cost_estimate=cost(width * width, members * points, 1),
        name="node_terms",
    )(core[None], summed, node_out, node_pre_grad, grad_rows, loss_row)

    node_half = add_partner(node_mine, node_other)
    pre_grad, node_half = lax.optimization_barrier((node_pre_grad, node_half))
    node_moved = across_space(node_half)
    columns = pl.BlockSpec((space, own_rows, TILE), lambda c: (0, 0, c))
    columns_shape = jax.ShapeDtypeStruct((space, own_rows, width), jnp.bfloat16)
    table_grad, project_mine, project_other = pl.pallas_call(
        table_kernel,
        grid=(width // TILE,),
        in_specs=[
            smem,
            whole(pre_grad),
            pl.BlockSpec((TILE, width), lambda c: (c, 0)),
            pl.BlockSpec((members, DEGREE, points, TILE), lambda c: (0, 0, 0, c)),
            whole(slot_row),
            whole(source_columns),
        ],
        out_specs=[
            pl.BlockSpec((members, table_rows, TILE), lambda c: (0, 0, c)), columns, columns,
        ],
        out_shape=[
            jax.ShapeDtypeStruct((members, table_rows, width), jnp.float32),
            columns_shape, columns_shape,
        ],
        scratch_shapes=[pltpu.VMEM((TABLE, DEGREE * points), jnp.bfloat16)],
        compiler_params=params(),
        cost_estimate=cost(members * points * width, 4 * width, 8),
        name="table",
    )(core[None], pre_grad, node_weight, edge_slope, slot_row, source_columns)
    table_grad, project_mine, project_other, node_moved = lax.optimization_barrier(
        (table_grad, project_mine, project_other, node_moved)
    )
    project_half = add_partner(project_mine, project_other)

    left_back = lax.ppermute(
        table_grad[:, own_nodes : own_nodes + send_rows].astype(jnp.bfloat16), "space", backward
    )
    right_back = lax.ppermute(
        table_grad[:, own_nodes + send_rows :].astype(jnp.bfloat16), "space", forward
    )
    project_half, left_back, right_back = lax.optimization_barrier(
        (project_half, left_back, right_back)
    )
    project_moved = across_space(project_half)
    projected_grad = (
        table_grad[:, :own_nodes]
        + jnp.einsum(
            "sn,msh->mnh", chosen[1], left_back, preferred_element_type=jnp.float32
        )
        + jnp.einsum(
            "sn,msh->mnh", chosen[0], right_back, preferred_element_type=jnp.float32
        )
    ).astype(jnp.bfloat16)
    grad_hidden = jnp.einsum(
        "mnk,hk->mnh", projected_grad, project_weight, preferred_element_type=jnp.float32
    ).astype(jnp.bfloat16)
    project_moved, grad_hidden = lax.optimization_barrier((project_moved, grad_hidden))
    project_part, node_part = (
        jnp.sum(moved.astype(jnp.float32), axis=0) for moved in (project_moved, node_moved)
    )
    sums = sum_members(jnp.concatenate([project_part, node_part], axis=1))
    output_at = 2 * width
    loss_at = output_at + variables
    return (
        grad_hidden,
        sums[:, :width] / total_points,
        sums[:, width:output_at] / total_points,
        sums[:, output_at:loss_at] / total_points,
        jnp.sum(sums[0, loss_at:]) / (total_points * variables),
    )


def solution(mesh):
    placed = (
        P("member", "space", None),
        P("space", None),
        P(),
        P(),
        P(),
        P(None, "space"),
        P(None, "space"),
        P("space"),
        P(),
        P("space"),
        P("space"),
        P("space"),
        P("space", None),
    )
    return jax.shard_map(
        shards,
        mesh=mesh,
        in_specs=placed,
        out_specs=(
            P("member", "space", None),
            P("space", None),
            P("space", None),
            P("space", None),
            P(),
        ),
        check_vma=False,
    )
```

```python
import functools

import jax
import jax.numpy as jnp
from jax import lax
from jax.experimental import pallas as pl
from jax.experimental.pallas import tpu as pltpu
from jax.sharding import PartitionSpec as P

SQRT_TWO_PI = 0.7978845608028654
CUBIC = 0.044715
ALPHA = 0.95
SOFT_EDGE = 0.05
DEGREE = 4
TABLE = 128
EMPTY = -64.0
CHUNK = 128
TILE = 256
PART = 32
PIECES = 1
VMEM_LIMIT = 56 * 1024 * 1024
LANES = 128


def tanh_of(u):
    s = u * u
    return s, jnp.tanh(u * (SQRT_TWO_PI + (SQRT_TWO_PI * CUBIC) * s))


def gelu_twice(u):
    _, t = tanh_of(u)
    return u + u * t


def slope_twice(u, s=None, t=None):
    if t is None:
        s, t = tanh_of(u)
    q = u * (SQRT_TWO_PI + (3.0 * SQRT_TWO_PI * CUBIC) * s)
    return (1.0 + t) * (1.0 + (1.0 - t) * q)


def dot(left, right):
    return lax.dot_general(
        left, right, (((1,), (0,)), ((), ())), preferred_element_type=jnp.float32
    )


def dot_nt(left, right):
    return lax.dot_general(
        left, right, (((1,), (1,)), ((), ())), preferred_element_type=jnp.float32
    )


def blocks(rows, piece):
    share = rows // PIECES
    first = piece * share
    return [(r, c) for r in range(first, first + share, PART) for c in range(0, TILE, LANES)]


def staged(tiles, work_ref, matmul, finish):
    for i in range(len(tiles) + 1):
        for piece in range(PIECES):
            if i < len(tiles):
                result = matmul(*tiles[i], piece)
                rows = result.shape[0]
                work_ref[i % 2][piece * rows : (piece + 1) * rows] = result
            if i:
                finish(work_ref[(i - 1) % 2], *tiles[i - 1], piece)


def edge_stage(pick_ref, comb_ref, work_ref, finish):
    members, _, width = comb_ref.shape
    tiles = [(m, h) for m in range(members) for h in range(0, width, TILE)]
    rows = pick_ref.shape[1] // PIECES

    def matmul(m, h, piece):
        return dot(pick_ref[0, piece * rows : (piece + 1) * rows], comb_ref[m, :, h : h + TILE])

    staged(tiles, work_ref, matmul, finish)


def node_stage(summed_ref, node_ref, work_ref, finish):
    members, rows, width = summed_ref.shape
    share = members // PIECES

    def matmul(h, piece):
        some = summed_ref[piece * share : (piece + 1) * share].reshape(share * rows, width)
        return dot(some, node_ref[:, h : h + TILE])

    def finish_members(buffer, h, piece):
        for m in range(piece * share, (piece + 1) * share):
            finish(buffer, m * rows, m, h)

    staged([(h,) for h in range(0, width, TILE)], work_ref, matmul, finish_members)


def forward_kernel(
    own_ref, left_ref, right_ref, project_ref, pick_ref, grid_ref, node_ref, output_ref, prior_ref,
    pred_ref, summed_ref, out_ref, slope_ref, table_ref, columns_ref,
    comb_ref, rows_ref, *work_ref,
):
    members, own_nodes, width = own_ref.shape
    table_rows = own_nodes + left_ref.shape[1] + right_ref.shape[1]

    @pl.when(pl.program_id(0) == 0)
    def _():
        for m in range(members):
            first = m * table_rows
            for ref in (own_ref, left_ref, right_ref):
                rows_ref[first : first + ref.shape[1]] = ref[m]
                first += ref.shape[1]
        projected = dot(rows_ref[...], project_ref[...]).astype(jnp.bfloat16)
        for m in range(members):
            comb_ref[m, :table_rows] = projected[m * table_rows : (m + 1) * table_rows]
            comb_ref[m, table_rows:TABLE] = jnp.full(
                (TABLE - table_rows, width), EMPTY, jnp.bfloat16
            )
        table_ref[...] = comb_ref[:, :TABLE]
        columns_ref[...] = rows_ref[...].astype(jnp.float32).T.astype(jnp.bfloat16)

    for m in range(members):
        comb_ref[m, TABLE:] = grid_ref[...]

    def sum_edges(buffer, m, h, piece):
        for r, c in blocks(CHUNK, piece):
            twice = sum(
                gelu_twice(buffer[k * CHUNK + r : k * CHUNK + r + PART, c : c + LANES])
                for k in range(DEGREE)
            )
            summed_ref[m, r : r + PART, h + c : h + c + LANES] = (0.5 * twice).astype(jnp.bfloat16)

    def node_values(buffer, first, m, h):
        for r in range(0, CHUNK, PART):
            for c in range(0, TILE, LANES):
                u = buffer[first + r : first + r + PART, c : c + LANES]
                s, t = tanh_of(u)
                place = (m, slice(r, r + PART), slice(h + c, h + c + LANES))
                out_ref[place] = (0.5 * (u + u * t)).astype(jnp.bfloat16)
                slope_ref[place] = (0.5 * slope_twice(u, s, t)).astype(jnp.bfloat16)

    edge_stage(pick_ref, comb_ref, work_ref, sum_edges)
    node_stage(summed_ref, node_ref, work_ref, node_values)
    for m in range(members):
        pred_ref[m] = jnp.zeros(pred_ref.shape[1:], jnp.float32)
        pred_ref[m, : prior_ref.shape[0]] = prior_ref[...] + dot_nt(output_ref[...], out_ref[m])


def edge_slope_kernel(comb_ref, pick_ref, grid_ref, edge_ref, both_ref, *work_ref):
    for m in range(comb_ref.shape[0]):
        both_ref[m, :TABLE] = comb_ref[m]
        both_ref[m, TABLE:] = grid_ref[...]

    def edge_slopes(buffer, m, h, piece):
        for k in range(DEGREE):
            for r, c in blocks(CHUNK, piece):
                value = 0.5 * slope_twice(
                    buffer[k * CHUNK + r : k * CHUNK + r + PART, c : c + LANES]
                )
                edge_ref[m, k, r : r + PART, h + c : h + c + LANES] = value.astype(jnp.bfloat16)

    edge_stage(pick_ref, both_ref, work_ref, edge_slopes)


def loss_kernel(
    core_index_ref, own_ref, core_ref, chip_ref, far_ref, truth_ref, weight_ref, slope_ref, output_ref,
    grad_ref, pre_ref, loss_ref, tall_ref, sum_ref,
):
    members = own_ref.shape[0]
    variables = truth_ref.shape[0]
    width = output_ref.shape[1]
    everyone = 4 * members
    fairness = 1.0 - (1.0 - ALPHA) / everyone
    edge = SOFT_EDGE * SOFT_EDGE

    @pl.when(pl.program_id(0) == 0)
    def _():
        sum_ref[...] = jnp.zeros_like(sum_ref)
        tall_ref[...] = jnp.zeros_like(tall_ref)

    everyones = [ref.at[k] for ref in (own_ref, core_ref, chip_ref, far_ref) for k in range(members)]
    total = jnp.zeros((1, CHUNK), jnp.float32)
    for first in range(0, variables, PART):
        rows = slice(first, min(first + PART, variables))
        weight = weight_ref[rows]
        truth = truth_ref[rows]
        terms = jnp.zeros_like(truth)
        for j in range(members):
            own = own_ref[j, rows]
            pair_abs = jnp.full_like(truth, -everyone * SOFT_EDGE)
            pair_sign = jnp.zeros_like(truth)
            for other in everyones:
                d = own - other[rows]
                square = d * d + edge
                r = lax.rsqrt(square)
                pair_abs = pair_abs + square * r
                pair_sign = pair_sign + d * r
            d = own - truth
            square = d * d + edge
            r = lax.rsqrt(square)
            terms = terms + (
                (square * r - SOFT_EDGE) / everyone
                - fairness / (2.0 * everyone * (everyone - 1)) * pair_abs
            )
            tall_ref[j, rows] = weight * (d * r - fairness / (everyone - 1) * pair_sign)
        total = total + jnp.sum(weight * terms, axis=0, keepdims=True)
    sum_ref[...] += total
    grads = []
    for j in range(members):
        tall = tall_ref[j].T.astype(jnp.bfloat16)
        grad_ref[j] = tall
        grads.append(tall)

    @pl.when(pl.program_id(0) == pl.num_programs(0) - 1)
    def _():
        rest = jnp.sum(sum_ref[...], axis=1, keepdims=True)
        lane = lax.broadcasted_iota(jnp.int32, (1, CHUNK), 1)
        row = jnp.zeros((1, CHUNK), jnp.float32)
        for part in range(3):
            piece = rest.astype(jnp.bfloat16).astype(jnp.float32)
            row = jnp.where(lane == variables + 3 * core_index_ref[0] + part, piece, row)
            rest = rest - piece
        loss_ref[...] = row

    stacked = jnp.concatenate(grads, axis=0)
    for h in range(0, width, TILE):
        node_grad = dot(stacked, output_ref[:, h : h + TILE]).reshape(members, CHUNK, TILE)
        slope = slope_ref[:, :, h : h + TILE].astype(jnp.float32)
        pre_ref[:, :, h : h + TILE] = (node_grad * slope).astype(jnp.bfloat16)


def dot_tn(left, right):
    return lax.dot_general(
        left, right, (((0,), (0,)), ((), ())), preferred_element_type=jnp.float32
    )


def split_rows(value, core, mine_ref, other_ref, columns):
    rows = mine_ref.shape[1]
    pairs = value.reshape(value.shape[0] // (2 * rows), 2, rows, value.shape[1])
    first, second = pairs[:, 0], pairs[:, 1]
    mine_ref[:, :, columns] = jnp.where(core == 0, first, second).astype(jnp.bfloat16)
    other_ref[:, :, columns] = jnp.where(core == 0, second, first).astype(jnp.bfloat16)


def node_term_kernel(
    core_ref, summed_ref, out_ref, pre_ref, grad_ref, loss_ref, mine_ref, other_ref,
):
    width = pre_ref.shape[2]
    core = core_ref[0]
    def flat(ref):
        return ref[...].reshape(ref.shape[0] * ref.shape[1], ref.shape[2])

    node = dot_tn(flat(summed_ref), flat(pre_ref))
    split_rows(node, core, mine_ref, other_ref, slice(0, width))
    output = dot_tn(flat(out_ref), flat(grad_ref)) + loss_ref[...]
    split_rows(output, core, mine_ref, other_ref, slice(width, width + TABLE))


def table_kernel(
    core_ref, pre_ref, node_ref, slope_ref, slot_ref, rows_ref,
    own_ref, left_ref, right_ref, mine_ref, other_ref, place_ref,
):
    members, points, width = pre_ref.shape
    own_nodes, send_rows = own_ref.shape[1], left_ref.shape[1]
    table_rows = own_nodes + 2 * send_rows

    @pl.when(pl.program_id(0) == 0)
    def _():
        for k in range(DEGREE):
            columns = slice(k * points, (k + 1) * points)
            row = lax.broadcasted_iota(jnp.int32, (TABLE, points), 0)
            picked = jnp.where(slot_ref[:, columns] == row, 1.0, 0.0)
            place_ref[:, columns] = picked.astype(jnp.bfloat16)

    summed_grads = dot_nt(pre_ref[...].reshape(members * points, width), node_ref[...])
    summed_grads = summed_grads.astype(jnp.bfloat16)
    cast = []
    for m in range(members):
        summed_grad = summed_grads[m * points : (m + 1) * points]
        table = sum(
            dot(place_ref[:, k * points : (k + 1) * points], summed_grad * slope_ref[m, k])
            for k in range(DEGREE)
        )[:table_rows]
        own_ref[m] = table[:own_nodes]
        rounded = table.astype(jnp.bfloat16)
        left_ref[m] = rounded[own_nodes : own_nodes + send_rows]
        right_ref[m] = rounded[own_nodes + send_rows :]
        cast.append(rounded)
    term = dot(rows_ref[...], jnp.concatenate(cast, axis=0))
    split_rows(term, core_ref[0], mine_ref, other_ref, slice(0, term.shape[1]))


def params():
    return pltpu.CompilerParams(
        dimension_semantics=("arbitrary",), vmem_limit_bytes=VMEM_LIMIT
    )


def cost(elements, depth, work):
    return pl.CostEstimate(
        flops=elements * (2 * depth + work), bytes_accessed=2 * elements, transcendentals=elements
    )


def whole(array):
    return pl.BlockSpec(array.shape, lambda c: (0,) * array.ndim)


def shards(
    hidden,
    grid_state,
    project_weight,
    node_weight,
    output_weight,
    prior_state,
    target,
    area_weight,
    variable_weight,
    edge_source,
    edge_target,
    edge_count,
    send_index,
):
    members, own_nodes, width = hidden.shape
    points = grid_state.shape[0]
    send_rows = send_index.shape[1]
    variables = output_weight.shape[1]
    slots = edge_source.shape[0]
    core = lax.axis_index("member") % 2
    space = lax.axis_size("space")
    total_points = points * space
    table_rows = own_nodes + 2 * send_rows
    chunks = points // CHUNK

    nodes = jnp.arange(own_nodes, dtype=jnp.int32)
    chosen = (send_index[:, :, None] == nodes).astype(jnp.bfloat16)
    packed = jnp.einsum(
        "dsn,mnh->dmsh", chosen, hidden, preferred_element_type=jnp.float32
    ).astype(jnp.bfloat16)
    forward = [(i, i + 1) for i in range(space - 1)]
    backward = [(i + 1, i) for i in range(space - 1)]
    from_left = lax.ppermute(packed[1], "space", forward)
    from_right = lax.ppermute(packed[0], "space", backward)

    edges = jnp.arange(slots, dtype=jnp.int32)
    live = edges < edge_count[0]
    owner = jnp.where(live, edge_target, points)
    ahead = jnp.pad(owner, (DEGREE - 1, 0), constant_values=-1)
    rank = sum(
        (lax.slice_in_dim(ahead, k, k + slots) == owner).astype(jnp.int32)
        for k in range(DEGREE - 1)
    )
    ranked = jnp.where(
        rank[None, :] == jnp.arange(DEGREE, dtype=jnp.int32)[:, None], edge_source[None, :] + 1, 0
    ).astype(jnp.bfloat16)
    owned = (owner[:, None] == jnp.arange(points, dtype=jnp.int32)).astype(jnp.bfloat16)
    found = jnp.einsum("ke,eg->kg", ranked, owned, preferred_element_type=jnp.float32)
    found = found.astype(jnp.int32)
    slot = jnp.where(found > 0, found - 1, table_rows)
    columns = jnp.arange(TABLE + CHUNK, dtype=jnp.int32)
    within = jnp.arange(CHUNK, dtype=jnp.int32)
    by_chunk = slot.reshape(DEGREE, chunks, CHUNK).transpose(1, 0, 2)
    pick = (
        (by_chunk[..., None] == columns) | ((within[:, None] + TABLE) == columns)
    ).astype(jnp.bfloat16).reshape(chunks, DEGREE * CHUNK, TABLE + CHUNK)
    slot_row = slot.reshape(1, DEGREE * points)
    output_rows = output_weight.T
    output_padded = jnp.pad(output_rows, ((0, TABLE - variables), (0, 0)))
    weight_map = variable_weight[:, None] * area_weight[None, :]

    chunk_rows = pl.BlockSpec((CHUNK, width), lambda c: (c, 0))
    member_rows = pl.BlockSpec((members, CHUNK, width), lambda c: (0, c, 0))
    pick_block = pl.BlockSpec((1, DEGREE * CHUNK, TABLE + CHUNK), lambda c: (c, 0, 0))
    by_variable = pl.BlockSpec((variables, CHUNK), lambda c: (0, c))
    tiled_rows = -(-variables // 8) * 8
    own_block = pl.BlockSpec((members, tiled_rows, CHUNK), lambda c: (0, 0, c))
    per_point = jax.ShapeDtypeStruct((members, points, width), jnp.bfloat16)
    pred, summed, node_out, node_slope, comb, source_columns = pl.pallas_call(
        forward_kernel,
        grid=(chunks,),
        in_specs=[
            whole(hidden), whole(from_left), whole(from_right), whole(project_weight), pick_block,
            chunk_rows,
            whole(node_weight), whole(output_rows), by_variable,
        ],
        out_specs=[
            own_block, member_rows, member_rows, member_rows,
            pl.BlockSpec((members, TABLE, width), lambda c: (0, 0, 0)),
            pl.BlockSpec((width, members * table_rows), lambda c: (0, 0)),
        ],
        out_shape=[
            jax.ShapeDtypeStruct((members, tiled_rows, points), jnp.float32), per_point, per_point,
            per_point, jax.ShapeDtypeStruct((members, TABLE, width), jnp.bfloat16),
            jax.ShapeDtypeStruct((width, members * table_rows), jnp.bfloat16),
        ],
        scratch_shapes=[
            pltpu.VMEM((members, TABLE + CHUNK, width), jnp.bfloat16),
            pltpu.VMEM((members * table_rows, width), jnp.bfloat16),
            pltpu.VMEM((DEGREE * CHUNK, TILE), jnp.float32),
            pltpu.VMEM((DEGREE * CHUNK, TILE), jnp.float32),
        ],
        compiler_params=params(),
        name="forward",
    )(hidden, from_left, from_right, project_weight, pick, grid_state, node_weight, output_rows, prior_state)

    def swap(value, flip):
        return lax.ppermute(value, "member", [(i, i ^ flip) for i in range(lax.axis_size("member"))])

    chip_pred = swap(pred, 2)
    core_pred = swap(pred, 1)

    edge_slope = pl.pallas_call(
        edge_slope_kernel,
        grid=(chunks,),
        in_specs=[whole(comb), pick_block, chunk_rows],
        out_specs=pl.BlockSpec((members, DEGREE, CHUNK, width), lambda c: (0, 0, c, 0)),
        out_shape=jax.ShapeDtypeStruct((members, DEGREE, points, width), jnp.bfloat16),
        scratch_shapes=[
            pltpu.VMEM((members, TABLE + CHUNK, width), jnp.bfloat16),
            pltpu.VMEM((DEGREE * CHUNK, TILE), jnp.float32),
            pltpu.VMEM((DEGREE * CHUNK, TILE), jnp.float32),
        ],
        compiler_params=params(),
        cost_estimate=cost(members * DEGREE * points * width, 2 * TABLE, 20),
        name="edge_slopes",
    )(comb, pick, grid_state)
    chip_pred, core_pred, edge_slope = lax.optimization_barrier((chip_pred, core_pred, edge_slope))
    far_pred = swap(chip_pred, 1)
    far_pred, weight_map, output_padded = lax.optimization_barrier(
        (far_pred, weight_map, output_padded)
    )
    grad_rows, node_pre_grad, loss_row = pl.pallas_call(
        loss_kernel,
        grid=(chunks,),
        in_specs=[
            pl.BlockSpec(memory_space=pltpu.SMEM),
            own_block, own_block, own_block, own_block, by_variable, by_variable, member_rows, whole(output_padded),
        ],
        out_specs=[
            pl.BlockSpec((members, CHUNK, TABLE), lambda c: (0, c, 0)), member_rows,
            pl.BlockSpec((1, CHUNK), lambda c: (0, 0)),
        ],
        out_shape=[
            jax.ShapeDtypeStruct((members, points, TABLE), jnp.bfloat16), per_point,
            jax.ShapeDtypeStruct((1, CHUNK), jnp.float32),
        ],
        scratch_shapes=[
            pltpu.VMEM((members, TABLE, CHUNK), jnp.float32), pltpu.VMEM((1, CHUNK), jnp.float32),
        ],
        compiler_params=params(),
        name="loss",
    )(core[None], pred, core_pred, chip_pred, far_pred, target, weight_map, node_slope, output_padded)

    own_rows = width // space // 2
    smem = pl.BlockSpec(memory_space=pltpu.SMEM)

    def add_partner(mine, other):
        return (mine.astype(jnp.float32) + swap(other, 1).astype(jnp.float32)).astype(jnp.bfloat16)

    def across_space(half):
        return lax.all_to_all(half, "space", 0, 0, tiled=True)

    def sum_members(part):
        mine = part + swap(part, 2)
        other = swap(part, 1) + swap(part, 3)
        return jnp.where(
            core == 0,
            jnp.concatenate([mine, other], axis=0),
            jnp.concatenate([other, mine], axis=0),
        )

    terms_block = pl.BlockSpec(
        (TILE // (2 * own_rows), own_rows, width + TABLE), lambda c: (c, 0, 0)
    )
    terms_shape = jax.ShapeDtypeStruct((space, own_rows, width + TABLE), jnp.bfloat16)
    some_columns = pl.BlockSpec((members, points, TILE), lambda c: (0, 0, c))
    node_mine, node_other = pl.pallas_call(
        node_term_kernel,
        grid=(width // TILE,),
        in_specs=[
            smem, some_columns, some_columns, whole(node_pre_grad), whole(grad_rows),
            whole(loss_row),
        ],
        out_specs=[terms_block, terms_block],
        out_shape=[terms_shape, terms_shape],
        compiler_params=params(),
        cost_estimate=cost(width * width, members * points, 1),
        name="node_terms",
    )(core[None], summed, node_out, node_pre_grad, grad_rows, loss_row)

    node_half = add_partner(node_mine, node_other)
    pre_grad, node_half = lax.optimization_barrier((node_pre_grad, node_half))
    node_moved = across_space(node_half)
    columns = pl.BlockSpec((space, own_rows, TILE), lambda c: (0, 0, c))
    halo_columns = pl.BlockSpec((members, send_rows, TILE), lambda c: (0, 0, c))
    halo_shape = jax.ShapeDtypeStruct((members, send_rows, width), jnp.bfloat16)
    columns_shape = jax.ShapeDtypeStruct((space, own_rows, width), jnp.bfloat16)
    own_grad, left_grad, right_grad, project_mine, project_other = pl.pallas_call(
        table_kernel,
        grid=(width // TILE,),
        in_specs=[
            smem,
            whole(pre_grad),
            pl.BlockSpec((TILE, width), lambda c: (c, 0)),
            pl.BlockSpec((members, DEGREE, points, TILE), lambda c: (0, 0, 0, c)),
            whole(slot_row),
            whole(source_columns),
        ],
        out_specs=[
            pl.BlockSpec((members, own_nodes, TILE), lambda c: (0, 0, c)), halo_columns,
            halo_columns, columns, columns,
        ],
        out_shape=[
            jax.ShapeDtypeStruct((members, own_nodes, width), jnp.float32), halo_shape, halo_shape,
            columns_shape, columns_shape,
        ],
        scratch_shapes=[pltpu.VMEM((TABLE, DEGREE * points), jnp.bfloat16)],
        compiler_params=params(),
        cost_estimate=cost(members * points * width, 4 * width, 8),
        name="table",
    )(core[None], pre_grad, node_weight, edge_slope, slot_row, source_columns)
    left_grad, right_grad, project_mine, project_other, node_moved = lax.optimization_barrier(
        (left_grad, right_grad, project_mine, project_other, node_moved)
    )
    project_half = add_partner(project_mine, project_other)

    left_back = lax.ppermute(left_grad, "space", backward)
    right_back = lax.ppermute(right_grad, "space", forward)
    project_half, left_back, right_back = lax.optimization_barrier(
        (project_half, left_back, right_back)
    )
    project_moved = across_space(project_half)
    projected_grad = (
        own_grad
        + jnp.einsum(
            "sn,msh->mnh", chosen[1], left_back, preferred_element_type=jnp.float32
        )
        + jnp.einsum(
            "sn,msh->mnh", chosen[0], right_back, preferred_element_type=jnp.float32
        )
    ).astype(jnp.bfloat16)
    grad_hidden = jnp.einsum(
        "mnk,hk->mnh", projected_grad, project_weight, preferred_element_type=jnp.float32
    ).astype(jnp.bfloat16)
    project_moved, grad_hidden = lax.optimization_barrier((project_moved, grad_hidden))
    project_part, node_part = (
        jnp.sum(moved.astype(jnp.float32), axis=0) for moved in (project_moved, node_moved)
    )
    sums = sum_members(jnp.concatenate([project_part, node_part], axis=1))
    output_at = 2 * width
    loss_at = output_at + variables
    return (
        grad_hidden,
        sums[:, :width] / total_points,
        sums[:, width:output_at] / total_points,
        sums[:, output_at:loss_at] / total_points,
        jnp.sum(sums[0, loss_at:]) / (total_points * variables),
    )


def solution(mesh):
    placed = (
        P("member", "space", None),
        P("space", None),
        P(),
        P(),
        P(),
        P(None, "space"),
        P(None, "space"),
        P("space"),
        P(),
        P("space"),
        P("space"),
        P("space"),
        P("space", None),
    )
    return jax.shard_map(
        shards,
        mesh=mesh,
        in_specs=placed,
        out_specs=(
            P("member", "space", None),
            P("space", None),
            P("space", None),
            P("space", None),
            P(),
        ),
        check_vma=False,
    )
```

```python
import functools

import jax
import jax.numpy as jnp
from jax import lax
from jax.experimental import pallas as pl
from jax.experimental.pallas import tpu as pltpu
from jax.sharding import PartitionSpec as P

SQRT_TWO_PI = 0.7978845608028654
CUBIC = 0.044715
ALPHA = 0.95
SOFT_EDGE = 0.05
DEGREE = 4
TABLE = 128
EMPTY = -64.0
CHUNK = 128
TILE = 256
PART = 32
PIECES = 1
VMEM_LIMIT = 56 * 1024 * 1024
BACKWARD_VMEM_LIMIT = 46 * 1024 * 1024
LANES = 128


def tanh_of(u):
    s = u * u
    return s, jnp.tanh(u * (SQRT_TWO_PI + (SQRT_TWO_PI * CUBIC) * s))


def gelu_twice(u):
    _, t = tanh_of(u)
    return u + u * t


def slope_twice(u, s=None, t=None):
    if t is None:
        s, t = tanh_of(u)
    q = u * (SQRT_TWO_PI + (3.0 * SQRT_TWO_PI * CUBIC) * s)
    return (1.0 + t) * (1.0 + (1.0 - t) * q)


def dot(left, right):
    return lax.dot_general(
        left, right, (((1,), (0,)), ((), ())), preferred_element_type=jnp.float32
    )


def dot_nt(left, right):
    return lax.dot_general(
        left, right, (((1,), (1,)), ((), ())), preferred_element_type=jnp.float32
    )


def blocks(rows, piece):
    share = rows // PIECES
    first = piece * share
    return [(r, c) for r in range(first, first + share, PART) for c in range(0, TILE, LANES)]


def staged(tiles, work_ref, matmul, finish):
    for i in range(len(tiles) + 1):
        for piece in range(PIECES):
            if i < len(tiles):
                result = matmul(*tiles[i], piece)
                rows = result.shape[0]
                work_ref[i % 2][piece * rows : (piece + 1) * rows] = result
            if i:
                finish(work_ref[(i - 1) % 2], *tiles[i - 1], piece)


def edge_stage(pick_ref, comb_ref, work_ref, finish):
    members, _, width = comb_ref.shape
    tiles = [(m, h) for m in range(members) for h in range(0, width, TILE)]
    rows = pick_ref.shape[1] // PIECES

    def matmul(m, h, piece):
        return dot(pick_ref[0, piece * rows : (piece + 1) * rows], comb_ref[m, :, h : h + TILE])

    staged(tiles, work_ref, matmul, finish)


def node_stage(summed_ref, node_ref, work_ref, finish):
    members, rows, width = summed_ref.shape
    share = members // PIECES

    def matmul(h, piece):
        some = summed_ref[piece * share : (piece + 1) * share].reshape(share * rows, width)
        return dot(some, node_ref[:, h : h + TILE])

    def finish_members(buffer, h, piece):
        for m in range(piece * share, (piece + 1) * share):
            finish(buffer, m * rows, m, h)

    staged([(h,) for h in range(0, width, TILE)], work_ref, matmul, finish_members)


def forward_kernel(
    own_ref, left_ref, right_ref, project_ref, pick_ref, grid_ref, node_ref, output_ref, prior_ref,
    pred_ref, summed_ref, out_ref, slope_ref, table_ref, columns_ref,
    comb_ref, rows_ref, *work_ref,
):
    members, own_nodes, width = own_ref.shape
    table_rows = own_nodes + left_ref.shape[1] + right_ref.shape[1]

    @pl.when(pl.program_id(0) == 0)
    def _():
        for m in range(members):
            first = m * table_rows
            for ref in (own_ref, left_ref, right_ref):
                rows_ref[first : first + ref.shape[1]] = ref[m]
                first += ref.shape[1]
        projected = dot(rows_ref[...], project_ref[...]).astype(jnp.bfloat16)
        for m in range(members):
            comb_ref[m, :table_rows] = projected[m * table_rows : (m + 1) * table_rows]
            comb_ref[m, table_rows:TABLE] = jnp.full(
                (TABLE - table_rows, width), EMPTY, jnp.bfloat16
            )
        table_ref[...] = comb_ref[:, :TABLE]
        columns_ref[...] = rows_ref[...].astype(jnp.float32).T.astype(jnp.bfloat16)

    for m in range(members):
        comb_ref[m, TABLE:] = grid_ref[...]

    def sum_edges(buffer, m, h, piece):
        for r, c in blocks(CHUNK, piece):
            twice = sum(
                gelu_twice(buffer[k * CHUNK + r : k * CHUNK + r + PART, c : c + LANES])
                for k in range(DEGREE)
            )
            summed_ref[m, r : r + PART, h + c : h + c + LANES] = (0.5 * twice).astype(jnp.bfloat16)

    def node_values(buffer, first, m, h):
        for r in range(0, CHUNK, PART):
            for c in range(0, TILE, LANES):
                u = buffer[first + r : first + r + PART, c : c + LANES]
                s, t = tanh_of(u)
                place = (m, slice(r, r + PART), slice(h + c, h + c + LANES))
                out_ref[place] = (0.5 * (u + u * t)).astype(jnp.bfloat16)
                slope_ref[place] = (0.5 * slope_twice(u, s, t)).astype(jnp.bfloat16)

    edge_stage(pick_ref, comb_ref, work_ref, sum_edges)
    node_stage(summed_ref, node_ref, work_ref, node_values)
    for m in range(members):
        pred_ref[m] = jnp.zeros(pred_ref.shape[1:], jnp.float32)
        pred_ref[m, : prior_ref.shape[0]] = prior_ref[...] + dot_nt(output_ref[...], out_ref[m])


def edge_slope_kernel(comb_ref, pick_ref, grid_ref, edge_ref, both_ref, *work_ref):
    for m in range(comb_ref.shape[0]):
        both_ref[m, :TABLE] = comb_ref[m]
        both_ref[m, TABLE:] = grid_ref[...]

    def edge_slopes(buffer, m, h, piece):
        for k in range(DEGREE):
            for r, c in blocks(CHUNK, piece):
                value = 0.5 * slope_twice(
                    buffer[k * CHUNK + r : k * CHUNK + r + PART, c : c + LANES]
                )
                edge_ref[m, k, r : r + PART, h + c : h + c + LANES] = value.astype(jnp.bfloat16)

    edge_stage(pick_ref, both_ref, work_ref, edge_slopes)


def loss_kernel(
    core_index_ref, own_ref, core_ref, chip_ref, far_ref, truth_ref, weight_ref, slope_ref, output_ref,
    grad_ref, pre_ref, loss_ref, tall_ref, sum_ref,
):
    members = own_ref.shape[0]
    variables = truth_ref.shape[0]
    width = output_ref.shape[1]
    everyone = 4 * members
    fairness = 1.0 - (1.0 - ALPHA) / everyone
    edge = SOFT_EDGE * SOFT_EDGE

    @pl.when(pl.program_id(0) == 0)
    def _():
        sum_ref[...] = jnp.zeros_like(sum_ref)
        tall_ref[...] = jnp.zeros_like(tall_ref)

    everyones = [ref.at[k] for ref in (own_ref, core_ref, chip_ref, far_ref) for k in range(members)]
    total = jnp.zeros((1, CHUNK), jnp.float32)
    for first in range(0, variables, PART):
        rows = slice(first, min(first + PART, variables))
        weight = weight_ref[rows]
        truth = truth_ref[rows]
        terms = jnp.zeros_like(truth)
        for j in range(members):
            own = own_ref[j, rows]
            pair_abs = jnp.full_like(truth, -everyone * SOFT_EDGE)
            pair_sign = jnp.zeros_like(truth)
            for other in everyones:
                d = own - other[rows]
                square = d * d + edge
                r = lax.rsqrt(square)
                pair_abs = pair_abs + square * r
                pair_sign = pair_sign + d * r
            d = own - truth
            square = d * d + edge
            r = lax.rsqrt(square)
            terms = terms + (
                (square * r - SOFT_EDGE) / everyone
                - fairness / (2.0 * everyone * (everyone - 1)) * pair_abs
            )
            tall_ref[j, rows] = weight * (d * r - fairness / (everyone - 1) * pair_sign)
        total = total + jnp.sum(weight * terms, axis=0, keepdims=True)
    sum_ref[...] += total
    grads = []
    for j in range(members):
        tall = tall_ref[j].T.astype(jnp.bfloat16)
        grad_ref[j] = tall
        grads.append(tall)

    @pl.when(pl.program_id(0) == pl.num_programs(0) - 1)
    def _():
        rest = jnp.sum(sum_ref[...], axis=1, keepdims=True)
        lane = lax.broadcasted_iota(jnp.int32, (1, CHUNK), 1)
        row = jnp.zeros((1, CHUNK), jnp.float32)
        for part in range(3):
            piece = rest.astype(jnp.bfloat16).astype(jnp.float32)
            row = jnp.where(lane == variables + 3 * core_index_ref[0] + part, piece, row)
            rest = rest - piece
        loss_ref[...] = row

    stacked = jnp.concatenate(grads, axis=0)
    for h in range(0, width, TILE):
        node_grad = dot(stacked, output_ref[:, h : h + TILE]).reshape(members, CHUNK, TILE)
        slope = slope_ref[:, :, h : h + TILE].astype(jnp.float32)
        pre_ref[:, :, h : h + TILE] = (node_grad * slope).astype(jnp.bfloat16)


def dot_tn(left, right):
    return lax.dot_general(
        left, right, (((0,), (0,)), ((), ())), preferred_element_type=jnp.float32
    )


def split_rows(value, core, mine_ref, other_ref, columns):
    rows = mine_ref.shape[1]
    pairs = value.reshape(value.shape[0] // (2 * rows), 2, rows, value.shape[1])
    first, second = pairs[:, 0], pairs[:, 1]
    mine_ref[:, :, columns] = jnp.where(core == 0, first, second).astype(jnp.bfloat16)
    other_ref[:, :, columns] = jnp.where(core == 0, second, first).astype(jnp.bfloat16)


def node_term_kernel(
    core_ref, summed_ref, out_ref, pre_ref, grad_ref, loss_ref, mine_ref, other_ref,
):
    width = pre_ref.shape[2]
    core = core_ref[0]
    def flat(ref):
        return ref[...].reshape(ref.shape[0] * ref.shape[1], ref.shape[2])

    node = dot_tn(flat(summed_ref), flat(pre_ref))
    split_rows(node, core, mine_ref, other_ref, slice(0, width))
    output = dot_tn(flat(out_ref), flat(grad_ref)) + loss_ref[...]
    split_rows(output, core, mine_ref, other_ref, slice(width, width + TABLE))


def table_kernel(
    core_ref, pre_ref, node_ref, slope_ref, slot_ref, rows_ref,
    own_ref, left_ref, right_ref, mine_ref, other_ref, place_ref,
):
    members, points, width = pre_ref.shape
    own_nodes, send_rows = own_ref.shape[1], left_ref.shape[1]
    table_rows = own_nodes + 2 * send_rows

    @pl.when(pl.program_id(0) == 0)
    def _():
        for k in range(DEGREE):
            columns = slice(k * points, (k + 1) * points)
            row = lax.broadcasted_iota(jnp.int32, (TABLE, points), 0)
            picked = jnp.where(slot_ref[:, columns] == row, 1.0, 0.0)
            place_ref[:, columns] = picked.astype(jnp.bfloat16)

    summed_grads = dot_nt(pre_ref[...].reshape(members * points, width), node_ref[...])
    summed_grads = summed_grads.astype(jnp.bfloat16)
    cast = []
    for m in range(members):
        summed_grad = summed_grads[m * points : (m + 1) * points]
        table = sum(
            dot(place_ref[:, k * points : (k + 1) * points], summed_grad * slope_ref[m, k])
            for k in range(DEGREE)
        )[:table_rows]
        own_ref[m] = table[:own_nodes]
        rounded = table.astype(jnp.bfloat16)
        left_ref[m] = rounded[own_nodes : own_nodes + send_rows]
        right_ref[m] = rounded[own_nodes + send_rows :]
        cast.append(rounded)
    term = dot(rows_ref[...], jnp.concatenate(cast, axis=0))
    split_rows(term, core_ref[0], mine_ref, other_ref, slice(0, term.shape[1]))


def params(limit=VMEM_LIMIT):
    return pltpu.CompilerParams(
        dimension_semantics=("arbitrary",), vmem_limit_bytes=limit
    )


def cost(elements, depth, work):
    return pl.CostEstimate(
        flops=elements * (2 * depth + work), bytes_accessed=2 * elements, transcendentals=elements
    )


def whole(array):
    return pl.BlockSpec(array.shape, lambda c: (0,) * array.ndim)


def shards(
    hidden,
    grid_state,
    project_weight,
    node_weight,
    output_weight,
    prior_state,
    target,
    area_weight,
    variable_weight,
    edge_source,
    edge_target,
    edge_count,
    send_index,
):
    members, own_nodes, width = hidden.shape
    points = grid_state.shape[0]
    send_rows = send_index.shape[1]
    variables = output_weight.shape[1]
    slots = edge_source.shape[0]
    core = lax.axis_index("member") % 2
    space = lax.axis_size("space")
    total_points = points * space
    table_rows = own_nodes + 2 * send_rows
    chunks = points // CHUNK

    nodes = jnp.arange(own_nodes, dtype=jnp.int32)
    chosen = (send_index[:, :, None] == nodes).astype(jnp.bfloat16)
    packed = jnp.einsum(
        "dsn,mnh->dmsh", chosen, hidden, preferred_element_type=jnp.float32
    ).astype(jnp.bfloat16)
    forward = [(i, i + 1) for i in range(space - 1)]
    backward = [(i + 1, i) for i in range(space - 1)]
    from_left = lax.ppermute(packed[1], "space", forward)
    from_right = lax.ppermute(packed[0], "space", backward)

    edges = jnp.arange(slots, dtype=jnp.int32)
    live = edges < edge_count[0]
    owner = jnp.where(live, edge_target, points)
    ahead = jnp.pad(owner, (DEGREE - 1, 0), constant_values=-1)
    rank = sum(
        (lax.slice_in_dim(ahead, k, k + slots) == owner).astype(jnp.int32)
        for k in range(DEGREE - 1)
    )
    ranked = jnp.where(
        rank[None, :] == jnp.arange(DEGREE, dtype=jnp.int32)[:, None], edge_source[None, :] + 1, 0
    ).astype(jnp.bfloat16)
    owned = (owner[:, None] == jnp.arange(points, dtype=jnp.int32)).astype(jnp.bfloat16)
    found = jnp.einsum("ke,eg->kg", ranked, owned, preferred_element_type=jnp.float32)
    found = found.astype(jnp.int32)
    slot = jnp.where(found > 0, found - 1, table_rows)
    columns = jnp.arange(TABLE + CHUNK, dtype=jnp.int32)
    within = jnp.arange(CHUNK, dtype=jnp.int32)
    by_chunk = slot.reshape(DEGREE, chunks, CHUNK).transpose(1, 0, 2)
    pick = (
        (by_chunk[..., None] == columns) | ((within[:, None] + TABLE) == columns)
    ).astype(jnp.bfloat16).reshape(chunks, DEGREE * CHUNK, TABLE + CHUNK)
    slot_row = slot.reshape(1, DEGREE * points)
    output_rows = output_weight.T
    output_padded = jnp.pad(output_rows, ((0, TABLE - variables), (0, 0)))
    weight_map = variable_weight[:, None] * area_weight[None, :]

    chunk_rows = pl.BlockSpec((CHUNK, width), lambda c: (c, 0))
    member_rows = pl.BlockSpec((members, CHUNK, width), lambda c: (0, c, 0))
    pick_block = pl.BlockSpec((1, DEGREE * CHUNK, TABLE + CHUNK), lambda c: (c, 0, 0))
    by_variable = pl.BlockSpec((variables, CHUNK), lambda c: (0, c))
    tiled_rows = -(-variables // 8) * 8
    own_block = pl.BlockSpec((members, tiled_rows, CHUNK), lambda c: (0, 0, c))
    per_point = jax.ShapeDtypeStruct((members, points, width), jnp.bfloat16)
    pred, summed, node_out, node_slope, comb, source_columns = pl.pallas_call(
        forward_kernel,
        grid=(chunks,),
        in_specs=[
            whole(hidden), whole(from_left), whole(from_right), whole(project_weight), pick_block,
            chunk_rows,
            whole(node_weight), whole(output_rows), by_variable,
        ],
        out_specs=[
            own_block, member_rows, member_rows, member_rows,
            pl.BlockSpec((members, TABLE, width), lambda c: (0, 0, 0)),
            pl.BlockSpec((width, members * table_rows), lambda c: (0, 0)),
        ],
        out_shape=[
            jax.ShapeDtypeStruct((members, tiled_rows, points), jnp.float32), per_point, per_point,
            per_point, jax.ShapeDtypeStruct((members, TABLE, width), jnp.bfloat16),
            jax.ShapeDtypeStruct((width, members * table_rows), jnp.bfloat16),
        ],
        scratch_shapes=[
            pltpu.VMEM((members, TABLE + CHUNK, width), jnp.bfloat16),
            pltpu.VMEM((members * table_rows, width), jnp.bfloat16),
            pltpu.VMEM((DEGREE * CHUNK, TILE), jnp.float32),
            pltpu.VMEM((DEGREE * CHUNK, TILE), jnp.float32),
        ],
        compiler_params=params(),
        name="forward",
    )(hidden, from_left, from_right, project_weight, pick, grid_state, node_weight, output_rows, prior_state)

    def swap(value, flip):
        return lax.ppermute(value, "member", [(i, i ^ flip) for i in range(lax.axis_size("member"))])

    chip_pred = swap(pred, 2)
    core_pred = swap(pred, 1)

    edge_slope = pl.pallas_call(
        edge_slope_kernel,
        grid=(chunks,),
        in_specs=[whole(comb), pick_block, chunk_rows],
        out_specs=pl.BlockSpec((members, DEGREE, CHUNK, width), lambda c: (0, 0, c, 0)),
        out_shape=jax.ShapeDtypeStruct((members, DEGREE, points, width), jnp.bfloat16),
        scratch_shapes=[
            pltpu.VMEM((members, TABLE + CHUNK, width), jnp.bfloat16),
            pltpu.VMEM((DEGREE * CHUNK, TILE), jnp.float32),
            pltpu.VMEM((DEGREE * CHUNK, TILE), jnp.float32),
        ],
        compiler_params=params(),
        cost_estimate=cost(members * DEGREE * points * width, 2 * TABLE, 20),
        name="edge_slopes",
    )(comb, pick, grid_state)
    chip_pred, core_pred, edge_slope = lax.optimization_barrier((chip_pred, core_pred, edge_slope))
    far_pred = swap(chip_pred, 1)
    far_pred, weight_map, output_padded = lax.optimization_barrier(
        (far_pred, weight_map, output_padded)
    )
    grad_rows, node_pre_grad, loss_row = pl.pallas_call(
        loss_kernel,
        grid=(chunks,),
        in_specs=[
            pl.BlockSpec(memory_space=pltpu.SMEM),
            own_block, own_block, own_block, own_block, by_variable, by_variable, member_rows, whole(output_padded),
        ],
        out_specs=[
            pl.BlockSpec((members, CHUNK, TABLE), lambda c: (0, c, 0)), member_rows,
            pl.BlockSpec((1, CHUNK), lambda c: (0, 0)),
        ],
        out_shape=[
            jax.ShapeDtypeStruct((members, points, TABLE), jnp.bfloat16), per_point,
            jax.ShapeDtypeStruct((1, CHUNK), jnp.float32),
        ],
        scratch_shapes=[
            pltpu.VMEM((members, TABLE, CHUNK), jnp.float32), pltpu.VMEM((1, CHUNK), jnp.float32),
        ],
        compiler_params=params(BACKWARD_VMEM_LIMIT),
        name="loss",
    )(core[None], pred, core_pred, chip_pred, far_pred, target, weight_map, node_slope, output_padded)

    own_rows = width // space // 2
    smem = pl.BlockSpec(memory_space=pltpu.SMEM)

    def add_partner(mine, other):
        return (mine.astype(jnp.float32) + swap(other, 1).astype(jnp.float32)).astype(jnp.bfloat16)

    def across_space(half):
        return lax.all_to_all(half, "space", 0, 0, tiled=True)

    def sum_members(part):
        mine = part + swap(part, 2)
        other = swap(part, 1) + swap(part, 3)
        return jnp.where(
            core == 0,
            jnp.concatenate([mine, other], axis=0),
            jnp.concatenate([other, mine], axis=0),
        )

    terms_block = pl.BlockSpec(
        (TILE // (2 * own_rows), own_rows, width + TABLE), lambda c: (c, 0, 0)
    )
    terms_shape = jax.ShapeDtypeStruct((space, own_rows, width + TABLE), jnp.bfloat16)
    some_columns = pl.BlockSpec((members, points, TILE), lambda c: (0, 0, c))
    node_mine, node_other = pl.pallas_call(
        node_term_kernel,
        grid=(width // TILE,),
        in_specs=[
            smem, some_columns, some_columns, whole(node_pre_grad), whole(grad_rows),
            whole(loss_row),
        ],
        out_specs=[terms_block, terms_block],
        out_shape=[terms_shape, terms_shape],
        compiler_params=params(BACKWARD_VMEM_LIMIT),
        cost_estimate=cost(width * width, members * points, 1),
        name="node_terms",
    )(core[None], summed, node_out, node_pre_grad, grad_rows, loss_row)

    node_half = add_partner(node_mine, node_other)
    pre_grad, node_half = lax.optimization_barrier((node_pre_grad, node_half))
    node_moved = across_space(node_half)
    columns = pl.BlockSpec((space, own_rows, TILE), lambda c: (0, 0, c))
    halo_columns = pl.BlockSpec((members, send_rows, TILE), lambda c: (0, 0, c))
    halo_shape = jax.ShapeDtypeStruct((members, send_rows, width), jnp.bfloat16)
    columns_shape = jax.ShapeDtypeStruct((space, own_rows, width), jnp.bfloat16)
    own_grad, left_grad, right_grad, project_mine, project_other = pl.pallas_call(
        table_kernel,
        grid=(width // TILE,),
        in_specs=[
            smem,
            whole(pre_grad),
            pl.BlockSpec((TILE, width), lambda c: (c, 0)),
            pl.BlockSpec((members, DEGREE, points, TILE), lambda c: (0, 0, 0, c)),
            whole(slot_row),
            whole(source_columns),
        ],
        out_specs=[
            pl.BlockSpec((members, own_nodes, TILE), lambda c: (0, 0, c)), halo_columns,
            halo_columns, columns, columns,
        ],
        out_shape=[
            jax.ShapeDtypeStruct((members, own_nodes, width), jnp.float32), halo_shape, halo_shape,
            columns_shape, columns_shape,
        ],
        scratch_shapes=[pltpu.VMEM((TABLE, DEGREE * points), jnp.bfloat16)],
        compiler_params=params(BACKWARD_VMEM_LIMIT),
        cost_estimate=cost(members * points * width, 4 * width, 8),
        name="table",
    )(core[None], pre_grad, node_weight, edge_slope, slot_row, source_columns)
    left_grad, right_grad, project_mine, project_other, node_moved = lax.optimization_barrier(
        (left_grad, right_grad, project_mine, project_other, node_moved)
    )
    project_half = add_partner(project_mine, project_other)

    left_back = lax.ppermute(left_grad, "space", backward)
    right_back = lax.ppermute(right_grad, "space", forward)
    project_half, left_back, right_back = lax.optimization_barrier(
        (project_half, left_back, right_back)
    )
    project_moved = across_space(project_half)
    projected_grad = (
        own_grad
        + jnp.einsum(
            "sn,msh->mnh", chosen[1], left_back, preferred_element_type=jnp.float32
        )
        + jnp.einsum(
            "sn,msh->mnh", chosen[0], right_back, preferred_element_type=jnp.float32
        )
    ).astype(jnp.bfloat16)
    grad_hidden = jnp.einsum(
        "mnk,hk->mnh", projected_grad, project_weight, preferred_element_type=jnp.float32
    ).astype(jnp.bfloat16)
    project_moved, grad_hidden = lax.optimization_barrier((project_moved, grad_hidden))
    project_part, node_part = (
        jnp.sum(moved.astype(jnp.float32), axis=0) for moved in (project_moved, node_moved)
    )
    sums = sum_members(jnp.concatenate([project_part, node_part], axis=1))
    output_at = 2 * width
    loss_at = output_at + variables
    return (
        grad_hidden,
        sums[:, :width] / total_points,
        sums[:, width:output_at] / total_points,
        sums[:, output_at:loss_at] / total_points,
        jnp.sum(sums[0, loss_at:]) / (total_points * variables),
    )


def solution(mesh):
    placed = (
        P("member", "space", None),
        P("space", None),
        P(),
        P(),
        P(),
        P(None, "space"),
        P(None, "space"),
        P("space"),
        P(),
        P("space"),
        P("space"),
        P("space"),
        P("space", None),
    )
    return jax.shard_map(
        shards,
        mesh=mesh,
        in_specs=placed,
        out_specs=(
            P("member", "space", None),
            P("space", None),
            P("space", None),
            P("space", None),
            P(),
        ),
        check_vma=False,
    )
```
